32 devices in a mesh: dp: 8 (over y, x, core), tensor: 4 (over z).
Axes of the slice: x: 2, y: 2, z: 4, core: 2. Of those that a mesh axis runs over, the one named last changes fastest.
Arguments:
- hidden_in: bfloat16 [8192, 2048], P(('dp', 'tensor')), may hold values from -6 to 6
- gain_attn: bfloat16 [2048], replicated, may hold values from 0.5 to 1.5
- w_query: bfloat16 [2048, 2048], P(None, 'tensor'), may hold values from -0.125 to 0.125
- w_key: bfloat16 [2048, 1024], P(None, 'tensor'), may hold values from -0.125 to 0.125
- w_value: bfloat16 [2048, 1024], P(None, 'tensor'), may hold values from -0.125 to 0.125
- w_out: bfloat16 [2048, 2048], P('tensor'), may hold values from -0.5 to 0.5
- gain_ffn: bfloat16 [2048], replicated, may hold values from 0.5 to 1.5
- w_gate: bfloat16 [2048, 8192], P(None, 'tensor'), may hold values from -0.125 to 0.125
- w_up: bfloat16 [2048, 8192], P(None, 'tensor'), may hold values from -0.125 to 0.125
- w_down: bfloat16 [8192, 2048], P('tensor'), may hold values from -0.0625 to 0.0625
- segments: int32 [8192], P('dp'), may hold values from 3 to 7, as said below
- parents: int32 [64], P('dp'), may hold values from 0 to 6, as said below
- cotangent: bfloat16 [8192, 2048], P(('dp', 'tensor')), may hold values from -6 to 6
Outputs:
- output: bfloat16 [8192, 2048], P(('dp', 'tensor'))
- input_grad: bfloat16 [8192, 2048], P(('dp', 'tensor'))
- gain_attn_grad: float32 [2048], P('dp')
- w_query_grad: float32 [2048, 2048], P('dp', 'tensor')
- w_key_grad: float32 [2048, 1024], P('dp', 'tensor')
- w_value_grad: float32 [2048, 1024], P('dp', 'tensor')
- w_out_grad: float32 [2048, 2048], P('tensor', 'dp')
- gain_ffn_grad: float32 [2048], P('dp')
- w_gate_grad: float32 [2048, 8192], P('dp', 'tensor')
- w_up_grad: float32 [2048, 8192], P('dp', 'tensor')
- w_down_grad: float32 [8192, 2048], P('tensor', 'dp')
The draws below stay inside these ranges and needn't reach their ends.
Inputs may be any that keep to these rules, and one draw needn't show every extreme that they name: `segments`: each tree is whole aligned blocks of 128 tokens inside one group of 1024 tokens and holds 4 to 8 blocks; some tree holds exactly 8 blocks. Every token of a tree carries the index, within its group of 8 blocks, of the tree's last block. `parents`: A tree's first block has 0; every other block names an earlier block of its own tree.
All inputs are finite; a program needn't handle non-finite values.
Results may differ from the reference program's by a relative error of at most 0.025.
Values may be sent and summed in bfloat16 or wider, within the bound.
A program may use at most 256 MiB of HBM per device.

```python
import jax
import jax.numpy as jnp
from jax import lax

D = 2048
H = 16
KV = 8
HD = 128
FF = 8192
BLK = 128
MINB = 4
MAXB = 8
GBLK = 8
TOKENS = 8192
N_DP = 8
N_TENSOR = 4


def tree_layout(key):
    group_count = N_DP
    size_count = MAXB - MINB + 1
    pick_key, size_key, parent_key, trunk_key = jax.random.split(key, 4)
    forced_group = jax.random.randint(pick_key, (), 0, group_count)
    short_group = (forced_group + 1) % group_count
    size_scores = jax.random.randint(size_key, (GBLK, group_count, size_count), 0, 1 << 20)
    parent_draws = jax.random.randint(parent_key, (GBLK, group_count), 0, 1 << 20)
    trunk_draws = jax.random.randint(trunk_key, (GBLK, group_count), 0, 2)
    size_options = MINB + jnp.arange(size_count, dtype=jnp.int32)
    group_ids = jnp.arange(group_count, dtype=jnp.int32)

    def advance(running, block_item):
        blocks_left, local_index = running
        score_row, parent_draw, trunk_draw, place = block_item
        remain = GBLK - place
        spare = remain - size_options
        usable = (size_options <= remain) & ((spare == 0) | (spare >= MINB))
        ranked = jnp.where(usable[None, :], score_row * size_count + jnp.arange(size_count, dtype=jnp.int32)[None, :], -1)
        chosen = MINB + jnp.argmax(ranked, axis=1).astype(jnp.int32)
        chosen = jnp.where((place == 0) & (group_ids == short_group), MINB, chosen)
        chosen = jnp.where((place == 0) & (group_ids == forced_group), MAXB, chosen)
        begins = blocks_left == 0
        blocks_left = jnp.where(begins, chosen - 1, blocks_left - 1)
        local_index = jnp.where(begins, 0, local_index + 1)
        last_block = place + blocks_left
        earlier = parent_draw % jnp.maximum(local_index, 1)
        trunk_now = (trunk_draw == 1) | (group_ids == forced_group) & (place == MAXB - 1)
        parent_local = jnp.where(local_index == 0, 0, jnp.where(trunk_now, local_index - 1, earlier))
        return ((blocks_left, local_index), (last_block, parent_local))
    zero_rows = jnp.zeros((group_count,), jnp.int32)
    final_state, (tree_ids, parent_ids) = lax.scan(advance, (zero_rows, zero_rows), (size_scores, parent_draws, trunk_draws, jnp.arange(GBLK, dtype=jnp.int32)))
    tree_ids = tree_ids.T
    parent_ids = parent_ids.T
    segment_ids = jnp.repeat(tree_ids, BLK, axis=1).reshape(-1)
    return (segment_ids.astype(jnp.int32), parent_ids.reshape(-1).astype(jnp.int32))


def draw_segments(key, part):
    layout = tree_layout(key)
    return layout[0]


def draw_parents(key, part):
    layout = tree_layout(key)
    return layout[1]


def steps_of(own_key, shape, cuts, low, high):
    gain, own = 1.0, jax.random.fold_in(own_key, 6)
    for position, blocks in cuts:
        steps = jnp.exp(jax.random.uniform(jax.random.fold_in(own, position), (blocks,), jnp.float32, low / len(cuts), high / len(cuts)))
        gain = gain * jnp.repeat(steps, shape[position] // blocks).reshape([-1 if axis == position else 1 for axis in range(len(shape))])
    return gain


def centred(stream_key, shape, width, most, cuts=(), held_as=jnp.bfloat16):
    entries = width * jax.random.normal(stream_key, shape, jnp.float32)
    if cuts:
        entries = entries * steps_of(stream_key, shape, cuts, -0.22, 0.18)
    return jnp.clip(entries, -most, most).astype(held_as)


def setup_inputs(seed: int = 0) -> dict:
    streams_of = jax.random.split(jax.random.key(seed), 14)
    hidden_in = centred(streams_of[0], (TOKENS, D), 1.0, 6.0, ((0, 32),))
    gain_attn = jnp.clip(1.0 + 0.1 * jax.random.normal(streams_of[1], (D,), jnp.float32), 0.5, 1.5).astype(jnp.bfloat16)
    w_query = centred(streams_of[2], (D, H * HD), D ** -0.5, 0.125, ((1, 4),))
    w_key = centred(streams_of[3], (D, KV * HD), D ** -0.5, 0.125, ((1, 4),))
    w_value = centred(streams_of[4], (D, KV * HD), D ** -0.5, 0.125, ((1, 4),))
    w_out = centred(streams_of[5], (H * HD, D), (H * HD // 16) ** -0.5, 0.5, ((0, 4),))
    gain_ffn = jnp.clip(1.0 + 0.1 * jax.random.normal(streams_of[6], (D,), jnp.float32), 0.5, 1.5).astype(jnp.bfloat16)
    w_gate = centred(streams_of[7], (D, FF), D ** -0.5, 0.125, ((1, 4),))
    w_up = centred(streams_of[8], (D, FF), D ** -0.5, 0.125, ((1, 4),))
    w_down = centred(streams_of[9], (FF, D), FF ** -0.5, 0.0625, ((0, 4),))
    segments = draw_segments(jax.random.fold_in(streams_of[13], 71), 0)
    parents = draw_parents(jax.random.fold_in(streams_of[13], 71), 0)
    cotangent = centred(streams_of[12], (TOKENS, D), 1.0, 6.0, ((0, 32),))
    return {"hidden_in": hidden_in, "gain_attn": gain_attn, "w_query": w_query, "w_key": w_key, "w_value": w_value, "w_out": w_out, "gain_ffn": gain_ffn, "w_gate": w_gate, "w_up": w_up, "w_down": w_down, "segments": segments, "parents": parents, "cotangent": cotangent}


NORM_EPS = 1e-05
ROPE_BASE = 1000000.0
HIGHEST = lax.Precision.HIGHEST

@jax.custom_vjp
def low(v):
    return lax.optimization_barrier(v.astype(jnp.bfloat16)).astype(jnp.float32)

@jax.custom_vjp
def low_back(v):
    return v

def low_keep(v):
    return (low(v), None)

def low_pass(kept, grad):
    return (grad,)

def back_keep(v):
    return (v, None)

def back_low(kept, grad):
    return (low(grad),)
low.defvjp(low_keep, low_pass)
low_back.defvjp(back_keep, back_low)

def tree_tables(segment_ids, parent_ids):
    block_count = parent_ids.shape[0]
    first_ids = segment_ids.reshape(block_count, -1)[:, 0]
    block_iota = jnp.arange(block_count, dtype=jnp.int32)
    same_tree = first_ids[:, None] == first_ids[None, :]
    tree_start = lax.optimization_barrier(jnp.min(jnp.where(same_tree, block_iota[None, :], block_count), axis=1)).astype(jnp.int32)
    parent_block = tree_start + parent_ids
    climb_step = (block_iota[None, :] == parent_block[:, None]).astype(jnp.float32)

    def climb(step_index, reach_now):
        return jnp.minimum(reach_now + jnp.dot(reach_now, climb_step, precision=HIGHEST), 1.0)
    ancestry = lax.fori_loop(0, MAXB - 1, climb, jnp.eye(block_count, dtype=jnp.float32))
    return (ancestry, lax.optimization_barrier(jnp.sum(ancestry, axis=1)) - 1.0)

def rope_tables(depth):
    token_total = depth.shape[0] * BLK
    offsets = (jnp.arange(token_total, dtype=jnp.int32) % BLK).astype(jnp.float32)
    places = jnp.repeat(depth, BLK) * BLK + offsets
    freq_index = jnp.arange(HD // 2, dtype=jnp.int32).astype(jnp.float32)
    inverse_freq = ROPE_BASE ** (-2.0 * freq_index / HD)
    angles = places[:, None] * inverse_freq[None, :]
    angles = jnp.concatenate([angles, angles], axis=1)
    return (jnp.cos(angles)[:, None, :], jnp.sin(angles)[:, None, :])

def rotate(heads_in, cosine, sine):
    half_width = heads_in.shape[-1] // 2
    turned = jnp.concatenate([-heads_in[..., half_width:], heads_in[..., :half_width]], axis=-1)
    return heads_in * cosine + turned * sine

def visible(ancestry, first_row, block_rows, token_total):
    sub_table = lax.dynamic_slice_in_dim(ancestry, first_row // BLK, block_rows // BLK, 0)
    spread_table = jnp.broadcast_to(sub_table[:, None, :, None], (block_rows // BLK, BLK, sub_table.shape[1], BLK))
    row_ids = first_row + jnp.arange(block_rows, dtype=jnp.int32)
    col_ids = jnp.arange(token_total, dtype=jnp.int32)
    return (spread_table.reshape(block_rows, token_total) > 0.5) & (col_ids[None, :] <= row_ids[:, None])

def attend(queries, key_heads, value_heads, ancestry):
    token_total, head_count = (queries.shape[0], queries.shape[1])
    block_rows = min(512, token_total)
    repeat_count = head_count // key_heads.shape[1]
    keys_wide = jnp.repeat(key_heads, repeat_count, axis=1)
    values_wide = jnp.repeat(value_heads, repeat_count, axis=1)
    scale = HD ** (-0.5)

    def one_block(block_item):
        query_block, block_index = block_item
        scores = low_back(jnp.einsum('qhd,khd->hqk', query_block, keys_wide, precision=HIGHEST) * scale)
        allowed = visible(ancestry, block_index * block_rows, block_rows, token_total)
        scores = jnp.where(allowed[None], scores, -1e+30)
        row_top = lax.optimization_barrier(jnp.max(scores, axis=-1, keepdims=True))
        exp_scores = jnp.exp(scores - row_top)
        soft_weights = exp_scores / lax.optimization_barrier(jnp.sum(exp_scores, axis=-1, keepdims=True))
        return jnp.einsum('hqk,khd->qhd', low(soft_weights), values_wide, precision=HIGHEST)
    block_count = token_total // block_rows
    blocks_out = lax.map(jax.checkpoint(one_block), (queries.reshape(block_count, block_rows, head_count, HD), jnp.arange(block_count, dtype=jnp.int32)))
    return blocks_out.reshape(token_total, head_count * HD)

def layer_forward(group_rows, segment_ids, parent_ids, gain_attn, w_query, w_key, w_value, w_out, gain_ffn, w_gate, w_up, w_down):
    ancestry, depth = tree_tables(segment_ids, parent_ids)
    cosine, sine = rope_tables(depth)
    token_total = group_rows.shape[0]
    query_cols = H * HD // N_TENSOR
    key_cols = KV * HD // N_TENSOR
    unit_cols = FF // N_TENSOR
    normed_attn = low(group_rows * lax.rsqrt(lax.optimization_barrier(jnp.mean(group_rows * group_rows, axis=-1, keepdims=True)) + NORM_EPS) * gain_attn)
    query_parts, key_parts, value_parts = ([], [], [])
    for shard_index in range(N_TENSOR):
        own_rows = low_back(normed_attn)
        query_parts.append(low_back(jnp.dot(own_rows, w_query[:, shard_index * query_cols:(shard_index + 1) * query_cols], precision=HIGHEST)))
        key_parts.append(low_back(jnp.dot(own_rows, w_key[:, shard_index * key_cols:(shard_index + 1) * key_cols], precision=HIGHEST)))
        value_parts.append(low_back(jnp.dot(own_rows, w_value[:, shard_index * key_cols:(shard_index + 1) * key_cols], precision=HIGHEST)))
    queries = low(rotate(jnp.concatenate(query_parts, axis=1).reshape(token_total, H, HD), cosine, sine))
    key_rows = low(rotate(jnp.concatenate(key_parts, axis=1).reshape(token_total, KV, HD), cosine, sine))
    value_rows = low(jnp.concatenate(value_parts, axis=1).reshape(token_total, KV, HD))
    mixed_heads = low(low_back(attend(queries, key_rows, value_rows, ancestry)))
    attn_terms = [low(jnp.dot(mixed_heads[:, shard_index * query_cols:(shard_index + 1) * query_cols], w_out[shard_index * query_cols:(shard_index + 1) * query_cols], precision=HIGHEST)) for shard_index in range(N_TENSOR)]
    middle = group_rows + low_back(sum(attn_terms))
    normed_ffn = low(middle * lax.rsqrt(lax.optimization_barrier(jnp.mean(middle * middle, axis=-1, keepdims=True)) + NORM_EPS) * gain_ffn)
    ffn_terms = []
    for shard_index in range(N_TENSOR):
        own_rows = low_back(normed_ffn)
        column_range = slice(shard_index * unit_cols, (shard_index + 1) * unit_cols)
        gate_pre = low_back(jnp.dot(own_rows, w_gate[:, column_range], precision=HIGHEST))
        up_pre = low_back(jnp.dot(own_rows, w_up[:, column_range], precision=HIGHEST))
        hidden_act = low(gate_pre * jax.nn.sigmoid(gate_pre) * up_pre)
        ffn_terms.append(low(jnp.dot(hidden_act, w_down[column_range], precision=HIGHEST)))
    return middle + low_back(sum(ffn_terms))

def reference(hidden_in, gain_attn, w_query, w_key, w_value, w_out, gain_ffn, w_gate, w_up, w_down, segments, parents, cotangent):
    group_tokens = GBLK * BLK
    segment_groups = segments.reshape(N_DP, group_tokens)
    parent_groups = parents.reshape(N_DP, GBLK)

    def forward(rows_all, *weights):

        def one_group(running, group_item):
            group_rows, segment_ids, parent_ids = group_item
            return (running, jax.checkpoint(layer_forward)(group_rows, segment_ids, parent_ids, *weights))
        unused, group_outs = lax.scan(one_group, None, (rows_all.reshape(N_DP, group_tokens, D), segment_groups, parent_groups))
        return group_outs.reshape(N_DP * group_tokens, D)
    inputs_wide = [array_in.astype(jnp.float32) for array_in in (hidden_in, gain_attn, w_query, w_key, w_value, w_out, gain_ffn, w_gate, w_up, w_down)]
    result, pullback = jax.vjp(forward, *inputs_wide)
    grads = pullback(cotangent.astype(jnp.float32))
    return (result.astype(jnp.bfloat16), grads[0].astype(jnp.bfloat16), grads[1], grads[2], grads[3], grads[4], grads[5], grads[6], grads[7], grads[8], grads[9])
```

```python
import functools
import math

import jax
import jax.numpy as jnp
from jax import lax
from jax.experimental import pallas as pl
from jax.experimental.pallas import tpu as pltpu
from jax.sharding import PartitionSpec as P

HD = 128
BLK = 128
NORM_EPS = 1e-05
ROPE_BASE = 1000000.0
SCALE = HD ** (-0.5)
SCALE2 = SCALE * math.log2(math.e)
NEG = -1e30
BF = jnp.bfloat16
F32 = jnp.float32
VMEM_LIMIT = 56 * 1024 * 1024


def mm(a, b):
    return jnp.dot(a, b, preferred_element_type=F32)


def mm_bt(a, b):
    return lax.dot_general(a, b, (((1,), (1,)), ((), ())), preferred_element_type=F32)


def mm_at(a, b):
    return lax.dot_general(a, b, (((0,), (0,)), ((), ())), preferred_element_type=F32)


def tree_tables(segment_ids, parent_ids):
    block_count = parent_ids.shape[0]
    first_ids = segment_ids.reshape(block_count, -1)[:, 0]
    block_iota = jnp.arange(block_count, dtype=jnp.int32)
    same_tree = first_ids[:, None] == first_ids[None, :]
    tree_start = jnp.min(jnp.where(same_tree, block_iota[None, :], block_count), axis=1)
    parent_block = tree_start + parent_ids
    step = (block_iota[None, :] == parent_block[:, None]) | (
        block_iota[None, :] == block_iota[:, None]
    )
    for _ in range(3):
        step = jnp.any(step[:, :, None] & step[None, :, :], axis=1)
    ancestry = step.astype(F32)
    return ancestry, jnp.sum(ancestry, axis=1) - 1.0


def rope_tables(depth):
    token_total = depth.shape[0] * BLK
    offsets = (jnp.arange(token_total, dtype=jnp.int32) % BLK).astype(F32)
    places = jnp.repeat(depth, BLK) * BLK + offsets
    freq_index = jnp.arange(HD // 2, dtype=jnp.int32).astype(F32)
    inverse_freq = ROPE_BASE ** (-2.0 * freq_index / HD)
    angles = places[:, None] * inverse_freq[None, :]
    cosine, sine = jnp.cos(angles), jnp.sin(angles)
    return jnp.concatenate([cosine, cosine], axis=1), jnp.concatenate([-sine, sine], axis=1)


def head_cols(h):
    return slice(h * HD, (h + 1) * HD)


def causal_tile(rep):
    rows = lax.broadcasted_iota(jnp.int32, (BLK, BLK), 0)
    cols = lax.broadcasted_iota(jnp.int32, (BLK, BLK), 1)
    tile = cols <= rows
    return jnp.concatenate([tile] * rep, axis=0) if rep > 1 else tile


def stack_heads(ref, rows, first, rep):
    parts = [ref[rows, head_cols(first + i)] for i in range(rep)]
    return jnp.concatenate(parts, axis=0) if rep > 1 else parts[0]


def attn_fwd_kernel(x_ref, wq_ref, wk_ref, wv_ref, cos_ref, sin_ref, bias_ref, q_ref, k_ref, v_ref, m_ref, lse_ref):
    tokens = x_ref.shape[0]
    heads = wq_ref.shape[1] // HD
    kv_heads = wk_ref.shape[1] // HD
    rep = heads // kv_heads
    for r in range(tokens // 256):
        rows = slice(r * 256, (r + 1) * 256)
        x = x_ref[rows, :]
        cosine, sine = cos_ref[rows, :], sin_ref[rows, :]
        for w_ref, out_ref, count in ((wq_ref, q_ref, heads), (wk_ref, k_ref, kv_heads)):
            raw = mm(x, w_ref[...])
            for h in range(count):
                u = raw[:, head_cols(h)]
                out_ref[rows, head_cols(h)] = (u * cosine + pltpu.roll(u, HD // 2, 1) * sine).astype(BF)
        v_ref[rows, :] = mm(x, wv_ref[...]).astype(BF)
    causal = causal_tile(rep)
    for g in range(kv_heads):
        for b in range(tokens // BLK):
            rows = slice(b * BLK, (b + 1) * BLK)
            q = stack_heads(q_ref, rows, g * rep, rep)
            s_diag = jnp.where(causal, mm_bt(q, k_ref[rows, head_cols(g)]) * SCALE2, NEG)
            top = jnp.max(s_diag, axis=1, keepdims=True)
            if b:
                past = slice(0, b * BLK)
                s_past = mm_bt(q, k_ref[past, head_cols(g)]) * SCALE2 + bias_ref[b : b + 1, past]
                top = jnp.maximum(top, jnp.max(s_past, axis=1, keepdims=True))
            e_diag = jnp.exp2(s_diag - top)
            mass = jnp.sum(e_diag, axis=1, keepdims=True)
            out = mm(e_diag.astype(BF), v_ref[rows, head_cols(g)])
            if b:
                e_past = jnp.exp2(s_past - top)
                mass = mass + jnp.sum(e_past, axis=1, keepdims=True)
                out = out + mm(e_past.astype(BF), v_ref[past, head_cols(g)])
            out = (out / mass).astype(BF)
            lse = jnp.broadcast_to(top + jnp.log2(mass), (rep * BLK, HD))
            for i in range(rep):
                m_ref[rows, head_cols(g * rep + i)] = out[i * BLK : (i + 1) * BLK]
                lse_ref[rows, head_cols(g * rep + i)] = lse[i * BLK : (i + 1) * BLK]


def attn_bwd_kernel(q_ref, k_ref, v_ref, o_ref, lse_ref, do_ref, cos_ref, sin_ref, bias_ref, d_ref, dk_acc, dv_acc):
    tokens = q_ref.shape[0]
    heads = q_ref.shape[1] // HD
    kv_heads = k_ref.shape[1] // HD
    rep = heads // kv_heads
    causal = causal_tile(rep)

    def turn_back(grad, rows):
        return (grad * cos_ref[rows, :] - pltpu.roll(grad, HD // 2, 1) * sin_ref[rows, :]).astype(BF)

    for g in range(kv_heads):
        for b in range(tokens // BLK - 1, -1, -1):
            rows = slice(b * BLK, (b + 1) * BLK)
            q = stack_heads(q_ref, rows, g * rep, rep)
            do = stack_heads(do_ref, rows, g * rep, rep)
            o = stack_heads(o_ref, rows, g * rep, rep)
            lse = stack_heads(lse_ref, rows, g * rep, rep)[:, :1]
            delta = jnp.sum(do.astype(F32) * o.astype(F32), axis=1, keepdims=True)
            k_d = k_ref[rows, head_cols(g)]
            p = jnp.where(causal, jnp.exp2(mm_bt(q, k_d) * SCALE2 - lse), 0.0)
            ds = (p * (mm_bt(do, v_ref[rows, head_cols(g)]) - delta)).astype(BF)
            dq = mm(ds, k_d)
            dk = mm_at(ds, q)
            dv = mm_at(p.astype(BF), do)
            if b < tokens // BLK - 1:
                dk = dk + dk_acc[rows, :]
                dv = dv + dv_acc[rows, :]
            d_ref[rows, head_cols(heads + g)] = turn_back(dk * SCALE, rows)
            d_ref[rows, head_cols(heads + kv_heads + g)] = dv.astype(BF)
            if b:
                past = slice(0, b * BLK)
                k_p = k_ref[past, head_cols(g)]
                p = jnp.exp2(mm_bt(q, k_p) * SCALE2 + (bias_ref[b : b + 1, past] - lse))
                ds = (p * (mm_bt(do, v_ref[past, head_cols(g)]) - delta)).astype(BF)
                dq = dq + mm(ds, k_p)
                dk = mm_at(ds, q)
                dv = mm_at(p.astype(BF), do)
                if b < tokens // BLK - 1:
                    dk = dk + dk_acc[past, :]
                    dv = dv + dv_acc[past, :]
                dk_acc[past, :] = dk
                dv_acc[past, :] = dv
            dq = dq * SCALE
            for i in range(rep):
                d_ref[rows, head_cols(g * rep + i)] = turn_back(dq[i * BLK : (i + 1) * BLK], rows)


def send(src, dst, send_sem, recv_sem, rank):
    return pltpu.make_async_remote_copy(
        src_ref=src,
        dst_ref=dst,
        send_sem=send_sem,
        recv_sem=recv_sem,
        device_id={"tensor": rank},
        device_id_type=pl.DeviceIdType.MESH,
    )


def line_barrier(t, n):
    barrier = pltpu.get_barrier_semaphore()

    @pl.when(t > 0)
    def _():
        pl.semaphore_signal(barrier, inc=1, device_id={"tensor": t - 1}, device_id_type=pl.DeviceIdType.MESH)

    @pl.when(t < n - 1)
    def _():
        pl.semaphore_signal(barrier, inc=1, device_id={"tensor": t + 1}, device_id_type=pl.DeviceIdType.MESH)

    is_end = (t == 0) | (t == n - 1)

    @pl.when(is_end)
    def _():
        pl.semaphore_wait(barrier, 1)

    @pl.when(jnp.logical_not(is_end))
    def _():
        pl.semaphore_wait(barrier, 2)


def arrival_order(t, n):
    near = jnp.minimum(t, n - 1 - t)
    order = [t]
    for i in range(1, n):
        both = t - (i + 1) // 2 if i % 2 else t + i // 2
        one_side = jnp.where(t > n - 1 - t, t - (i - near), t + (i - near))
        order.append(jnp.where(i <= 2 * near, both, one_side))
    return order


def ffn_kernel(
    n,
    own_ref,
    cot_ref,
    wg_hbm,
    wu_hbm,
    wd_hbm,
    h_out,
    gg_out,
    ug_out,
    n_out,
    fb_out,
    fi_out,
    wg_ref,
    wu_ref,
    wd_ref,
    n_buf,
    c_buf,
    h_st,
    gg_st,
    ug_st,
    fb_st,
    fi_part,
    got,
    fb_acc,
    fi_acc,
    w_sem,
    c_sem,
    st_sem,
    n_sem,
    ag_send,
    ag_recv,
    rs_send,
    rs_recv,
):
    t = lax.axis_index("tensor")
    rows, width = own_ref.shape
    units = wg_ref.shape[1]
    tile = min(512, units)
    tiles = units // tile
    parts = rs_send.shape[2]
    part_rows = rows // parts
    order = arrival_order(t, n)
    is_mid = (t > 0) & (t < n - 1)

    def load_weights(j):
        cols = pl.ds(j * tile, tile)
        return [
            pltpu.make_async_copy(wg_hbm.at[:, cols], wg_ref.at[:, cols], w_sem.at[0, j]),
            pltpu.make_async_copy(wu_hbm.at[:, cols], wu_ref.at[:, cols], w_sem.at[1, j]),
            pltpu.make_async_copy(wd_hbm.at[cols, :], wd_ref.at[cols, :], w_sem.at[2, j]),
        ]

    def load_cot(i):
        return pltpu.make_async_copy(cot_ref.at[order[i]], c_buf.at[i % 2], c_sem.at[i % 2])

    def gather(s, to_right, src=None):
        return send(
            n_buf.at[s] if src is None else src,
            n_buf.at[s],
            ag_send.at[0 if to_right else 1, s],
            ag_recv.at[s],
            t + 1 if to_right else t - 1,
        )

    def keep_rows(i):
        return pltpu.make_async_copy(own_ref if i == 0 else n_buf.at[order[i]], n_out.at[order[i]], n_sem.at[i])

    def scatter(s, c, to_right):
        d, slot = (0, s - 1) if to_right else (1, n - 2 - s)
        piece = pl.ds(c * part_rows, part_rows)
        return send(
            fi_part.at[s, piece],
            got.at[d, slot, piece],
            rs_send.at[d, slot, c],
            rs_recv.at[d, slot, c],
            t + 1 if to_right else t - 1,
        )

    for copy in load_weights(0):
        copy.start()
    load_cot(0).start()
    line_barrier(t, n)

    @pl.when(t < n - 1)
    def _():
        gather(t, True, own_ref).start()

    @pl.when(t > 0)
    def _():
        gather(t, False, own_ref).start()

    for j in range(1, tiles):
        for copy in load_weights(j):
            copy.start()
    keep_rows(0).start()

    def arrive(i):
        s = order[i]
        gather(s, True).wait_recv()

        @pl.when((s < t) & (t < n - 1))
        def _():
            gather(s, True).start()

        @pl.when((s > t) & (t > 0))
        def _():
            gather(s, False).start()

        keep_rows(i).start()

    def stage_out(i):
        slot = i % 2
        return [
            pltpu.make_async_copy(st.at[slot], out.at[order[i]], st_sem.at[k, slot])
            for k, (st, out) in enumerate(((h_st, h_out), (gg_st, gg_out), (ug_st, ug_out), (fb_st, fb_out)))
        ]

    for i in range(n):
        s = order[i]
        slot = i % 2
        if i == 1:
            arrive(1)
            if n > 2:
                pl.when(is_mid)(functools.partial(arrive, 2))
        elif i > 1:
            pl.when(jnp.logical_not(is_mid))(functools.partial(arrive, i))
        if i + 1 < n:
            load_cot(i + 1).start()
        load_cot(i).wait()
        if i >= 2:
            for copy in stage_out(i - 2):
                copy.wait()
        x_ref = own_ref if i == 0 else n_buf.at[s]
        fb_acc[...] = jnp.zeros_like(fb_acc)
        fi_acc[...] = jnp.zeros_like(fi_acc)

        def one_tile(j, carry):
            if i == 0:
                for copy in load_weights(j):
                    copy.wait()
            if 2 <= i < n - 1:
                pl.when(is_mid & (j == tiles // 2))(functools.partial(arrive, i + 1))
            cols = pl.ds(pl.multiple_of(j * tile, tile), tile)
            x = x_ref[...]
            wg, wu, wd = wg_ref[:, cols], wu_ref[:, cols], wd_ref[cols, :]
            gate = mm(x, wg)
            up = mm(x, wu)
            act_grad = mm_bt(c_buf[slot], wd)
            sig = jax.nn.sigmoid(gate)
            silu = gate * sig
            h = (silu * up).astype(BF)
            gg = (act_grad * up * (sig * (1.0 + gate * (1.0 - sig)))).astype(BF)
            ug = (act_grad * silu).astype(BF)
            h_st[slot, :, cols] = h
            gg_st[slot, :, cols] = gg
            ug_st[slot, :, cols] = ug
            for k in range(0, width, 512):
                piece = slice(k, k + 512)
                fb_acc[:, piece] += mm(h, wd_ref[cols, piece])
                fi_acc[:, piece] += mm_bt(gg, wg_ref[piece, cols]) + mm_bt(ug, wu_ref[piece, cols])
            return carry

        lax.fori_loop(0, tiles, one_tile, 0)
        fb_st[slot] = fb_acc[...].astype(BF)
        for copy in stage_out(i):
            copy.start()
        if i == 0:
            fi_out[...] = fi_acc[...]
        else:
            fi_part[s] = fi_acc[...].astype(BF)

            @pl.when(t == 0)
            def _():
                for c in range(parts):
                    scatter(i, c, True).start()

            @pl.when(t == n - 1)
            def _():
                for c in range(parts):
                    scatter(n - 1 - i, c, False).start()

    for index in range(1, n):
        for c in range(parts):
            piece = pl.ds(c * part_rows, part_rows)
            for to_right in (True, False):
                s = index if to_right else n - 1 - index
                d = 0 if to_right else 1
                has_source = t > 0 if to_right else t < n - 1
                beyond = s > t if to_right else s < t

                @pl.when(has_source & beyond)
                def _():
                    scatter(s, c, to_right).wait_recv()
                    total = fi_part[s, piece].astype(F32) + got[d, index - 1, piece].astype(F32)
                    fi_part[s, piece] = total.astype(BF)
                    scatter(s, c, to_right).start()

                @pl.when(has_source & (s == t))
                def _():
                    scatter(s, c, to_right).wait_recv()
                    fi_out[piece] += got[d, index - 1, piece].astype(F32)

    for i in range(max(0, n - 2), n):
        for copy in stage_out(i):
            copy.wait()
    for i in range(n):
        keep_rows(i).wait()
    for s in range(n):
        for to_right in (True, False):
            goes_on = t < n - 1 if to_right else t > 0

            @pl.when(goes_on & (s <= t if to_right else s >= t))
            def _():
                gather(s, to_right).wait_send()

            @pl.when(goes_on & (s > t if to_right else s < t))
            def _():
                for c in range(parts):
                    scatter(s, c, to_right).wait_send()


def ffn_call(n, own_rows, cot_all, w_gate, w_up, w_down):
    rows, width = own_rows.shape
    units = w_gate.shape[1]
    tile = min(512, units)
    tiles = units // tile
    parts = max(1, rows // 64)
    tall = jax.ShapeDtypeStruct((n, rows, units), BF)
    wide = jax.ShapeDtypeStruct((n, rows, width), BF)
    any_spec = pl.BlockSpec(memory_space=pl.ANY)
    vmem_spec = pl.BlockSpec(memory_space=pltpu.VMEM)
    dma = pltpu.SemaphoreType.DMA
    return pl.pallas_call(
        functools.partial(ffn_kernel, n),
        out_shape=[tall, tall, tall, wide, wide, jax.ShapeDtypeStruct((rows, width), F32)],
        in_specs=[vmem_spec] + [any_spec] * 4,
        out_specs=[any_spec] * 5 + [vmem_spec],
        scratch_shapes=[
            pltpu.VMEM((width, units), BF),
            pltpu.VMEM((width, units), BF),
            pltpu.VMEM((units, width), BF),
            pltpu.VMEM((n, rows, width), BF),
            pltpu.VMEM((2, rows, width), BF),
            pltpu.VMEM((2, rows, units), BF),
            pltpu.VMEM((2, rows, units), BF),
            pltpu.VMEM((2, rows, units), BF),
            pltpu.VMEM((2, rows, width), BF),
            pltpu.VMEM((n, rows, width), BF),
            pltpu.VMEM((2, n - 1, rows, width), BF),
            pltpu.VMEM((rows, width), F32),
            pltpu.VMEM((rows, width), F32),
            dma((3, tiles)),
            dma((2,)),
            dma((4, 2)),
            dma((n,)),
            dma((2, n)),
            dma((n,)),
            dma((2, n - 1, parts)),
            dma((2, n - 1, parts)),
        ],
        compiler_params=pltpu.CompilerParams(
            vmem_limit_bytes=63 * 1024 * 1024, collective_id=1, has_side_effects=True
        ),
        cost_estimate=pl.CostEstimate(
            flops=12 * n * rows * width * units, bytes_accessed=6 * width * units, transcendentals=0
        ),
        name="ffn",
    )(own_rows, cot_all, w_gate, w_up, w_down)


def full_call(kernel, out_shapes, args, scratch=(), flops=0, name=None):
    spec = pl.BlockSpec(memory_space=pltpu.VMEM)
    return pl.pallas_call(
        kernel,
        out_shape=out_shapes,
        in_specs=[spec] * len(args),
        out_specs=[spec] * len(out_shapes),
        scratch_shapes=list(scratch),
        compiler_params=pltpu.CompilerParams(vmem_limit_bytes=VMEM_LIMIT),
        cost_estimate=pl.CostEstimate(flops=flops, bytes_accessed=flops // 400, transcendentals=0),
        name=name,
    )(*args)


def normalize(rows_wide, gain_wide):
    inverse = lax.rsqrt(jnp.mean(rows_wide * rows_wide, axis=-1, keepdims=True) + NORM_EPS)
    scaled_rows = rows_wide * inverse
    return scaled_rows, inverse, (scaled_rows * gain_wide).astype(BF)


def norm_back(normed_grad, scaled_rows, inverse, gain_wide):
    weighted = normed_grad * gain_wide
    return inverse * (weighted - scaled_rows * jnp.mean(weighted * scaled_rows, axis=-1, keepdims=True))


def pairs(n, bit):
    return [(i, i ^ bit) for i in range(n)]


def pick(array, index, axis):
    return lax.dynamic_index_in_dim(array, index, axis, keepdims=False)


def dp_scatter(give, keep, n_dp):
    me = lax.axis_index("dp")
    total = keep + lax.ppermute(give, "dp", pairs(n_dp, 1))
    if n_dp != 8:
        bit = 2
        while total.shape[0] > 1:
            parts = total.reshape(-1, 2, *total.shape[1:])
            mine = (me // bit) % 2
            total = pick(parts, mine, 1) + lax.ppermute(pick(parts, 1 - mine, 1), "dp", pairs(n_dp, bit))
            bit *= 2
        return total[0].astype(F32)
    x, y = (me // 2) % 2, me // 4
    cols = total.shape[-1] // 2
    parts = total.reshape(2, 2, *total.shape[1:])
    a, b = parts[..., :cols], parts[..., cols:]
    got_a = lax.ppermute(pick(a, 1 - x, 1), "dp", pairs(n_dp, 2))
    got_b = lax.ppermute(pick(b, 1 - y, 0), "dp", pairs(n_dp, 4))
    a = pick(a, x, 1) + got_a
    b = pick(b, y, 0) + got_b
    got_a = lax.ppermute(pick(a, 1 - y, 0), "dp", pairs(n_dp, 4))
    got_b = lax.ppermute(pick(b, 1 - x, 0), "dp", pairs(n_dp, 2))
    a = pick(a, y, 0).astype(F32) + got_a.astype(F32)
    b = pick(b, x, 0).astype(F32) + got_b.astype(F32)
    return jnp.concatenate([a, b], axis=-1)


def core_split(rows, n_dp):
    tokens, width = rows.shape
    core = lax.axis_index("dp") % 2
    parts = rows.reshape(tokens, n_dp // 2, 2, width // n_dp)
    return [pick(parts, c, 2).reshape(tokens, width // 2) for c in (1 - core, core)]


def grad_scatter(split_rows, cols, n_dp):
    give, keep = [
        mm_at(part, cols).astype(BF).reshape(n_dp // 2, 2 * part.shape[1] // n_dp, cols.shape[1])
        for part in split_rows
    ]
    return dp_scatter(give, keep, n_dp)


def after(value, *others):
    return lax.optimization_barrier((value, *others))[0]


def shards(n_dp, n_t, hidden_in, gain_attn, w_query, w_key, w_value, w_out, gain_ffn, w_gate, w_up, w_down, segments, parents, cotangent):
    tokens = segments.shape[0]
    own, width = hidden_in.shape
    q_cols, kv_cols, units = w_query.shape[1], w_key.shape[1], w_gate.shape[1]
    heads = q_cols // HD
    me_t = lax.axis_index("tensor")
    me_dp = lax.axis_index("dp")
    gain_attn_wide = gain_attn.astype(F32)
    gain_ffn_wide = gain_ffn.astype(F32)

    def ring(value, shift):
        return lax.ppermute(value, "tensor", [(i, (i + shift) % n_t) for i in range(n_t)])

    rows_wide = hidden_in.astype(F32)
    scaled_attn, inverse_attn, normed_attn = normalize(rows_wide, gain_attn_wide)
    x_all = lax.all_gather(normed_attn, "tensor", axis=0, tiled=True)

    share = q_cols // n_dp
    w_share = lax.dynamic_slice_in_dim(w_out, me_dp * share, share, 0)
    w_share = jnp.stack([ring(w_share, d) for d in range(1, n_t)])
    w_rest = lax.all_gather(after(w_share, x_all), "dp", axis=1, tiled=True)
    cot_all = lax.all_gather(after(cotangent, w_rest), "tensor", axis=0, tiled=True)

    ancestry, depth = tree_tables(segments, parents)
    cosine, sine = rope_tables(depth)
    bias = jnp.where(jnp.repeat(ancestry, BLK, axis=1) > 0.5, 0.0, NEG)

    queries, keys, values, mixed, lse = full_call(
        attn_fwd_kernel,
        [
            jax.ShapeDtypeStruct((tokens, q_cols), BF),
            jax.ShapeDtypeStruct((tokens, kv_cols), BF),
            jax.ShapeDtypeStruct((tokens, kv_cols), BF),
            jax.ShapeDtypeStruct((tokens, q_cols), BF),
            jax.ShapeDtypeStruct((tokens, q_cols), F32),
        ],
        (x_all, w_query, w_key, w_value, cosine, sine, bias),
        flops=2 * tokens * width * (q_cols + 2 * kv_cols) + 4 * heads * tokens * tokens * HD,
        name="attn_fwd",
    )

    mixed_blocks = mixed.reshape(n_t, own, q_cols)
    mixed_own = [pick(mixed_blocks, me_t, 0)] + [
        ring(pick(mixed_blocks, (me_t + d) % n_t, 0), d) for d in range(1, n_t)
    ]
    w_rest = w_rest.reshape(n_t - 1, q_cols, width)
    w_pieces = [w_out] + [w_rest[d] for d in range(n_t - 1)]
    branch = mm(mixed_own[0], w_pieces[0])
    for d in range(1, n_t):
        branch = branch + mm(mixed_own[d], w_pieces[d])
    middle = rows_wide + branch
    scaled_ffn, inverse_ffn, normed_ffn = normalize(middle, gain_ffn_wide)

    h_all, gg_all, ug_all, n_all, fb_part, ffn_in_grad = ffn_call(
        n_t, normed_ffn, cot_all.reshape(n_t, own, width), w_gate, w_up, w_down
    )
    h_all, gg_all, ug_all = [a.reshape(tokens, units) for a in (h_all, gg_all, ug_all)]
    n_all = n_all.reshape(tokens, width)
    fb_sum = lax.psum_scatter(fb_part.reshape(tokens, width), "tensor", scatter_dimension=0, tiled=True)
    output = (middle + fb_sum.astype(F32)).astype(BF)

    cot_split = core_split(cot_all.reshape(tokens, width), n_dp)
    normed_split = core_split(n_all, n_dp)
    w_down_grad = grad_scatter(cot_split, h_all, n_dp).T
    w_gate_grad = grad_scatter(normed_split, gg_all, n_dp)
    w_up_grad = grad_scatter(normed_split, ug_all, n_dp)

    middle_grad = cotangent.astype(F32) + norm_back(ffn_in_grad, scaled_ffn, inverse_ffn, gain_ffn_wide)
    branch_grad = middle_grad.astype(BF)
    mixed_grads = [mm_bt(branch_grad, w_pieces[d]).astype(BF) for d in range(n_t)]
    mixed_grads = [mixed_grads[0]] + [ring(mixed_grads[d], n_t - d) for d in range(1, n_t)]
    mixed_grad = jnp.roll(jnp.concatenate(mixed_grads, axis=0), me_t * own, axis=0)

    (project_grad,) = full_call(
        attn_bwd_kernel,
        [jax.ShapeDtypeStruct((tokens, q_cols + 2 * kv_cols), BF)],
        (queries, keys, values, mixed, lse, mixed_grad, cosine, sine, bias),
        scratch=[pltpu.VMEM((tokens, HD), F32)] * 2,
        flops=10 * heads * tokens * tokens * HD,
        name="attn_bwd",
    )
    dq, dk, dv = (
        project_grad[:, :q_cols],
        project_grad[:, q_cols : q_cols + kv_cols],
        project_grad[:, q_cols + kv_cols :],
    )
    w_project = jnp.concatenate([w_query, w_key, w_value], axis=1)
    attn_in_part = mm_bt(project_grad, w_project).astype(BF)
    attn_in_grad = lax.psum_scatter(attn_in_part, "tensor", scatter_dimension=0, tiled=True).astype(F32)

    mixed_wide = jnp.concatenate(mixed_own, axis=1)
    out_grad = grad_scatter(core_split(branch_grad, n_dp), mixed_wide, n_dp)
    out_parts = out_grad.reshape(-1, n_t, q_cols)
    w_out_grad = out_parts[:, 0]
    for d in range(1, n_t):
        w_out_grad = w_out_grad + ring(out_parts[:, d].astype(BF), n_t - d).astype(F32)
    w_out_grad = w_out_grad.T

    project_wgrad = grad_scatter(core_split(x_all, n_dp), project_grad, n_dp)
    w_query_grad = project_wgrad[:, :q_cols]
    w_key_grad = project_wgrad[:, q_cols : q_cols + kv_cols]
    w_value_grad = project_wgrad[:, q_cols + kv_cols :]

    def own_rows(array):
        return lax.dynamic_slice_in_dim(array, me_dp * (width // n_dp), width // n_dp, 0).astype(F32)

    gain_sums = jnp.stack(
        [
            jnp.sum(own_rows(w_project) * project_wgrad, axis=1),
            jnp.sum(own_rows(w_gate) * w_gate_grad, axis=1) + jnp.sum(own_rows(w_up) * w_up_grad, axis=1),
        ]
    )
    bit = 1
    while bit < n_t:
        gain_sums = gain_sums + lax.ppermute(gain_sums, "tensor", pairs(n_t, bit))
        bit *= 2
    gain_attn_grad = gain_sums[0] / own_rows(gain_attn)
    gain_ffn_grad = gain_sums[1] / own_rows(gain_ffn)

    input_grad = (middle_grad + norm_back(attn_in_grad, scaled_attn, inverse_attn, gain_attn_wide)).astype(BF)
    return (
        output,
        input_grad,
        gain_attn_grad,
        w_query_grad,
        w_key_grad,
        w_value_grad,
        w_out_grad,
        gain_ffn_grad,
        w_gate_grad,
        w_up_grad,
        w_down_grad,
    )


def solution(mesh):
    return jax.shard_map(
        functools.partial(shards, mesh.shape["dp"], mesh.shape["tensor"]),
        mesh=mesh,
        in_specs=(
            P(("dp", "tensor"), None),
            P(),
            P(None, "tensor"),
            P(None, "tensor"),
            P(None, "tensor"),
            P("tensor", None),
            P(),
            P(None, "tensor"),
            P(None, "tensor"),
            P("tensor", None),
            P("dp"),
            P("dp"),
            P(("dp", "tensor"), None),
        ),
        out_specs=(
            P(("dp", "tensor"), None),
            P(("dp", "tensor"), None),
            P("dp"),
            P("dp", "tensor"),
            P("dp", "tensor"),
            P("dp", "tensor"),
            P("tensor", "dp"),
            P("dp"),
            P("dp", "tensor"),
            P("dp", "tensor"),
            P("tensor", "dp"),
        ),
        check_vma=False,
    )
```

```python
import functools
import math
import types

import jax
import jax.numpy as jnp
from jax import lax
from jax.experimental import pallas as pl
from jax.experimental.pallas import tpu as pltpu
from jax.sharding import PartitionSpec as P

HD = 128
BLK = 128
NORM_EPS = 1e-05
ROPE_BASE = 1000000.0
SCALE = HD ** (-0.5)
SCALE2 = SCALE * math.log2(math.e)
NEG = -1e30
BF = jnp.bfloat16
F32 = jnp.float32
VMEM_LIMIT = 56 * 1024 * 1024


def mm(a, b):
    return jnp.dot(a, b, preferred_element_type=F32)


def mm_bt(a, b):
    return lax.dot_general(a, b, (((1,), (1,)), ((), ())), preferred_element_type=F32)


def mm_at(a, b):
    return lax.dot_general(a, b, (((0,), (0,)), ((), ())), preferred_element_type=F32)


def tree_tables(segment_ids, parent_ids):
    block_count = parent_ids.shape[0]
    first_ids = segment_ids.reshape(block_count, -1)[:, 0]
    block_iota = jnp.arange(block_count, dtype=jnp.int32)
    same_tree = first_ids[:, None] == first_ids[None, :]
    tree_start = jnp.min(jnp.where(same_tree, block_iota[None, :], block_count), axis=1)
    parent_block = tree_start + parent_ids
    step = (block_iota[None, :] == parent_block[:, None]) | (
        block_iota[None, :] == block_iota[:, None]
    )
    for _ in range(3):
        step = jnp.any(step[:, :, None] & step[None, :, :], axis=1)
    ancestry = step.astype(F32)
    return ancestry, jnp.sum(ancestry, axis=1) - 1.0


def rope_tables(depth):
    token_total = depth.shape[0] * BLK
    offsets = (jnp.arange(token_total, dtype=jnp.int32) % BLK).astype(F32)
    places = jnp.repeat(depth, BLK) * BLK + offsets
    freq_index = jnp.arange(HD // 2, dtype=jnp.int32).astype(F32)
    inverse_freq = ROPE_BASE ** (-2.0 * freq_index / HD)
    angles = places[:, None] * inverse_freq[None, :]
    cosine, sine = jnp.cos(angles), jnp.sin(angles)
    return jnp.concatenate([cosine, cosine], axis=1), jnp.concatenate([-sine, sine], axis=1)


def head_cols(h):
    return slice(h * HD, (h + 1) * HD)


def causal_tile(rep):
    rows = lax.broadcasted_iota(jnp.int32, (BLK, BLK), 0)
    cols = lax.broadcasted_iota(jnp.int32, (BLK, BLK), 1)
    tile = cols <= rows
    return jnp.concatenate([tile] * rep, axis=0) if rep > 1 else tile


def stack_heads(ref, rows, first, rep):
    parts = [ref[rows, head_cols(first + i)] for i in range(rep)]
    return jnp.concatenate(parts, axis=0) if rep > 1 else parts[0]


def attend_block(b, q_ref, k_ref, v_ref, bias_ref, m_ref, lse_ref, causal, rep):
    rows = slice(b * BLK, (b + 1) * BLK)
    past = slice(0, b * BLK)
    for g in range(k_ref.shape[1] // HD):
        q = stack_heads(q_ref, rows, g * rep, rep)
        s_diag = jnp.where(causal, mm_bt(q, k_ref[rows, head_cols(g)]) * SCALE2, NEG)
        top = jnp.max(s_diag, axis=1, keepdims=True)
        if b:
            s_past = mm_bt(q, k_ref[past, head_cols(g)]) * SCALE2 + bias_ref[b : b + 1, past]
            top = jnp.maximum(top, jnp.max(s_past, axis=1, keepdims=True))
        e_diag = jnp.exp2(s_diag - top)
        mass = jnp.sum(e_diag, axis=1, keepdims=True)
        out = mm(e_diag.astype(BF), v_ref[rows, head_cols(g)])
        if b:
            e_past = jnp.exp2(s_past - top)
            mass = mass + jnp.sum(e_past, axis=1, keepdims=True)
            out = out + mm(e_past.astype(BF), v_ref[past, head_cols(g)])
        out = (out / mass).astype(BF)
        lse = top + jnp.log2(mass)
        for i in range(rep):
            h = g * rep + i
            m_ref[rows, head_cols(h)] = out[i * BLK : (i + 1) * BLK]
            lse_ref[rows, h : h + 1] = lse[i * BLK : (i + 1) * BLK]


def copy_to(src, dst, send_sem, recv_sem, **where):
    return pltpu.make_async_remote_copy(
        src_ref=src,
        dst_ref=dst,
        send_sem=send_sem,
        recv_sem=recv_sem,
        device_id=where,
        device_id_type=pl.DeviceIdType.MESH,
    )


def group_barrier(masks, n, d, t):
    barrier = pltpu.get_barrier_semaphore()
    for k in range(1, n):
        pl.semaphore_signal(
            barrier, inc=1, device_id={"tensor": lax.rem(t + k, n)}, device_id_type=pl.DeviceIdType.MESH
        )
    for mask in masks:
        pl.semaphore_signal(barrier, inc=1, device_id={"dp": d ^ mask}, device_id_type=pl.DeviceIdType.MESH)
    pl.semaphore_wait(barrier, n - 1 + len(masks))


def attn_kernel(
    n_dp,
    n,
    one_hop,
    hidden_ref,
    cot_ref,
    gain_a_ref,
    gain_f_ref,
    wq_hbm,
    wk_hbm,
    wv_hbm,
    wo_hbm,
    cos_ref,
    sin_ref,
    bias_ref,
    x_out,
    cot_out,
    wo_out,
    q_ref,
    k_ref,
    v_ref,
    m_ref,
    lse_ref,
    mixed_ref,
    middle_ref,
    normed_ref,
    own_buf,
    x_buf,
    wq_ref,
    wk_ref,
    wv_ref,
    wo_ref,
    w_sem,
    x_sem,
    misc_sem,
    ag_send,
    ag_recv,
    cot_send,
    cot_recv,
    wz_send,
    wz_recv,
    wp_send,
    wp_recv,
    wc_send,
    wc_recv,
    m_send,
    m_recv,
):
    t, d = lax.axis_index("tensor"), lax.axis_index("dp")
    rows, width = hidden_ref.shape
    q_cols = wq_ref.shape[1]
    heads, kv_heads = q_cols // HD, wk_ref.shape[1] // HD
    rep = heads // kv_heads
    share = q_cols // n_dp
    half = q_cols // 2
    order = arrival_order(t, n)
    is_mid = (t > 0) & (t < n - 1)
    core, plane = lax.rem(d, 2), d // 2
    masks = list(range(2, n_dp, 2))

    load_w = [
        pltpu.make_async_copy(src, dst, w_sem.at[i])
        for i, (src, dst) in enumerate(((wq_hbm, wq_ref), (wk_hbm, wk_ref), (wv_hbm, wv_ref)))
    ]
    own_wo = pltpu.make_async_copy(wo_hbm, wo_ref.at[t], misc_sem.at[0])
    own_cot = pltpu.make_async_copy(cot_ref, cot_out.at[t], misc_sem.at[1])
    for copy in load_w:
        copy.start()
    own_wo.start()
    own_cot.start()

    def norm(values, gain_ref):
        inverse = lax.rsqrt(jnp.mean(values * values, axis=-1, keepdims=True) + NORM_EPS)
        return (values * inverse * gain_ref[...].astype(F32)).astype(BF)

    for r in range(0, rows, 64):
        part = slice(r, r + 64)
        own_buf[part, :] = norm(hidden_ref[part, :].astype(F32), gain_a_ref)
    group_barrier([1, *masks], n, d, t)

    def line_copy(buf, send_sem, recv_sem, s, to_right, src=None):
        return copy_to(
            buf.at[s] if src is None else src,
            buf.at[s],
            send_sem.at[0 if to_right else 1, s],
            recv_sem.at[s],
            tensor=t + 1 if to_right else t - 1,
        )

    gather_x = functools.partial(line_copy, x_buf, ag_send, ag_recv)
    gather_cot = functools.partial(line_copy, cot_out, cot_send, cot_recv)

    def first_hop(gather, src):
        pl.when(t < n - 1)(lambda: gather(t, True, src).start())
        pl.when(t > 0)(lambda: gather(t, False, src).start())

    def arrive(gather, i):
        s = order[i]
        gather(s, True).wait_recv()
        pl.when((s < t) & (t < n - 1))(lambda: gather(s, True).start())
        pl.when((s > t) & (t > 0))(lambda: gather(s, False).start())

    def keep_rows(i):
        return pltpu.make_async_copy(own_buf if i == 0 else x_buf.at[order[i]], x_out.at[order[i]], x_sem.at[i])

    my_rows = pl.ds(pl.multiple_of(core * half + plane * share, 16), share)
    my_half = pl.ds(pl.multiple_of(core * half, 16), half)

    def wo_line(k):
        return copy_to(
            wo_hbm.at[my_rows],
            wo_ref.at[t, my_rows],
            wz_send.at[k - 1],
            wz_recv.at[k - 1],
            tensor=lax.rem(t + k, n),
        )

    def wo_plane(k, j):
        s = lax.rem(t + n - k, n)
        return copy_to(
            wo_ref.at[s, my_rows],
            wo_ref.at[s, my_rows],
            wp_send.at[k - 1, j],
            wp_recv.at[k - 1, j],
            dp=d ^ masks[j],
        )

    def wo_core(k):
        s = lax.rem(t + n - k, n)
        return copy_to(
            wo_ref.at[s, my_half], wo_ref.at[s, my_half], wc_send.at[k - 1], wc_recv.at[k - 1], dp=d ^ 1
        )

    first_hop(gather_x, own_buf)
    for k in range(1, n):
        wo_line(k).start()
    keep_rows(0).start()

    for copy in load_w:
        copy.wait()
    for i in range(n):
        s = order[i]
        if i == 1:
            arrive(gather_x, 1)
            if n > 2:
                pl.when(is_mid)(lambda: arrive(gather_x, 2))
        elif i > 1:
            if i > 2:
                arrive(gather_x, i)
            else:
                pl.when(jnp.logical_not(is_mid))(lambda: arrive(gather_x, 2))
        if i:
            keep_rows(i).start()
        x = own_buf[...] if i == 0 else x_buf[s]
        here = pl.ds(pl.multiple_of(s * rows, rows), rows)
        cosine, sine = cos_ref[here, :], sin_ref[here, :]
        for w_ref, out_ref, count in ((wq_ref, q_ref, heads), (wk_ref, k_ref, kv_heads)):
            raw = mm(x, w_ref[...])
            for h in range(count):
                u = raw[:, head_cols(h)]
                out_ref[here, head_cols(h)] = (u * cosine + pltpu.roll(u, HD // 2, 1) * sine).astype(BF)
        v_ref[here, :] = mm(x, wv_ref[...]).astype(BF)
        if i == 1:
            for k in range(1, n):
                wo_line(k).wait_recv()
                for j in range(len(masks)):
                    wo_plane(k, j).start()
        if i == n - 1:
            first_hop(gather_cot, cot_ref)
            for k in range(1, n):
                for j in range(len(masks)):
                    wo_plane(k, j).wait_recv()
                wo_core(k).start()

    def heads_to(r):
        here = pl.ds(r * rows, rows)
        return copy_to(m_ref.at[here], mixed_ref.at[t], m_send.at[r], m_recv.at[t], tensor=r)

    causal = causal_tile(rep)
    for b in range(n * rows // BLK):
        attend_block(b, q_ref, k_ref, v_ref, bias_ref, m_ref, lse_ref, causal, rep)
        if (b + 1) * BLK % rows == 0:
            r = (b + 1) * BLK // rows - 1
            pl.when(t != r)(lambda: heads_to(r).start())

            @pl.when(t == r)
            def _():
                mixed_ref[r] = m_ref[r * rows : (r + 1) * rows, :]

    if n > 2 and not one_hop:

        @pl.when(is_mid)
        def _():
            arrive(gather_cot, 1)
            arrive(gather_cot, 2)

    own_wo.wait()
    for k in range(1, n):
        s = lax.rem(t + n - k, n)
        copy_to(m_ref.at[pl.ds(0, rows)], mixed_ref.at[s], m_send.at[0], m_recv.at[s], tensor=s).wait_recv()
        wo_core(k).wait_recv()
    keep_wo = pltpu.make_async_copy(wo_ref, wo_out, misc_sem.at[0])
    keep_wo.start()
    for r in range(0, rows, 128):
        part = slice(r, r + 128)
        total = hidden_ref[part, :].astype(F32)
        for s in range(n):
            total = total + mm(mixed_ref[s, part, :], wo_ref[s])
        middle_ref[part, :] = total
        normed_ref[part, :] = norm(total, gain_f_ref)

    if one_hop:
        pl.when(t > 0)(lambda: gather_cot(t - 1, True).wait_recv())
        pl.when(t < n - 1)(lambda: gather_cot(t + 1, False).wait_recv())
    else:
        for i in range(1, n):
            if i > 2:
                arrive(gather_cot, i)
            else:
                pl.when(jnp.logical_not(is_mid))(functools.partial(arrive, gather_cot, i))
    own_cot.wait()
    keep_wo.wait()
    for i in range(n):
        keep_rows(i).wait()
    for k in range(1, n):
        wo_line(k).wait_send()
        wo_core(k).wait_send()
        for j in range(len(masks)):
            wo_plane(k, j).wait_send()
    if one_hop:
        pl.when(t < n - 1)(lambda: gather_cot(t, True).wait_send())
        pl.when(t > 0)(lambda: gather_cot(t, False).wait_send())
    for s in range(n):
        pl.when(t != s)(lambda: heads_to(s).wait_send())
        for to_right in (True, False):
            goes_on = t < n - 1 if to_right else t > 0

            @pl.when(goes_on & (s <= t if to_right else s >= t))
            def _():
                gather_x(s, to_right).wait_send()
                if not one_hop:
                    gather_cot(s, to_right).wait_send()


def attn_call(n_dp, n, one_hop, hidden, cot, gain_a, gain_f, wq, wk, wv, wo, cosine, sine, bias):
    rows, width = hidden.shape
    q_cols, kv_cols = wq.shape[1], wk.shape[1]
    tokens = n * rows
    any_spec = pl.BlockSpec(memory_space=pl.ANY)
    vmem_spec = pl.BlockSpec(memory_space=pltpu.VMEM)
    dma = pltpu.SemaphoreType.DMA
    masks = n_dp // 2 - 1
    shape = jax.ShapeDtypeStruct
    return pl.pallas_call(
        functools.partial(attn_kernel, n_dp, n, one_hop),
        out_shape=[
            shape((n, rows, width), BF),
            shape((n, rows, width), BF),
            shape((n, q_cols, width), BF),
            shape((tokens, q_cols), BF),
            shape((tokens, kv_cols), BF),
            shape((tokens, kv_cols), BF),
            shape((tokens, q_cols), BF),
            shape((tokens, HD), F32),
            shape((n, rows, q_cols), BF),
            shape((rows, width), F32),
            shape((rows, width), BF),
        ],
        in_specs=[vmem_spec, any_spec, vmem_spec, vmem_spec] + [any_spec] * 4 + [vmem_spec] * 3,
        out_specs=[any_spec] * 3 + [vmem_spec] * 8,
        scratch_shapes=[
            pltpu.VMEM((rows, width), BF),
            pltpu.VMEM((n, rows, width), BF),
            pltpu.VMEM((width, q_cols), BF),
            pltpu.VMEM((width, kv_cols), BF),
            pltpu.VMEM((width, kv_cols), BF),
            pltpu.VMEM((n, q_cols, width), BF),
            dma((3,)),
            dma((n,)),
            dma((2,)),
            dma((2, n)),
            dma((n,)),
            dma((2, n)),
            dma((n,)),
            dma((n - 1,)),
            dma((n - 1,)),
            dma((n - 1, masks)),
            dma((n - 1, masks)),
            dma((n - 1,)),
            dma((n - 1,)),
            dma((n,)),
            dma((n,)),
        ],
        compiler_params=pltpu.CompilerParams(
            vmem_limit_bytes=VMEM_LIMIT, collective_id=2, has_side_effects=True
        ),
        cost_estimate=pl.CostEstimate(
            flops=2 * tokens * width * (q_cols + 2 * kv_cols), bytes_accessed=1 << 25, transcendentals=0
        ),
        name="attn",
    )(hidden, cot, gain_a, gain_f, wq, wk, wv, wo, cosine, sine, bias)


def arrival_order(t, n):
    near = jnp.minimum(t, n - 1 - t)
    order = [t]
    for i in range(1, n):
        both = t - (i + 1) // 2 if i % 2 else t + i // 2
        one_side = jnp.where(t > n - 1 - t, t - (i - near), t + (i - near))
        order.append(jnp.where(i <= 2 * near, both, one_side))
    return order


def attend_back_block(g, b, q_ref, k_ref, v_ref, o_ref, lse_ref, do_ref, turn_back, bias_ref, d_ref, dk_acc, dv_acc):
    heads, kv_heads = q_ref.shape[1] // HD, k_ref.shape[1] // HD
    rep = heads // kv_heads
    last = q_ref.shape[0] // BLK - 1
    causal = causal_tile(rep)
    rows = slice(b * BLK, (b + 1) * BLK)
    q = stack_heads(q_ref, rows, g * rep, rep)
    do = stack_heads(do_ref, rows, g * rep, rep)
    o = stack_heads(o_ref, rows, g * rep, rep)
    lse = [lse_ref[rows, h : h + 1] for h in range(g * rep, (g + 1) * rep)]
    lse = jnp.concatenate(lse, axis=0) if rep > 1 else lse[0]
    delta = jnp.sum(do.astype(F32) * o.astype(F32), axis=1, keepdims=True)
    k_d = k_ref[rows, head_cols(g)]
    p = jnp.where(causal, jnp.exp2(mm_bt(q, k_d) * SCALE2 - lse), 0.0)
    ds = (p * (mm_bt(do, v_ref[rows, head_cols(g)]) - delta)).astype(BF)
    dq = mm(ds, k_d)
    dk = mm_at(ds, q)
    dv = mm_at(p.astype(BF), do)
    if b < last:
        dk = dk + dk_acc[rows, head_cols(g)]
        dv = dv + dv_acc[rows, head_cols(g)]
    d_ref[rows, head_cols(heads + g)] = turn_back(dk * SCALE, rows)
    d_ref[rows, head_cols(heads + kv_heads + g)] = dv.astype(BF)
    if b:
        past = slice(0, b * BLK)
        k_p = k_ref[past, head_cols(g)]
        p = jnp.exp2(mm_bt(q, k_p) * SCALE2 + (bias_ref[b : b + 1, past] - lse))
        ds = (p * (mm_bt(do, v_ref[past, head_cols(g)]) - delta)).astype(BF)
        dq = dq + mm(ds, k_p)
        dk = mm_at(ds, q)
        dv = mm_at(p.astype(BF), do)
        if b < last:
            dk = dk + dk_acc[past, head_cols(g)]
            dv = dv + dv_acc[past, head_cols(g)]
        dk_acc[past, head_cols(g)] = dk
        dv_acc[past, head_cols(g)] = dv
    dq = dq * SCALE
    for i in range(rep):
        d_ref[rows, head_cols(g * rep + i)] = turn_back(dq[i * BLK : (i + 1) * BLK], rows)


def attn_bwd_kernel(q_ref, k_ref, v_ref, o_ref, lse_ref, do_ref, cos_ref, sin_ref, bias_ref, d_ref, dk_acc, dv_acc):
    def turn_back(grad, rows):
        return (grad * cos_ref[rows, :] - pltpu.roll(grad, HD // 2, 1) * sin_ref[rows, :]).astype(BF)

    for b in range(q_ref.shape[0] // BLK - 1, -1, -1):
        for g in range(k_ref.shape[1] // HD):
            attend_back_block(
                g, b, q_ref, k_ref, v_ref, o_ref, lse_ref, do_ref, turn_back, bias_ref, d_ref, dk_acc, dv_acc
            )


BACK_INS = ("fi", "mid", "cot", "hid", "q", "k", "v", "m", "lse", "cos", "sin", "mixed", "wq", "wk", "wv")
BACK_NAMES = (
    BACK_INS,
    ("gain_a", "gain_f", "bias", "x_h", "wo_h", "tot_h", "two_h"),
    ("input_grad", "project_grad", "out_grad", "gain_grad", "three_h"),
    tuple(name + "_b" for name in BACK_INS),
    ("wo", "bg", "mg", "do", "dqkv", "dk_acc", "dv_acc", "got", "one_o", "one_p", "two_o", "two_p"),
    ("three_o", "three_p", "s3", "give", "zr", "gain_st", "gain_dp", "gain_line"),
    ("in_sem", "wo_sem", "x_sem", "s3_sem", "mg_send", "mg_recv", "th_send", "th_recv", "one_send", "one_recv"),
    ("stw_send", "stw_recv", "sth_send", "sth_recv", "z_send", "z_recv", "rs_send", "rs_recv"),
    ("gd_send", "gd_recv", "gl_send", "gl_recv"),
)


def back_kernel(n, *refs):
    names = [name for group in BACK_NAMES for name in group]
    r = types.SimpleNamespace(**dict(zip(names, refs, strict=True)))
    t, d = lax.axis_index("tensor"), lax.axis_index("dp")
    rows, width = r.bg.shape
    q_cols, kv_cols = r.q_b.shape[1], r.k_b.shape[1]
    all_cols = q_cols + 2 * kv_cols
    tokens = n * rows
    core, x, y = lax.rem(d, 2), lax.rem(d // 2, 2), d // 4
    chunk = width // 8
    parts = r.rs_send.shape[2]
    part_rows = rows // parts
    order = arrival_order(t, n)
    is_mid = (t > 0) & (t < n - 1)
    pairs_o = [(2 * y + x, 2 * y + 1 - x, 2), (2 * (1 - y) + x, 2 * (1 - y) + 1 - x, 2)]
    pairs_o += [(2 * y + x, 2 * (1 - y) + x, 4), (2 * y + 1 - x, 2 * (1 - y) + 1 - x, 4)]

    loads = {
        name: pltpu.make_async_copy(getattr(r, name), getattr(r, name + "_b"), r.in_sem.at[i])
        for i, name in enumerate(BACK_INS)
    }
    load_wo = [pltpu.make_async_copy(r.wo_h.at[s], r.wo.at[s], r.wo_sem.at[s]) for s in range(n)]
    load_x = [pltpu.make_async_copy(r.x_h.at[s], r.wo.at[s, pl.ds(0, rows)], r.x_sem.at[s]) for s in range(n)]
    half = r.s3.shape[3]
    load_s3 = []
    for w in range(3):
        for k in range(2):
            load_s3.append(pltpu.make_async_copy(r.tot_h.at[w, 2 * k + 1], r.s3.at[w, k], r.s3_sem.at[0, w, k]))
            landing = r.wo.at[w, pl.ds(rows, rows), pl.ds(k * half, half)]
            load_s3.append(pltpu.make_async_copy(r.two_h.at[w, 2 * k + 1], landing, r.s3_sem.at[1, w, k]))
    for name in ("fi", "mid", "cot"):
        loads[name].start()
    for copy in load_wo:
        copy.start()
    for name in BACK_INS[3:]:
        loads[name].start()
    for copy in load_s3[::2]:
        copy.start()
    group_barrier(range(1, 8), n, d, t)

    for name in ("fi", "mid", "cot"):
        loads[name].wait()

    def norm_back_part(grad, values, gain_ref):
        inverse = lax.rsqrt(jnp.mean(values * values, axis=-1, keepdims=True) + NORM_EPS)
        scaled = values * inverse
        weighted = grad * gain_ref[...].astype(F32)
        back = inverse * (weighted - scaled * jnp.mean(weighted * scaled, axis=-1, keepdims=True))
        return back, grad * scaled

    def gain_along_dp(mask):
        return copy_to(
            r.gain_st.at[d ^ mask, pl.ds(0, 8)],
            r.gain_dp.at[mask - 1],
            r.gd_send.at[mask - 1],
            r.gd_recv.at[mask - 1],
            dp=d ^ mask,
        )

    gain_sum = jnp.zeros((8, width), F32)
    for first in range(0, rows, 64):
        part = slice(first, first + 64)
        back, gain_part = norm_back_part(r.fi_b[part, :], r.mid_b[part, :], r.gain_f)
        gain_sum = gain_sum + jnp.sum(gain_part.reshape(8, 8, width), axis=0)
        total = r.cot_b[part, :].astype(F32) + back
        r.fi_b[part, :] = total
        r.bg[part, :] = total.astype(BF)
    for c in range(8):
        r.gain_st[c, 0:8, :] = gain_sum[:, c * chunk : (c + 1) * chunk]
    for mask in range(1, 8):
        gain_along_dp(mask).start()

    def rows_of(s):
        return pl.ds(pl.multiple_of(s * rows, rows), rows)

    def heads_back(k):
        s = lax.rem(t + k, n)
        return copy_to(r.mg.at[s], r.do.at[rows_of(t)], r.mg_send.at[k - 1], r.mg_recv.at[k - 1], tensor=s)

    for copy in load_wo:
        copy.wait()
    for k in range(1, n):
        s = lax.rem(t + k, n)
        r.mg[s] = mm_bt(r.bg[...], r.wo[s]).astype(BF)
        heads_back(k).start()
    r.do[rows_of(t), :] = mm_bt(r.bg[...], r.wo[t]).astype(BF)

    for copy in load_s3[1::2] + load_x:
        copy.start()

    def ffn_three(w, k):
        return copy_to(r.s3.at[w, k], r.three_h.at[w, k], r.th_send.at[w, k], r.th_recv.at[w, k], dp=d ^ (4, 2)[k])

    for w in range(3):
        for k in range(2):
            for copy in load_s3[4 * w + 2 * k : 4 * w + 2 * k + 2]:
                copy.wait()
            other = r.wo[w, rows : 2 * rows, k * half : (k + 1) * half]
            r.s3[w, k] = (r.s3[w, k].astype(F32) + other.astype(F32)).astype(BF)
            ffn_three(w, k).start()

    ones, twos, threes = (r.one_o, r.one_p), (r.two_o, r.two_p), (r.three_o, r.three_p)

    def stage_one(i, j):
        cols = pl.ds(0, ones[i].shape[2])
        src = r.give.at[lax.rem(j, 2), :, cols]
        return copy_to(src, ones[i].at[j], r.one_send.at[i, j], r.one_recv.at[i, j], dp=d ^ 1)

    def halves(i, k):
        size = ones[i].shape[2] // 2
        return pl.ds((k // 2) * size, size)

    def stage_two(i, k):
        src = ones[i].at[pairs_o[k][1]].at[:, halves(i, k)]
        return copy_to(src, twos[i].at[k], r.stw_send.at[i, k], r.stw_recv.at[i, k], dp=d ^ pairs_o[k][2])

    def stage_three(i, k):
        j = (2 * (1 - y) + x, 2 * y + 1 - x)[k]
        src = ones[i].at[j].at[:, halves(i, 2 * k)]
        return copy_to(src, threes[i].at[k], r.sth_send.at[i, k], r.sth_recv.at[i, k], dp=d ^ (4, 2)[k])

    def start_three(i):
        for k in range(2):
            stage_two(i, 2 * k + 1).wait_recv()
            j = (2 * (1 - y) + x, 2 * y + 1 - x)[k]
            piece = ones[i].at[j].at[:, halves(i, 2 * k)]
            piece[...] = (piece[...].astype(F32) + twos[i][2 * k + 1].astype(F32)).astype(BF)
            stage_three(i, k).start()

    def final_half(i, k):
        stage_two(i, 2 * k).wait_recv()
        stage_three(i, k).wait_recv()
        total = ones[i].at[2 * y + x].at[:, halves(i, 2 * k)][...].astype(F32)
        return total + twos[i][2 * k].astype(F32) + threes[i][k].astype(F32)

    def dp_start(i, terms):
        def give(j, carry):
            @pl.when(j >= 2)
            def _():
                stage_one(i, j - 2).wait_send()

            for cols, value in terms(2 * j + 1 - core):
                r.give[lax.rem(j, 2), :, cols] = value.astype(BF)
            stage_one(i, j).start()
            return carry

        def keep(j, carry):
            stage_one(i, j).wait_recv()
            for cols, value in terms(2 * j + core):
                piece = ones[i].at[j].at[:, cols]
                piece[...] = (piece[...].astype(F32) + value).astype(BF)
            return carry

        lax.fori_loop(0, 4, give, 0)
        lax.fori_loop(0, 4, keep, 0)
        for j in (2, 3):
            stage_one(i, j).wait_send()
        for k in (1, 3, 0, 2):
            stage_two(i, k).start()

    loads["mixed"].wait()

    def out_terms(c):
        grads = r.bg[:, pl.ds(pl.multiple_of(c * chunk, chunk), chunk)]
        for s in range(n):
            yield slice(s * q_cols, (s + 1) * q_cols), mm_at(grads, r.mixed_b[s])

    dp_start(0, out_terms)

    for name in BACK_INS[3:]:
        if name != "mixed":
            loads[name].wait()
    for k in range(1, n):
        heads_back(k).wait_recv()

    def turn_back(grad, part):
        return (grad * r.cos_b[part, :] - pltpu.roll(grad, HD // 2, 1) * r.sin_b[part, :]).astype(BF)

    for b in range(tokens // BLK - 1, -1, -1):
        for g in range(kv_cols // HD):
            attend_back_block(
                g,
                b,
                r.q_b,
                r.k_b,
                r.v_b,
                r.m_b,
                r.lse_b,
                r.do,
                turn_back,
                r.bias,
                r.dqkv,
                r.dk_acc,
                r.dv_acc,
            )

    def scatter(s, c, to_right):
        k, slot = (0, s - 1) if to_right else (1, n - 2 - s)
        piece = pl.ds(c * part_rows, part_rows)
        return copy_to(
            r.wo.at[s, pl.ds(rows + c * part_rows, part_rows)],
            r.got.at[k, slot, piece],
            r.rs_send.at[k, slot, c],
            r.rs_recv.at[k, slot, c],
            tensor=t + 1 if to_right else t - 1,
        )

    for i in range(n - 1, -1, -1):
        s = order[i]
        here = rows_of(s)
        for first in range(0, width, 512):
            cols = slice(first, first + 512)
            term = mm_bt(r.dqkv[here, :q_cols], r.wq_b[cols, :])
            term = term + mm_bt(r.dqkv[here, q_cols : q_cols + kv_cols], r.wk_b[cols, :])
            term = term + mm_bt(r.dqkv[here, q_cols + kv_cols :], r.wv_b[cols, :])
            if i:
                r.wo[s, rows : 2 * rows, cols] = term.astype(BF)
            else:
                r.mid_b[:, cols] = term
        if i == n - 1:
            for c in range(parts):
                pl.when(t == 0)(lambda: scatter(n - 1, c, True).start())
                pl.when(t == n - 1)(lambda: scatter(0, c, False).start())

    def next_sends(i):
        for c in range(parts):

            @pl.when(t == 0)
            def _():
                scatter(i + 1, c, True).wait_send()
                scatter(i, c, True).start()

            @pl.when(t == n - 1)
            def _():
                scatter(n - 2 - i, c, False).wait_send()
                scatter(n - 1 - i, c, False).start()

    from_left = t * 2 < n - 1

    def pass_on(index, near):
        for c in range(parts):
            piece = pl.ds(c * part_rows, part_rows)
            for to_right in (True, False):
                s = index if to_right else n - 1 - index
                way = 0 if to_right else 1
                has_source = t > 0 if to_right else t < n - 1
                now = from_left == (to_right == near)

                @pl.when(has_source & now & (s > t if to_right else s < t))
                def _():
                    scatter(s, c, to_right).wait_recv()
                    term = r.wo.at[s, pl.ds(rows + c * part_rows, part_rows)]
                    term[...] = (term[...].astype(F32) + r.got[way, index - 1, piece].astype(F32)).astype(BF)
                    scatter(s, c, to_right).start()

    def take_own():
        for to_right in (True, False):
            way = 0 if to_right else 1
            has_source = t > 0 if to_right else t < n - 1
            for index in range(1, n):
                s = index if to_right else n - 1 - index

                @pl.when(has_source & (s == t))
                def _():
                    for c in range(parts):
                        scatter(s, c, to_right).wait_recv()
                    r.mid_b[...] += r.got[way, index - 1].astype(F32)

    for copy in load_x:
        copy.wait()

    def project_terms(c):
        cols = pl.ds(pl.multiple_of(c * chunk, chunk), chunk)
        normed = r.wo[:, 0:rows, cols].reshape(tokens, chunk)
        for first in range(0, all_cols, 512):
            part = slice(first, first + 512)
            yield part, mm_at(normed, r.dqkv[:, part])

    dp_start(1, project_terms)
    start_three(0)
    next_sends(2)
    pass_on(3, True)
    start_three(1)
    next_sends(1)
    pass_on(3, False)
    pass_on(2, True)
    for k in range(1, n):
        heads_back(k).wait_send()

    def out_piece(k):
        s = lax.rem(t + k, n)
        return copy_to(r.mg.at[s], r.zr.at[k - 1], r.z_send.at[k - 1], r.z_recv.at[k - 1], tensor=s)

    per_half = n // 2
    for k in range(2):
        total = final_half(0, k)
        for i in range(per_half):
            s = k * per_half + i
            value = total[:, i * q_cols : (i + 1) * q_cols]
            r.mg[s] = value.astype(BF)

            @pl.when(s == t)
            def _():
                r.out_grad[...] = value

    for k in range(1, n):
        out_piece(k).start()
    mine = pl.ds(pl.multiple_of(d * chunk, chunk), chunk)
    size = all_cols // 2
    gain_terms = jnp.zeros((8, chunk), F32)
    for k in range(2):
        value = final_half(1, k)
        r.project_grad[:, k * size : (k + 1) * size] = value
        weight = r.wq_b[mine, :] if k == 0 else jnp.concatenate([r.wk_b[mine, :], r.wv_b[mine, :]], axis=1)
        gain_terms = gain_terms + lax.dot_general(
            jnp.ones((8, size), F32),
            value * weight.astype(F32),
            (((1,), (1,)), ((), ())),
            precision=lax.Precision.HIGHEST,
            preferred_element_type=F32,
        )
    r.gain_st[8, 0:8, :] = gain_terms
    total = r.gain_st[d, 0:8]
    for mask in range(1, 8):
        gain_along_dp(mask).wait_recv()
        total = total + r.gain_dp[mask - 1]
    r.gain_st[8, 8:16, :] = total

    def gain_along_line(k):
        s = lax.rem(t + k, n)
        return copy_to(r.gain_st.at[8], r.gain_line.at[k - 1], r.gl_send.at[k - 1], r.gl_recv.at[k - 1], tensor=s)

    for k in range(1, n):
        gain_along_line(k).start()
    take_own()
    for first in range(0, rows, 64):
        part = slice(first, first + 64)
        back, unused = norm_back_part(r.mid_b[part, :], r.hid_b[part, :].astype(F32), r.gain_a)
        r.input_grad[part, :] = (r.fi_b[part, :] + back).astype(BF)
    for k in range(1, n):
        out_piece(k).wait_recv()
        r.out_grad[...] += r.zr[k - 1].astype(F32)
    total = r.gain_st[8]
    for k in range(1, n):
        gain_along_line(k).wait_recv()
        total = total + r.gain_line[k - 1]
    r.gain_grad[0:1, :] = total[0:1] / r.gain_a[:, mine].astype(F32)
    r.gain_grad[1:2, :] = jnp.sum(total[8:16], axis=0, keepdims=True)
    for k in range(1, n):
        gain_along_line(k).wait_send()
    for mask in range(1, 8):
        gain_along_dp(mask).wait_send()

    for k in range(1, n):
        out_piece(k).wait_send()
    for w in range(3):
        for k in range(2):
            ffn_three(w, k).wait()
    for i in range(2):
        for k in range(4):
            stage_two(i, k).wait_send()
        for k in range(2):
            stage_three(i, k).wait_send()
    for s in range(n):
        for to_right in (True, False):
            goes_on = t < n - 1 if to_right else t > 0

            @pl.when(goes_on & (s > t if to_right else s < t) & (is_mid | (s == (t + 1 if to_right else t - 1))))
            def _():
                for c in range(parts):
                    scatter(s, c, to_right).wait_send()


def back_call(n, arrays, gain_a, gain_f, bias, x_all, w_out_all, totals, twos):
    rows, width = arrays["hid"].shape
    q_cols, kv_cols = arrays["q"].shape[1], arrays["k"].shape[1]
    all_cols = q_cols + 2 * kv_cols
    tokens = n * rows
    chunk = width // 8
    parts = rows // 64
    any_spec = pl.BlockSpec(memory_space=pl.ANY)
    vmem_spec = pl.BlockSpec(memory_space=pltpu.VMEM)
    dma = pltpu.SemaphoreType.DMA
    shape = jax.ShapeDtypeStruct
    return pl.pallas_call(
        functools.partial(back_kernel, n),
        out_shape=[
            shape((rows, width), BF),
            shape((chunk, all_cols), F32),
            shape((chunk, q_cols), F32),
            shape((8, chunk), F32),
            shape((3, 2, chunk, width // 2), BF),
        ],
        in_specs=[any_spec] * len(BACK_INS) + [vmem_spec] * 3 + [any_spec] * 4,
        out_specs=[vmem_spec] * 4 + [any_spec],
        scratch_shapes=[pltpu.VMEM(arrays[name].shape, arrays[name].dtype) for name in BACK_INS]
        + [
            pltpu.VMEM((n, q_cols, width), BF),
            pltpu.VMEM((rows, width), BF),
            pltpu.VMEM((n, rows, q_cols), BF),
            pltpu.VMEM((tokens, q_cols), BF),
            pltpu.VMEM((tokens, all_cols), BF),
            pltpu.VMEM((tokens, kv_cols), F32),
            pltpu.VMEM((tokens, kv_cols), F32),
            pltpu.VMEM((2, n - 1, rows, width), BF),
            pltpu.VMEM((4, chunk, n * q_cols), BF),
            pltpu.VMEM((4, chunk, all_cols), BF),
            pltpu.VMEM((4, chunk, n * q_cols // 2), BF),
            pltpu.VMEM((4, chunk, all_cols // 2), BF),
            pltpu.VMEM((2, chunk, n * q_cols // 2), BF),
            pltpu.VMEM((2, chunk, all_cols // 2), BF),
            pltpu.VMEM((3, 2, chunk, width // 2), BF),
            pltpu.VMEM((2, chunk, n * q_cols), BF),
            pltpu.VMEM((n - 1, chunk, q_cols), BF),
            pltpu.VMEM((9, 16, chunk), F32),
            pltpu.VMEM((7, 8, chunk), F32),
            pltpu.VMEM((n - 1, 16, chunk), F32),
            dma((len(BACK_INS),)),
            dma((n,)),
            dma((n,)),
            dma((2, 3, 2)),
            dma((n - 1,)),
            dma((n - 1,)),
            dma((3, 2)),
            dma((3, 2)),
            dma((2, 4)),
            dma((2, 4)),
            dma((2, 4)),
            dma((2, 4)),
            dma((2, 2)),
            dma((2, 2)),
            dma((n - 1,)),
            dma((n - 1,)),
            dma((2, n - 1, parts)),
            dma((2, n - 1, parts)),
            dma((7,)),
            dma((7,)),
            dma((n - 1,)),
            dma((n - 1,)),
        ],
        compiler_params=pltpu.CompilerParams(
            vmem_limit_bytes=63 * 1024 * 1024, collective_id=3, has_side_effects=True
        ),
        cost_estimate=pl.CostEstimate(flops=1 << 36, bytes_accessed=1 << 26, transcendentals=0),
        name="back",
    )(*[arrays[name] for name in BACK_INS], gain_a, gain_f, bias, x_all, w_out_all, totals, twos)


def ffn_kernel(
    n,
    own_ref,
    cot_ref,
    wg_hbm,
    wu_hbm,
    wd_hbm,
    h_out,
    gg_out,
    ug_out,
    n_out,
    fb_out,
    fi_out,
    wg_ref,
    wu_ref,
    wd_ref,
    n_buf,
    c_buf,
    st_buf,
    fi_part,
    got,
    fb_acc,
    fi_acc,
    w_sem,
    c_sem,
    st_sem,
    n_sem,
    ag_send,
    ag_recv,
    rs_send,
    rs_recv,
):
    t, d = lax.axis_index("tensor"), lax.axis_index("dp")
    rows, width = own_ref.shape
    units = wg_ref.shape[1]
    tile = min(512, units)
    tiles = units // tile
    parts = rs_send.shape[2]
    part_rows = rows // parts
    order = arrival_order(t, n)
    is_mid = (t > 0) & (t < n - 1)

    def load_weights(j):
        cols = pl.ds(j * tile, tile)
        return [
            pltpu.make_async_copy(wg_hbm.at[:, cols], wg_ref.at[:, cols], w_sem.at[0, j]),
            pltpu.make_async_copy(wu_hbm.at[:, cols], wu_ref.at[:, cols], w_sem.at[1, j]),
            pltpu.make_async_copy(wd_hbm.at[cols, :], wd_ref.at[cols, :], w_sem.at[2, j]),
        ]

    def load_cot(i):
        return pltpu.make_async_copy(cot_ref.at[order[i]], c_buf.at[i % 2], c_sem.at[i % 2])

    def gather(s, to_right, src=None):
        return copy_to(
            n_buf.at[s] if src is None else src,
            n_buf.at[s],
            ag_send.at[0 if to_right else 1, s],
            ag_recv.at[s],
            tensor=t + 1 if to_right else t - 1,
        )

    def keep_rows(i):
        return pltpu.make_async_copy(own_ref if i == 0 else n_buf.at[order[i]], n_out.at[order[i]], n_sem.at[i])

    def scatter(s, c, to_right):
        k, slot = (0, s - 1) if to_right else (1, n - 2 - s)
        piece = pl.ds(c * part_rows, part_rows)
        return copy_to(
            fi_part.at[s, piece],
            got.at[k, slot, piece],
            rs_send.at[k, slot, c],
            rs_recv.at[k, slot, c],
            tensor=t + 1 if to_right else t - 1,
        )

    for copy in load_weights(0):
        copy.start()
    load_cot(0).start()
    group_barrier([], n, d, t)
    pl.when(t < n - 1)(lambda: gather(t, True, own_ref).start())
    pl.when(t > 0)(lambda: gather(t, False, own_ref).start())
    for j in range(1, tiles):
        for copy in load_weights(j):
            copy.start()
    keep_rows(0).start()

    def arrive(i):
        s = order[i]
        gather(s, True).wait_recv()
        pl.when((s < t) & (t < n - 1))(lambda: gather(s, True).start())
        pl.when((s > t) & (t > 0))(lambda: gather(s, False).start())
        keep_rows(i).start()

    def stage_out(i):
        return [
            pltpu.make_async_copy(
                st_buf.at[i % 2, k, :, pl.ds(0, out.shape[2])], out.at[order[i]], st_sem.at[k, i % 2]
            )
            for k, out in enumerate((h_out, gg_out, ug_out, fb_out))
        ]

    for i in range(n):
        s = order[i]
        slot = i % 2
        if i == 1:
            arrive(1)
            if n > 2:
                pl.when(is_mid)(functools.partial(arrive, 2))
        elif i > 1:
            pl.when(jnp.logical_not(is_mid))(functools.partial(arrive, i))
        if i + 1 < n:
            load_cot(i + 1).start()
        load_cot(i).wait()
        if i >= 2:
            for copy in stage_out(i - 2):
                copy.wait()
        x_ref = own_ref if i == 0 else n_buf.at[s]
        fb_acc[...] = jnp.zeros_like(fb_acc)
        fi_acc[...] = jnp.zeros_like(fi_acc)

        def one_tile(j, carry):
            if i == 0:
                for copy in load_weights(j):
                    copy.wait()
            if 2 <= i < n - 1:
                pl.when(is_mid & (j == tiles // 2))(functools.partial(arrive, i + 1))
            cols = pl.ds(pl.multiple_of(j * tile, tile), tile)
            x = x_ref[...]
            wg, wu, wd = wg_ref[:, cols], wu_ref[:, cols], wd_ref[cols, :]
            gate = mm(x, wg)
            up = mm(x, wu)
            act_grad = mm_bt(c_buf[slot], wd)
            sig = jax.nn.sigmoid(gate)
            silu = gate * sig
            h = (silu * up).astype(BF)
            gg = (act_grad * up * (sig * (1.0 + gate * (1.0 - sig)))).astype(BF)
            ug = (act_grad * silu).astype(BF)
            for k, value in enumerate((h, gg, ug)):
                st_buf[slot, k, :, cols] = value
            for k in range(0, width, 512):
                piece = slice(k, k + 512)
                fb_acc[:, piece] += mm(h, wd_ref[cols, piece])
                fi_acc[:, piece] += mm_bt(gg, wg_ref[piece, cols]) + mm_bt(ug, wu_ref[piece, cols])
            return carry

        lax.fori_loop(0, tiles, one_tile, 0)
        st_buf[slot, 3, :, :width] = fb_acc[...].astype(BF)
        for copy in stage_out(i):
            copy.start()
        if i == 0:
            fi_out[...] = fi_acc[...]
        else:
            fi_part[s] = fi_acc[...].astype(BF)

            @pl.when(t == 0)
            def _():
                for c in range(parts):
                    scatter(i, c, True).start()

            @pl.when(t == n - 1)
            def _():
                for c in range(parts):
                    scatter(n - 1 - i, c, False).start()

    def pass_on(index, c):
        piece = pl.ds(c * part_rows, part_rows)
        for to_right in (True, False):
            s = index if to_right else n - 1 - index
            k = 0 if to_right else 1
            has_source = t > 0 if to_right else t < n - 1
            beyond = s > t if to_right else s < t

            @pl.when(has_source & beyond)
            def _():
                scatter(s, c, to_right).wait_recv()
                total = fi_part[s, piece].astype(F32) + got[k, index - 1, piece].astype(F32)
                fi_part[s, piece] = total.astype(BF)
                scatter(s, c, to_right).start()

            @pl.when(has_source & (s == t))
            def _():
                scatter(s, c, to_right).wait_recv()
                fi_out[piece] += got[k, index - 1, piece].astype(F32)

    for i in range(max(0, n - 2), n):
        for copy in stage_out(i):
            copy.wait()
    for index in range(1, n):
        for c in range(parts):
            pass_on(index, c)
    for i in range(n):
        keep_rows(i).wait()
    for s in range(n):
        for to_right in (True, False):
            goes_on = t < n - 1 if to_right else t > 0

            @pl.when(goes_on & (s <= t if to_right else s >= t))
            def _():
                gather(s, to_right).wait_send()

            @pl.when(goes_on & (s > t if to_right else s < t))
            def _():
                for c in range(parts):
                    scatter(s, c, to_right).wait_send()


def ffn_call(n, own_rows, cot_all, w_gate, w_up, w_down):
    rows, width = own_rows.shape
    units = w_gate.shape[1]
    tile = min(512, units)
    tiles = units // tile
    parts = max(1, rows // 64)
    tall = jax.ShapeDtypeStruct((n, rows, units), BF)
    wide = jax.ShapeDtypeStruct((n, rows, width), BF)
    any_spec = pl.BlockSpec(memory_space=pl.ANY)
    vmem_spec = pl.BlockSpec(memory_space=pltpu.VMEM)
    dma = pltpu.SemaphoreType.DMA
    return pl.pallas_call(
        functools.partial(ffn_kernel, n),
        out_shape=[tall, tall, tall, wide, wide, jax.ShapeDtypeStruct((rows, width), F32)],
        in_specs=[vmem_spec] + [any_spec] * 4,
        out_specs=[any_spec] * 5 + [vmem_spec],
        scratch_shapes=[
            pltpu.VMEM((width, units), BF),
            pltpu.VMEM((width, units), BF),
            pltpu.VMEM((units, width), BF),
            pltpu.VMEM((n, rows, width), BF),
            pltpu.VMEM((2, rows, width), BF),
            pltpu.VMEM((2, 4, rows, max(units, width)), BF),
            pltpu.VMEM((n, rows, width), BF),
            pltpu.VMEM((2, n - 1, rows, width), BF),
            pltpu.VMEM((rows, width), F32),
            pltpu.VMEM((rows, width), F32),
            dma((3, tiles)),
            dma((2,)),
            dma((4, 2)),
            dma((n,)),
            dma((2, n)),
            dma((n,)),
            dma((2, n - 1, parts)),
            dma((2, n - 1, parts)),
        ],
        compiler_params=pltpu.CompilerParams(
            vmem_limit_bytes=63 * 1024 * 1024, collective_id=4, has_side_effects=True
        ),
        cost_estimate=pl.CostEstimate(
            flops=12 * n * rows * width * units, bytes_accessed=6 * width * units, transcendentals=0
        ),
        name="ffn_plain",
    )(own_rows, cot_all, w_gate, w_up, w_down)


MID_NAMES = (
    ("own", "cot_in", "wg_h", "wu_h", "wd_h"),
    ("cot", "h_out", "tot", "two", "fi_out", "fb_out"),
    ("wg", "wu", "wd", "n_buf", "gu", "h_st", "c_buf", "part", "land", "acc"),
    ("w_sem", "own_sem", "c_sem", "h_sem", "re_sem", "tot_sem", "out_sem", "ready"),
    ("ag_send", "ag_recv", "ct_send", "ct_recv", "rs_send", "rs_recv"),
    ("one_send", "one_recv", "two_send", "two_recv"),
)


def middle_kernel(n, *refs):
    names = [name for group in MID_NAMES for name in group]
    r = types.SimpleNamespace(**dict(zip(names, refs, strict=True)))
    t, d = lax.axis_index("tensor"), lax.axis_index("dp")
    rows, width = r.own.shape
    units = r.wg.shape[1]
    tokens = n * rows
    tile = 512
    tiles = units // tile
    parts = r.rs_send.shape[3]
    part_rows = rows // parts
    order = arrival_order(t, n)
    is_mid = (t > 0) & (t < n - 1)
    is_end = jnp.logical_not(is_mid)
    core, x, y = lax.rem(d, 2), lax.rem(d // 2, 2), d // 4
    chunk = width // 8
    halves = units // 2

    def load_weights(j):
        cols = pl.ds(j * tile, tile)
        return [
            pltpu.make_async_copy(r.wg_h.at[:, cols], r.wg.at[:, cols], r.w_sem.at[0, j]),
            pltpu.make_async_copy(r.wu_h.at[:, cols], r.wu.at[:, cols], r.w_sem.at[1, j]),
            pltpu.make_async_copy(r.wd_h.at[cols, :], r.wd.at[cols, :], r.w_sem.at[2, j]),
        ]

    def line(buf, send_sem, recv_sem, s, to_right, src=None):
        return copy_to(
            buf.at[s] if src is None else src,
            buf.at[s],
            send_sem.at[0 if to_right else 1, s],
            recv_sem.at[s],
            tensor=t + 1 if to_right else t - 1,
        )

    gather = functools.partial(line, r.n_buf, r.ag_send, r.ag_recv)
    gather_cot = functools.partial(line, r.cot, r.ct_send, r.ct_recv)
    own_rows = pltpu.make_async_copy(r.own, r.n_buf.at[t], r.own_sem.at[0])

    def load_cot(i):
        return pltpu.make_async_copy(r.cot.at[order[i]], r.c_buf.at[i % 2], r.c_sem.at[i % 2])

    def keep_h(i):
        return pltpu.make_async_copy(r.h_st, r.h_out.at[order[i]], r.h_sem.at[0])

    def scatter(q, s, c, to_right):
        k, index = (0, s - 1) if to_right else (1, n - 2 - s)
        piece = pl.ds(c * part_rows, part_rows)
        to = t + 1 if to_right else t - 1
        slot = s if to_right else jnp.where(to == s, n, s)
        return copy_to(
            r.part.at[q, s, piece],
            r.land.at[q, slot, piece],
            r.rs_send.at[q, k, index, c],
            r.rs_recv.at[q, k, index, c],
            tensor=to,
        )

    own_rows.start()
    for copy in load_weights(0):
        copy.start()
    load_cot(0).start()
    group_barrier([1, 2, 4], n, d, t)
    own_rows.wait()
    pl.when(t < n - 1)(lambda: gather(t, True).start())
    pl.when(t > 0)(lambda: gather(t, False).start())
    for j in range(1, tiles):
        for copy in load_weights(j):
            copy.start()

    def arrive(which, i):
        s = order[i]
        which(s, True).wait_recv()
        pl.when((s < t) & (t < n - 1))(lambda: which(s, True).start())
        pl.when((s > t) & (t > 0))(lambda: which(s, False).start())

    def end_sends(q, i, chunks):
        @pl.when(t == 0)
        def _():
            for c in chunks:
                scatter(q, i, c, True).start()

        @pl.when(t == n - 1)
        def _():
            for c in chunks:
                scatter(q, n - 1 - i, c, False).start()

    def forward(i):
        s = order[i]
        if i:
            keep_h(i - 1).wait()
        r.acc[...] = jnp.zeros_like(r.acc)

        def one_tile(j, carry):
            if i == 0:
                for copy in load_weights(j):
                    copy.wait()
            if 2 <= i < n - 1:
                pl.when(is_mid & (j == tiles // 2))(functools.partial(arrive, gather, i + 1))
            cols = pl.ds(pl.multiple_of(j * tile, tile), tile)
            rows_in = r.n_buf[s]
            gate = mm(rows_in, r.wg[:, cols])
            up = mm(rows_in, r.wu[:, cols])
            sig = jax.nn.sigmoid(gate)
            silu = gate * sig
            h = (silu * up).astype(BF)
            r.h_st[:, cols] = h
            r.gu[0, s, :, cols] = (up * (sig * (1.0 + gate * (1.0 - sig)))).astype(BF)
            r.gu[1, s, :, cols] = silu.astype(BF)
            for k in range(0, width, 512):
                piece = slice(k, k + 512)
                r.acc[:, piece] += mm(h, r.wd[cols, piece])
            return carry

        lax.fori_loop(0, tiles, one_tile, 0)
        keep_h(i).start()
        r.part[0, s] = r.acc[...].astype(BF)
        if i:
            end_sends(0, i, range(parts))

    def backward(i, chunks):
        s = order[i]
        r.acc[...] = jnp.zeros_like(r.acc)
        load_cot(i).wait()

        def one_tile(j, carry):
            cols = pl.ds(pl.multiple_of(j * tile, tile), tile)
            act_grad = mm_bt(r.c_buf[i % 2], r.wd[cols, :])
            gg = (act_grad * r.gu[0, s, :, cols].astype(F32)).astype(BF)
            ug = (act_grad * r.gu[1, s, :, cols].astype(F32)).astype(BF)
            r.gu[0, s, :, cols] = gg
            r.gu[1, s, :, cols] = ug
            for k in range(0, width, 512):
                piece = slice(k, k + 512)
                r.acc[:, piece] += mm_bt(gg, r.wg[piece, cols]) + mm_bt(ug, r.wu[piece, cols])
            return carry

        lax.fori_loop(0, tiles, one_tile, 0)
        r.part[1, s] = r.acc[...].astype(BF)
        if i:
            end_sends(1, i, chunks)

    from_left = t * 2 < n - 1

    def pass_on(q, index, near):
        for c in range(parts):
            piece = pl.ds(c * part_rows, part_rows)
            for to_right in (True, False):
                s = index if to_right else n - 1 - index
                has_source = t > 0 if to_right else t < n - 1
                now = from_left == (to_right == near)

                @pl.when(has_source & now & (s > t if to_right else s < t))
                def _():
                    scatter(q, s, c, to_right).wait_recv()
                    total = r.part[q, s, piece].astype(F32) + r.land[q, s, piece].astype(F32)
                    r.part[q, s, piece] = total.astype(BF)
                    scatter(q, s, c, to_right).start()

    everything = range(parts)
    forward(0)
    load_cot(1).start()
    backward(0, everything)
    arrive(gather, 1)
    pl.when(is_mid)(functools.partial(arrive, gather, 2))
    pl.when(is_mid)(lambda: load_cot(2).start())
    forward(1)
    backward(1, everything)
    pl.when(is_end)(functools.partial(arrive, gather, 2))
    forward(2)
    pl.when(is_mid)(functools.partial(backward, 2, everything))
    pl.when(is_end)(functools.partial(arrive, gather, 3))
    forward(3)

    @pl.when(is_mid)
    def _():
        gather_cot(t - 1, True).start()
        gather_cot(t + 1, False).start()

    @pl.when(is_end)
    def _():
        arrive(gather_cot, 2)
        load_cot(2).start()
        backward(2, everything)

    arrive(gather_cot, 3)
    load_cot(3).start()
    backward(3, (0, 1))
    keep_h(3).wait()

    first, second = pl.ds(0, tokens), pl.ds(tokens, tokens)
    reload = []
    for k, (src, dst, base) in enumerate(((r.h_out, r.wg, 0), (r.cot, r.wu, tokens))):
        for s in range(n):
            place = dst.at[pl.ds(base + s * rows, rows)]
            reload.append(pltpu.make_async_copy(src.at[s], place, r.re_sem.at[k, s]))
    for copy in reload:
        copy.start()
    pl.semaphore_signal(r.ready, inc=1, device_id={"dp": d ^ 1}, device_id_type=pl.DeviceIdType.MESH)
    pl.semaphore_wait(r.ready, 1)

    def block(w, j):
        if w == 2:
            return r.wg.at[pl.ds(tokens + j * chunk, chunk)]
        return r.wd.at[pl.ds((w * 4 + j) * chunk, chunk)]

    def lhs(w, j, who):
        cols = pl.ds(pl.multiple_of((2 * j + who) * chunk, chunk), chunk)
        if w == 0:
            return r.wu[second, cols]
        return r.n_buf[:, :, cols].reshape(tokens, chunk)

    def rhs(w, part):
        if w == 0:
            return r.wg[first, part]
        return r.gu[w - 1, :, :, part].reshape(tokens, part.stop - part.start)

    def stage_one(w, j):
        return copy_to(r.c_buf.at[lax.rem(j, 2)], block(w, j), r.one_send.at[w, j], r.one_recv.at[w, j], dp=d ^ 1)

    def stage_two(w, k):
        j = (2 * y + 1 - x, 2 * (1 - y) + 1 - x, 2 * (1 - y) + x, 2 * (1 - y) + 1 - x)[k]
        cols = pl.ds((k // 2) * halves, halves)
        return copy_to(
            block(w, j).at[:, cols], r.two.at[w, k], r.two_send.at[w, k], r.two_recv.at[w, k], dp=d ^ (2, 2, 4, 4)[k]
        )

    def keep_total(w, k):
        j = (2 * y + x, 2 * (1 - y) + x, 2 * y + x, 2 * y + 1 - x)[k]
        cols = pl.ds((k // 2) * halves, halves)
        return pltpu.make_async_copy(block(w, j).at[:, cols], r.tot.at[w, k], r.tot_sem.at[w, k])

    for w in range(3):
        if w == 0:
            for copy in reload:
                copy.wait()

        def give(j, carry):
            @pl.when(j >= 2)
            def _():
                stage_one(w, j - 2).wait_send()

            grads = lhs(w, j, 1 - core)
            for k in range(0, units, 512):
                part = slice(k, k + 512)
                r.c_buf[lax.rem(j, 2), :, part] = mm_at(grads, rhs(w, part)).astype(BF)
            stage_one(w, j).start()
            return carry

        def keep(j, carry):
            stage_one(w, j).wait_recv()
            grads = lhs(w, j, core)
            for k in range(0, units, 512):
                part = slice(k, k + 512)
                piece = block(w, j).at[:, part]
                piece[...] = (piece[...].astype(F32) + mm_at(grads, rhs(w, part))).astype(BF)
            return carry

        lax.fori_loop(0, 4, give, 0)
        if w == 0:
            end_sends(1, 3, (2,))
        lax.fori_loop(0, 4, keep, 0)
        if w == 0:
            end_sends(1, 3, (3,))
        for j in (2, 3):
            stage_one(w, j).wait_send()
        for k in range(4):
            stage_two(w, k).start()
            keep_total(w, k).start()
        if w == 0:
            pass_on(0, 2, True)
    pass_on(0, 3, True)
    pass_on(0, 3, False)
    pass_on(1, 2, True)
    pass_on(1, 3, True)
    pass_on(1, 3, False)

    def total_of(q):
        r.acc[...] = r.part[q, t].astype(F32)
        for to_right in (True, False):
            has_source = t > 0 if to_right else t < n - 1

            @pl.when(has_source)
            def _():
                for s in range(n):

                    @pl.when(s == t)
                    def _():
                        for c in range(parts):
                            scatter(q, s, c, to_right).wait_recv()

                slot = t if to_right else n
                r.acc[...] += r.land[q, slot].astype(F32)

    for q, out in ((0, r.fb_out), (1, r.fi_out)):
        total_of(q)
        copy = pltpu.make_async_copy(r.acc, out, r.out_sem.at[q])
        copy.start()
        copy.wait()

    for w in range(3):
        for k in range(4):
            keep_total(w, k).wait()
            stage_two(w, k).wait()
    for s in range(n):
        for to_right in (True, False):
            goes_on = t < n - 1 if to_right else t > 0

            @pl.when(goes_on & (s <= t if to_right else s >= t))
            def _():
                gather(s, to_right).wait_send()

            @pl.when(goes_on & (s < t if to_right else s > t))
            def _():
                gather_cot(s, to_right).wait_send()

            @pl.when(goes_on & (s > t if to_right else s < t))
            def _():
                for q in range(2):
                    for c in range(parts):
                        scatter(q, s, c, to_right).wait_send()


def middle_call(n, own_rows, cot_part, w_gate, w_up, w_down):
    rows, width = own_rows.shape
    units = w_gate.shape[1]
    parts = rows // 64
    shape = jax.ShapeDtypeStruct
    wide = shape((n, rows, width), BF)
    pieces = shape((3, 4, width // 8, units // 2), BF)
    any_spec = pl.BlockSpec(memory_space=pl.ANY)
    dma = pltpu.SemaphoreType.DMA
    return pl.pallas_call(
        functools.partial(middle_kernel, n),
        out_shape=[wide, shape((n, rows, units), BF), pieces, pieces] + [shape((rows, width), F32)] * 2,
        in_specs=[any_spec] * 5,
        out_specs=[any_spec] * 6,
        input_output_aliases={1: 0},
        scratch_shapes=[
            pltpu.VMEM((width, units), BF),
            pltpu.VMEM((width, units), BF),
            pltpu.VMEM((units, width), BF),
            pltpu.VMEM((n, rows, width), BF),
            pltpu.VMEM((2, n, rows, units), BF),
            pltpu.VMEM((rows, units), BF),
            pltpu.VMEM((2, rows, width), BF),
            pltpu.VMEM((2, n, rows, width), BF),
            pltpu.VMEM((2, n + 1, rows, width), BF),
            pltpu.VMEM((rows, width), F32),
            dma((3, units // 512)),
            dma((1,)),
            dma((2,)),
            dma((1,)),
            dma((2, n)),
            dma((3, 4)),
            dma((2,)),
            pltpu.SemaphoreType.REGULAR,
            dma((2, n)),
            dma((n,)),
            dma((2, n)),
            dma((n,)),
            dma((2, 2, n - 1, parts)),
            dma((2, 2, n - 1, parts)),
            dma((3, 4)),
            dma((3, 4)),
            dma((3, 4)),
            dma((3, 4)),
        ],
        compiler_params=pltpu.CompilerParams(
            vmem_limit_bytes=64 * 1024 * 1024 - 65536, collective_id=1, has_side_effects=True
        ),
        cost_estimate=pl.CostEstimate(
            flops=18 * n * rows * width * units, bytes_accessed=6 * width * units, transcendentals=0
        ),
        name="middle",
    )(own_rows, cot_part, w_gate, w_up, w_down)


def full_call(kernel, out_shapes, args, scratch=(), flops=0, name=None):
    spec = pl.BlockSpec(memory_space=pltpu.VMEM)
    return pl.pallas_call(
        kernel,
        out_shape=out_shapes,
        in_specs=[spec] * len(args),
        out_specs=[spec] * len(out_shapes),
        scratch_shapes=list(scratch),
        compiler_params=pltpu.CompilerParams(vmem_limit_bytes=VMEM_LIMIT),
        cost_estimate=pl.CostEstimate(flops=flops, bytes_accessed=flops // 400, transcendentals=0),
        name=name,
    )(*args)


def normalize(rows_wide, gain_wide):
    inverse = lax.rsqrt(jnp.mean(rows_wide * rows_wide, axis=-1, keepdims=True) + NORM_EPS)
    scaled_rows = rows_wide * inverse
    return scaled_rows, inverse, (scaled_rows * gain_wide).astype(BF)


def norm_back(normed_grad, scaled_rows, inverse, gain_wide):
    weighted = normed_grad * gain_wide
    return inverse * (weighted - scaled_rows * jnp.mean(weighted * scaled_rows, axis=-1, keepdims=True))


def pairs(n, bit):
    return [(i, i ^ bit) for i in range(n)]


def pick(array, index, axis):
    return lax.dynamic_index_in_dim(array, index, axis, keepdims=False)


def dp_scatter(give, keep, n_dp):
    me = lax.axis_index("dp")
    total = keep + lax.ppermute(give, "dp", pairs(n_dp, 1))
    if n_dp != 8:
        bit = 2
        while total.shape[0] > 1:
            parts = total.reshape(-1, 2, *total.shape[1:])
            mine = (me // bit) % 2
            total = pick(parts, mine, 1) + lax.ppermute(pick(parts, 1 - mine, 1), "dp", pairs(n_dp, bit))
            bit *= 2
        return total[0].astype(F32)
    x, y = (me // 2) % 2, me // 4
    cols = total.shape[-1] // 2
    parts = total.reshape(2, 2, *total.shape[1:])
    a, b = parts[..., :cols], parts[..., cols:]
    got_a = lax.ppermute(pick(a, 1 - x, 1), "dp", pairs(n_dp, 2))
    got_b = lax.ppermute(pick(b, 1 - y, 0), "dp", pairs(n_dp, 4))
    a = pick(a, x, 1) + got_a
    b = pick(b, y, 0) + got_b
    got_a = lax.ppermute(pick(a, 1 - y, 0), "dp", pairs(n_dp, 4))
    got_b = lax.ppermute(pick(b, 1 - x, 0), "dp", pairs(n_dp, 2))
    a = pick(a, y, 0).astype(F32) + got_a.astype(F32)
    b = pick(b, x, 0).astype(F32) + got_b.astype(F32)
    return jnp.concatenate([a, b], axis=-1)


def core_split(rows, n_dp):
    tokens, width = rows.shape
    core = lax.axis_index("dp") % 2
    parts = rows.reshape(tokens, n_dp // 2, 2, width // n_dp)
    return [pick(parts, c, 2).reshape(tokens, width // 2) for c in (1 - core, core)]


def grad_scatter(split_rows, cols, n_dp):
    give, keep = [
        mm_at(part, cols).astype(BF).reshape(n_dp // 2, 2 * part.shape[1] // n_dp, cols.shape[1])
        for part in split_rows
    ]
    return dp_scatter(give, keep, n_dp)


def after(value, *others):
    return lax.optimization_barrier((value, *others))[0]


def shards(n_dp, n_t, hidden_in, gain_attn, w_query, w_key, w_value, w_out, gain_ffn, w_gate, w_up, w_down, segments, parents, cotangent):
    tokens = segments.shape[0]
    own, width = hidden_in.shape
    q_cols, kv_cols, units = w_query.shape[1], w_key.shape[1], w_gate.shape[1]
    heads = q_cols // HD
    me_t = lax.axis_index("tensor")
    me_dp = lax.axis_index("dp")
    gain_attn_wide = gain_attn.astype(F32)
    gain_ffn_wide = gain_ffn.astype(F32)

    def ring(value, shift):
        return lax.ppermute(value, "tensor", [(i, (i + shift) % n_t) for i in range(n_t)])

    ancestry, depth = tree_tables(segments, parents)
    cosine, sine = rope_tables(depth)
    bias = jnp.where(jnp.repeat(ancestry, BLK, axis=1) > 0.5, 0.0, NEG)
    fused = n_dp == 8 and n_t == 4 and units == width and q_cols == 2 * own and tokens * 2 == width
    x_all, cot_all, w_out_all, queries, keys, values, mixed, lse, mixed_own, middle, normed_ffn = attn_call(
        n_dp, n_t, fused, hidden_in, cotangent, gain_attn[None], gain_ffn[None], w_query, w_key, w_value, w_out, cosine, sine, bias
    )
    x_all = x_all.reshape(tokens, width)
    w_out_all = w_out_all.reshape(n_t * q_cols, width)
    rows_wide = hidden_in.astype(F32)
    if fused:
        unused_cot, unused_h, totals, twos, ffn_in_grad, fb_sum = middle_call(
            n_t, normed_ffn, cot_all, w_gate, w_up, w_down
        )
        output = (middle + fb_sum).astype(BF)
        arrays = dict(
            fi=ffn_in_grad,
            mid=middle,
            cot=cotangent,
            hid=hidden_in,
            q=queries,
            k=keys,
            v=values,
            m=mixed,
            lse=lse,
            cos=cosine,
            sin=sine,
            mixed=mixed_own,
            wq=w_query,
            wk=w_key,
            wv=w_value,
        )
        input_grad, project_wgrad, w_out_grad, gain_grads, threes = back_call(
            n_t,
            arrays,
            gain_attn[None],
            gain_ffn[None],
            bias,
            x_all.reshape(n_t, own, width),
            w_out_all.reshape(n_t, q_cols, width),
            totals,
            twos,
        )
        w_out_grad = w_out_grad.T
        final = [totals[:, k].astype(F32) + twos[:, k].astype(F32) + threes[:, k // 2].astype(F32) for k in (0, 2)]
        w_down_grad, w_gate_grad, w_up_grad = [jnp.concatenate([f[w] for f in final], axis=1) for w in range(3)]
        w_down_grad = w_down_grad.T
        w_query_grad = project_wgrad[:, :q_cols]
        w_key_grad = project_wgrad[:, q_cols : q_cols + kv_cols]
        w_value_grad = project_wgrad[:, q_cols + kv_cols :]
        gain_attn_grad, gain_ffn_grad = gain_grads[0], gain_grads[1]
    else:
        w_project = jnp.concatenate([w_query, w_key, w_value], axis=1)
        h_all, gg_all, ug_all, n_all, fb_part, ffn_in_grad = ffn_call(n_t, normed_ffn, cot_all, w_gate, w_up, w_down)
        fb_sum = lax.psum_scatter(fb_part.reshape(tokens, width), "tensor", scatter_dimension=0, tiled=True)
        output = (middle + fb_sum.astype(F32)).astype(BF)
        h_all, gg_all, ug_all = [a.reshape(tokens, units) for a in (h_all, gg_all, ug_all)]
        cot_split = core_split(cot_all.reshape(tokens, width), n_dp)
        normed_split = core_split(n_all.reshape(tokens, width), n_dp)
        w_down_grad = grad_scatter(cot_split, h_all, n_dp).T
        w_gate_grad = grad_scatter(normed_split, gg_all, n_dp)
        w_up_grad = grad_scatter(normed_split, ug_all, n_dp)

        scaled_attn, inverse_attn, _ = normalize(rows_wide, gain_attn_wide)
        scaled_ffn, inverse_ffn, _ = normalize(middle, gain_ffn_wide)
        middle_grad = cotangent.astype(F32) + norm_back(ffn_in_grad, scaled_ffn, inverse_ffn, gain_ffn_wide)
        branch_grad = middle_grad.astype(BF)
        mixed_grads = mm_bt(branch_grad, w_out_all).astype(BF).reshape(own, n_t, q_cols)
        mixed_grads = [pick(mixed_grads, (me_t + n_t - d) % n_t, 1) for d in range(n_t)]
        mixed_grads = [mixed_grads[0]] + [ring(mixed_grads[d], n_t - d) for d in range(1, n_t)]
        mixed_grad = jnp.roll(jnp.concatenate(mixed_grads, axis=0), me_t * own, axis=0)

        (project_grad,) = full_call(
            attn_bwd_kernel,
            [jax.ShapeDtypeStruct((tokens, q_cols + 2 * kv_cols), BF)],
            (queries, keys, values, mixed, lse, mixed_grad, cosine, sine, bias),
            scratch=[pltpu.VMEM((tokens, kv_cols), F32)] * 2,
            flops=10 * heads * tokens * tokens * HD,
            name="attn_bwd",
        )
        dq, dk, dv = (
            project_grad[:, :q_cols],
            project_grad[:, q_cols : q_cols + kv_cols],
            project_grad[:, q_cols + kv_cols :],
        )
        attn_in_part = mm_bt(project_grad, w_project).astype(BF)
        attn_in_grad = lax.psum_scatter(attn_in_part, "tensor", scatter_dimension=0, tiled=True).astype(F32)

        mixed_wide = jnp.moveaxis(mixed_own, 0, 1).reshape(own, n_t * q_cols)
        out_grad = grad_scatter(core_split(branch_grad, n_dp), mixed_wide, n_dp)
        out_parts = out_grad.reshape(-1, n_t, q_cols)
        w_out_grad = pick(out_parts, me_t, 1)
        for d in range(1, n_t):
            piece = pick(out_parts, (me_t + d) % n_t, 1).astype(BF)
            w_out_grad = w_out_grad + ring(piece, d).astype(F32)
        w_out_grad = w_out_grad.T

        project_wgrad = grad_scatter(core_split(x_all, n_dp), project_grad, n_dp)
        w_query_grad = project_wgrad[:, :q_cols]
        w_key_grad = project_wgrad[:, q_cols : q_cols + kv_cols]
        w_value_grad = project_wgrad[:, q_cols + kv_cols :]

        input_grad = (middle_grad + norm_back(attn_in_grad, scaled_attn, inverse_attn, gain_attn_wide)).astype(BF)

        def own_rows(array):
            return lax.dynamic_slice_in_dim(array, me_dp * (width // n_dp), width // n_dp, 0).astype(F32)

        gain_sums = jnp.stack(
            [
                jnp.sum(own_rows(w_project) * project_wgrad, axis=1),
                jnp.sum(own_rows(w_gate) * w_gate_grad, axis=1) + jnp.sum(own_rows(w_up) * w_up_grad, axis=1),
            ]
        )
        bit = 1
        while bit < n_t:
            gain_sums = gain_sums + lax.ppermute(gain_sums, "tensor", pairs(n_t, bit))
            bit *= 2
        gain_attn_grad = gain_sums[0] / own_rows(gain_attn)
        gain_ffn_grad = gain_sums[1] / own_rows(gain_ffn)

    return (
        output,
        input_grad,
        gain_attn_grad,
        w_query_grad,
        w_key_grad,
        w_value_grad,
        w_out_grad,
        gain_ffn_grad,
        w_gate_grad,
        w_up_grad,
        w_down_grad,
    )


def solution(mesh):
    return jax.shard_map(
        functools.partial(shards, mesh.shape["dp"], mesh.shape["tensor"]),
        mesh=mesh,
        in_specs=(
            P(("dp", "tensor"), None),
            P(),
            P(None, "tensor"),
            P(None, "tensor"),
            P(None, "tensor"),
            P("tensor", None),
            P(),
            P(None, "tensor"),
            P(None, "tensor"),
            P("tensor", None),
            P("dp"),
            P("dp"),
            P(("dp", "tensor"), None),
        ),
        out_specs=(
            P(("dp", "tensor"), None),
            P(("dp", "tensor"), None),
            P("dp"),
            P("dp", "tensor"),
            P("dp", "tensor"),
            P("dp", "tensor"),
            P("tensor", "dp"),
            P("dp"),
            P("dp", "tensor"),
            P("dp", "tensor"),
            P("tensor", "dp"),
        ),
        check_vma=False,
    )
```

```python
import functools
import math
import types

import jax
import jax.numpy as jnp
from jax import lax
from jax.experimental import pallas as pl
from jax.experimental.pallas import tpu as pltpu
from jax.sharding import PartitionSpec as P

HD = 128
BLK = 128
NORM_EPS = 1e-05
ROPE_BASE = 1000000.0
SCALE = HD ** (-0.5)
SCALE2 = SCALE * math.log2(math.e)
NEG = -1e30
BF = jnp.bfloat16
F32 = jnp.float32
VMEM_LIMIT = 56 * 1024 * 1024


def mm(a, b):
    return jnp.dot(a, b, preferred_element_type=F32)


def mm_bt(a, b):
    return lax.dot_general(a, b, (((1,), (1,)), ((), ())), preferred_element_type=F32)


def mm_at(a, b):
    return lax.dot_general(a, b, (((0,), (0,)), ((), ())), preferred_element_type=F32)


def tree_tables(segment_ids, parent_ids):
    block_count = parent_ids.shape[0]
    first_ids = segment_ids.reshape(block_count, -1)[:, 0]
    block_iota = jnp.arange(block_count, dtype=jnp.int32)
    same_tree = first_ids[:, None] == first_ids[None, :]
    tree_start = jnp.min(jnp.where(same_tree, block_iota[None, :], block_count), axis=1)
    parent_block = tree_start + parent_ids
    step = (block_iota[None, :] == parent_block[:, None]) | (
        block_iota[None, :] == block_iota[:, None]
    )
    for _ in range(3):
        step = jnp.any(step[:, :, None] & step[None, :, :], axis=1)
    ancestry = step.astype(F32)
    return ancestry, jnp.sum(ancestry, axis=1) - 1.0


def rope_tables(depth):
    token_total = depth.shape[0] * BLK
    offsets = (jnp.arange(token_total, dtype=jnp.int32) % BLK).astype(F32)
    places = jnp.repeat(depth, BLK) * BLK + offsets
    freq_index = jnp.arange(HD // 2, dtype=jnp.int32).astype(F32)
    inverse_freq = ROPE_BASE ** (-2.0 * freq_index / HD)
    angles = places[:, None] * inverse_freq[None, :]
    cosine, sine = jnp.cos(angles), jnp.sin(angles)
    return jnp.concatenate([cosine, cosine], axis=1), jnp.concatenate([-sine, sine], axis=1)


def head_cols(h):
    return slice(h * HD, (h + 1) * HD)


def causal_tile(rep):
    rows = lax.broadcasted_iota(jnp.int32, (BLK, BLK), 0)
    cols = lax.broadcasted_iota(jnp.int32, (BLK, BLK), 1)
    tile = cols <= rows
    return jnp.concatenate([tile] * rep, axis=0) if rep > 1 else tile


def stack_heads(ref, rows, first, rep):
    parts = [ref[rows, head_cols(first + i)] for i in range(rep)]
    return jnp.concatenate(parts, axis=0) if rep > 1 else parts[0]


def attend_block(b, q_ref, k_ref, v_ref, bias_ref, m_ref, lse_ref, causal, rep):
    rows = slice(b * BLK, (b + 1) * BLK)
    past = slice(0, b * BLK)
    for g in range(k_ref.shape[1] // HD):
        q = stack_heads(q_ref, rows, g * rep, rep)
        s_diag = jnp.where(causal, mm_bt(q, k_ref[rows, head_cols(g)]) * SCALE2, NEG)
        top = jnp.max(s_diag, axis=1, keepdims=True)
        if b:
            s_past = mm_bt(q, k_ref[past, head_cols(g)]) * SCALE2 + bias_ref[b : b + 1, past]
            top = jnp.maximum(top, jnp.max(s_past, axis=1, keepdims=True))
        e_diag = jnp.exp2(s_diag - top)
        mass = jnp.sum(e_diag, axis=1, keepdims=True)
        out = mm(e_diag.astype(BF), v_ref[rows, head_cols(g)])
        if b:
            e_past = jnp.exp2(s_past - top)
            mass = mass + jnp.sum(e_past, axis=1, keepdims=True)
            out = out + mm(e_past.astype(BF), v_ref[past, head_cols(g)])
        out = (out / mass).astype(BF)
        lse = top + jnp.log2(mass)
        for i in range(rep):
            h = g * rep + i
            m_ref[rows, head_cols(h)] = out[i * BLK : (i + 1) * BLK]
            lse_ref[rows, h : h + 1] = lse[i * BLK : (i + 1) * BLK]


def copy_to(src, dst, send_sem, recv_sem, **where):
    return pltpu.make_async_remote_copy(
        src_ref=src,
        dst_ref=dst,
        send_sem=send_sem,
        recv_sem=recv_sem,
        device_id=where,
        device_id_type=pl.DeviceIdType.MESH,
    )


def group_barrier(masks, n, d, t):
    barrier = pltpu.get_barrier_semaphore()
    for k in range(1, n):
        pl.semaphore_signal(
            barrier, inc=1, device_id={"tensor": lax.rem(t + k, n)}, device_id_type=pl.DeviceIdType.MESH
        )
    for mask in masks:
        pl.semaphore_signal(barrier, inc=1, device_id={"dp": d ^ mask}, device_id_type=pl.DeviceIdType.MESH)
    pl.semaphore_wait(barrier, n - 1 + len(masks))


def attn_kernel(
    n_dp,
    n,
    one_hop,
    hidden_ref,
    cot_ref,
    gain_a_ref,
    gain_f_ref,
    wq_hbm,
    wk_hbm,
    wv_hbm,
    wo_hbm,
    cos_ref,
    sin_ref,
    bias_ref,
    x_out,
    cot_out,
    wo_out,
    q_ref,
    k_ref,
    v_ref,
    m_ref,
    lse_ref,
    mixed_ref,
    middle_ref,
    normed_ref,
    own_buf,
    x_buf,
    wq_ref,
    wk_ref,
    wv_ref,
    wo_ref,
    w_sem,
    x_sem,
    misc_sem,
    ag_send,
    ag_recv,
    cot_send,
    cot_recv,
    wz_send,
    wz_recv,
    wp_send,
    wp_recv,
    wc_send,
    wc_recv,
    m_send,
    m_recv,
):
    t, d = lax.axis_index("tensor"), lax.axis_index("dp")
    rows, width = hidden_ref.shape
    q_cols = wq_ref.shape[1]
    heads, kv_heads = q_cols // HD, wk_ref.shape[1] // HD
    rep = heads // kv_heads
    share = q_cols // n_dp
    half = q_cols // 2
    order = arrival_order(t, n)
    is_mid = (t > 0) & (t < n - 1)
    core, plane = lax.rem(d, 2), d // 2
    masks = list(range(2, n_dp, 2))

    load_w = [
        pltpu.make_async_copy(src, dst, w_sem.at[i])
        for i, (src, dst) in enumerate(((wq_hbm, wq_ref), (wk_hbm, wk_ref), (wv_hbm, wv_ref)))
    ]
    own_wo = pltpu.make_async_copy(wo_hbm, wo_ref.at[t], misc_sem.at[0])
    own_cot = pltpu.make_async_copy(cot_ref, cot_out.at[t], misc_sem.at[1])
    for copy in load_w:
        copy.start()
    own_wo.start()
    own_cot.start()

    def norm(values, gain_ref):
        inverse = lax.rsqrt(jnp.mean(values * values, axis=-1, keepdims=True) + NORM_EPS)
        return (values * inverse * gain_ref[...].astype(F32)).astype(BF)

    for r in range(0, rows, 64):
        part = slice(r, r + 64)
        own_buf[part, :] = norm(hidden_ref[part, :].astype(F32), gain_a_ref)
    group_barrier([1, *masks], n, d, t)

    def line_copy(buf, send_sem, recv_sem, s, to_right, src=None):
        return copy_to(
            buf.at[s] if src is None else src,
            buf.at[s],
            send_sem.at[0 if to_right else 1, s],
            recv_sem.at[s],
            tensor=t + 1 if to_right else t - 1,
        )

    gather_x = functools.partial(line_copy, x_buf, ag_send, ag_recv)
    gather_cot = functools.partial(line_copy, cot_out, cot_send, cot_recv)

    def first_hop(gather, src):
        pl.when(t < n - 1)(lambda: gather(t, True, src).start())
        pl.when(t > 0)(lambda: gather(t, False, src).start())

    def arrive(gather, i):
        s = order[i]
        gather(s, True).wait_recv()
        pl.when((s < t) & (t < n - 1))(lambda: gather(s, True).start())
        pl.when((s > t) & (t > 0))(lambda: gather(s, False).start())

    def keep_rows(i):
        return pltpu.make_async_copy(own_buf if i == 0 else x_buf.at[order[i]], x_out.at[order[i]], x_sem.at[i])

    my_rows = pl.ds(pl.multiple_of(core * half + plane * share, 16), share)
    my_half = pl.ds(pl.multiple_of(core * half, 16), half)

    def wo_line(k):
        return copy_to(
            wo_hbm.at[my_rows],
            wo_ref.at[t, my_rows],
            wz_send.at[k - 1],
            wz_recv.at[k - 1],
            tensor=lax.rem(t + k, n),
        )

    def wo_plane(k, j):
        s = lax.rem(t + n - k, n)
        return copy_to(
            wo_ref.at[s, my_rows],
            wo_ref.at[s, my_rows],
            wp_send.at[k - 1, j],
            wp_recv.at[k - 1, j],
            dp=d ^ masks[j],
        )

    def wo_core(k):
        s = lax.rem(t + n - k, n)
        return copy_to(
            wo_ref.at[s, my_half], wo_ref.at[s, my_half], wc_send.at[k - 1], wc_recv.at[k - 1], dp=d ^ 1
        )

    first_hop(gather_x, own_buf)
    for k in range(1, n):
        wo_line(k).start()
    keep_rows(0).start()

    for copy in load_w:
        copy.wait()
    for i in range(n):
        s = order[i]
        if i == 1:
            arrive(gather_x, 1)
            if n > 2:
                pl.when(is_mid)(lambda: arrive(gather_x, 2))
        elif i > 1:
            if i > 2:
                arrive(gather_x, i)
            else:
                pl.when(jnp.logical_not(is_mid))(lambda: arrive(gather_x, 2))
        if i:
            keep_rows(i).start()
        x = own_buf[...] if i == 0 else x_buf[s]
        here = pl.ds(pl.multiple_of(s * rows, rows), rows)
        cosine, sine = cos_ref[here, :], sin_ref[here, :]
        for w_ref, out_ref, count in ((wq_ref, q_ref, heads), (wk_ref, k_ref, kv_heads)):
            raw = mm(x, w_ref[...])
            for h in range(count):
                u = raw[:, head_cols(h)]
                out_ref[here, head_cols(h)] = (u * cosine + pltpu.roll(u, HD // 2, 1) * sine).astype(BF)
        v_ref[here, :] = mm(x, wv_ref[...]).astype(BF)
        if i == 1:
            for k in range(1, n):
                wo_line(k).wait_recv()
                for j in range(len(masks)):
                    wo_plane(k, j).start()
        if i == n - 1:
            first_hop(gather_cot, cot_ref)
            for k in range(1, n):
                for j in range(len(masks)):
                    wo_plane(k, j).wait_recv()
                wo_core(k).start()

    def heads_to(r):
        here = pl.ds(r * rows, rows)
        return copy_to(m_ref.at[here], mixed_ref.at[t], m_send.at[r], m_recv.at[t], tensor=r)

    causal = causal_tile(rep)
    for b in range(n * rows // BLK):
        attend_block(b, q_ref, k_ref, v_ref, bias_ref, m_ref, lse_ref, causal, rep)
        if (b + 1) * BLK % rows == 0:
            r = (b + 1) * BLK // rows - 1
            pl.when(t != r)(lambda: heads_to(r).start())

            @pl.when(t == r)
            def _():
                mixed_ref[r] = m_ref[r * rows : (r + 1) * rows, :]

    if n > 2 and not one_hop:

        @pl.when(is_mid)
        def _():
            arrive(gather_cot, 1)
            arrive(gather_cot, 2)

    own_wo.wait()
    for k in range(1, n):
        s = lax.rem(t + n - k, n)
        copy_to(m_ref.at[pl.ds(0, rows)], mixed_ref.at[s], m_send.at[0], m_recv.at[s], tensor=s).wait_recv()
        wo_core(k).wait_recv()
    keep_wo = pltpu.make_async_copy(wo_ref, wo_out, misc_sem.at[0])
    keep_wo.start()
    for r in range(0, rows, 128):
        part = slice(r, r + 128)
        total = hidden_ref[part, :].astype(F32)
        for s in range(n):
            total = total + mm(mixed_ref[s, part, :], wo_ref[s])
        middle_ref[part, :] = total
        normed_ref[part, :] = norm(total, gain_f_ref)

    if one_hop:
        pl.when(t > 0)(lambda: gather_cot(t - 1, True).wait_recv())
        pl.when(t < n - 1)(lambda: gather_cot(t + 1, False).wait_recv())
    else:
        for i in range(1, n):
            if i > 2:
                arrive(gather_cot, i)
            else:
                pl.when(jnp.logical_not(is_mid))(functools.partial(arrive, gather_cot, i))
    own_cot.wait()
    keep_wo.wait()
    for i in range(n):
        keep_rows(i).wait()
    for k in range(1, n):
        wo_line(k).wait_send()
        wo_core(k).wait_send()
        for j in range(len(masks)):
            wo_plane(k, j).wait_send()
    if one_hop:
        pl.when(t < n - 1)(lambda: gather_cot(t, True).wait_send())
        pl.when(t > 0)(lambda: gather_cot(t, False).wait_send())
    for s in range(n):
        pl.when(t != s)(lambda: heads_to(s).wait_send())
        for to_right in (True, False):
            goes_on = t < n - 1 if to_right else t > 0

            @pl.when(goes_on & (s <= t if to_right else s >= t))
            def _():
                gather_x(s, to_right).wait_send()
                if not one_hop:
                    gather_cot(s, to_right).wait_send()


def attn_call(n_dp, n, one_hop, hidden, cot, gain_a, gain_f, wq, wk, wv, wo, cosine, sine, bias):
    rows, width = hidden.shape
    q_cols, kv_cols = wq.shape[1], wk.shape[1]
    tokens = n * rows
    any_spec = pl.BlockSpec(memory_space=pl.ANY)
    vmem_spec = pl.BlockSpec(memory_space=pltpu.VMEM)
    dma = pltpu.SemaphoreType.DMA
    masks = n_dp // 2 - 1
    shape = jax.ShapeDtypeStruct
    return pl.pallas_call(
        functools.partial(attn_kernel, n_dp, n, one_hop),
        out_shape=[
            shape((n, rows, width), BF),
            shape((n, rows, width), BF),
            shape((n, q_cols, width), BF),
            shape((tokens, q_cols), BF),
            shape((tokens, kv_cols), BF),
            shape((tokens, kv_cols), BF),
            shape((tokens, q_cols), BF),
            shape((tokens, HD), F32),
            shape((n, rows, q_cols), BF),
            shape((rows, width), F32),
            shape((rows, width), BF),
        ],
        in_specs=[vmem_spec, any_spec, vmem_spec, vmem_spec] + [any_spec] * 4 + [vmem_spec] * 3,
        out_specs=[any_spec] * 3 + [vmem_spec] * 8,
        scratch_shapes=[
            pltpu.VMEM((rows, width), BF),
            pltpu.VMEM((n, rows, width), BF),
            pltpu.VMEM((width, q_cols), BF),
            pltpu.VMEM((width, kv_cols), BF),
            pltpu.VMEM((width, kv_cols), BF),
            pltpu.VMEM((n, q_cols, width), BF),
            dma((3,)),
            dma((n,)),
            dma((2,)),
            dma((2, n)),
            dma((n,)),
            dma((2, n)),
            dma((n,)),
            dma((n - 1,)),
            dma((n - 1,)),
            dma((n - 1, masks)),
            dma((n - 1, masks)),
            dma((n - 1,)),
            dma((n - 1,)),
            dma((n,)),
            dma((n,)),
        ],
        compiler_params=pltpu.CompilerParams(
            vmem_limit_bytes=VMEM_LIMIT, collective_id=2, has_side_effects=True
        ),
        cost_estimate=pl.CostEstimate(
            flops=2 * tokens * width * (q_cols + 2 * kv_cols), bytes_accessed=1 << 25, transcendentals=0
        ),
        name="attn",
    )(hidden, cot, gain_a, gain_f, wq, wk, wv, wo, cosine, sine, bias)


def arrival_order(t, n):
    near = jnp.minimum(t, n - 1 - t)
    order = [t]
    for i in range(1, n):
        both = t - (i + 1) // 2 if i % 2 else t + i // 2
        one_side = jnp.where(t > n - 1 - t, t - (i - near), t + (i - near))
        order.append(jnp.where(i <= 2 * near, both, one_side))
    return order


def attend_back_block(g, b, q_ref, k_ref, v_ref, o_ref, lse_ref, do_ref, turn_back, bias_ref, d_ref, dk_acc, dv_acc):
    heads, kv_heads = q_ref.shape[1] // HD, k_ref.shape[1] // HD
    rep = heads // kv_heads
    last = q_ref.shape[0] // BLK - 1
    causal = causal_tile(rep)
    rows = slice(b * BLK, (b + 1) * BLK)
    q = stack_heads(q_ref, rows, g * rep, rep)
    do = stack_heads(do_ref, rows, g * rep, rep)
    o = stack_heads(o_ref, rows, g * rep, rep)
    lse = [lse_ref[rows, h : h + 1] for h in range(g * rep, (g + 1) * rep)]
    lse = jnp.concatenate(lse, axis=0) if rep > 1 else lse[0]
    delta = jnp.sum(do.astype(F32) * o.astype(F32), axis=1, keepdims=True)
    k_d = k_ref[rows, head_cols(g)]
    p = jnp.where(causal, jnp.exp2(mm_bt(q, k_d) * SCALE2 - lse), 0.0)
    ds = (p * (mm_bt(do, v_ref[rows, head_cols(g)]) - delta)).astype(BF)
    dq = mm(ds, k_d)
    dk = mm_at(ds, q)
    dv = mm_at(p.astype(BF), do)
    if b < last:
        dk = dk + dk_acc[rows, head_cols(g)]
        dv = dv + dv_acc[rows, head_cols(g)]
    d_ref[rows, head_cols(heads + g)] = turn_back(dk * SCALE, rows)
    d_ref[rows, head_cols(heads + kv_heads + g)] = dv.astype(BF)
    if b:
        past = slice(0, b * BLK)
        k_p = k_ref[past, head_cols(g)]
        p = jnp.exp2(mm_bt(q, k_p) * SCALE2 + (bias_ref[b : b + 1, past] - lse))
        ds = (p * (mm_bt(do, v_ref[past, head_cols(g)]) - delta)).astype(BF)
        dq = dq + mm(ds, k_p)
        dk = mm_at(ds, q)
        dv = mm_at(p.astype(BF), do)
        if b < last:
            dk = dk + dk_acc[past, head_cols(g)]
            dv = dv + dv_acc[past, head_cols(g)]
        dk_acc[past, head_cols(g)] = dk
        dv_acc[past, head_cols(g)] = dv
    dq = dq * SCALE
    for i in range(rep):
        d_ref[rows, head_cols(g * rep + i)] = turn_back(dq[i * BLK : (i + 1) * BLK], rows)


def attn_bwd_kernel(q_ref, k_ref, v_ref, o_ref, lse_ref, do_ref, cos_ref, sin_ref, bias_ref, d_ref, dk_acc, dv_acc):
    def turn_back(grad, rows):
        return (grad * cos_ref[rows, :] - pltpu.roll(grad, HD // 2, 1) * sin_ref[rows, :]).astype(BF)

    for b in range(q_ref.shape[0] // BLK - 1, -1, -1):
        for g in range(k_ref.shape[1] // HD):
            attend_back_block(
                g, b, q_ref, k_ref, v_ref, o_ref, lse_ref, do_ref, turn_back, bias_ref, d_ref, dk_acc, dv_acc
            )


BACK_INS = ("fi", "mid", "cot", "hid", "q", "k", "v", "m", "lse", "cos", "sin", "mixed", "wq", "wk", "wv")
BACK_NAMES = (
    BACK_INS,
    ("gain_a", "gain_f", "bias", "x_h", "wo_h", "tot_h", "two_h", "late_h"),
    ("input_grad", "project_grad", "out_grad", "gain_grad", "three_h", "late_two"),
    tuple(name + "_b" for name in BACK_INS),
    ("wo", "bg", "mg", "do", "dqkv", "dk_acc", "dv_acc", "got", "one_o", "one_p", "two_o", "two_p"),
    ("three_o", "three_p", "s3", "give", "zr", "gain_st", "gain_dp", "gain_line"),
    ("in_sem", "wo_sem", "x_sem", "s3_sem", "mg_send", "mg_recv", "th_send", "th_recv", "one_send", "one_recv"),
    ("stw_send", "stw_recv", "sth_send", "sth_recv", "z_send", "z_recv", "rs_send", "rs_recv"),
    ("gd_send", "gd_recv", "gl_send", "gl_recv", "lt_send", "lt_recv"),
)


def back_kernel(n, *refs):
    names = [name for group in BACK_NAMES for name in group]
    r = types.SimpleNamespace(**dict(zip(names, refs, strict=True)))
    t, d = lax.axis_index("tensor"), lax.axis_index("dp")
    rows, width = r.bg.shape
    q_cols, kv_cols = r.q_b.shape[1], r.k_b.shape[1]
    all_cols = q_cols + 2 * kv_cols
    tokens = n * rows
    core, x, y = lax.rem(d, 2), lax.rem(d // 2, 2), d // 4
    chunk = width // 8
    parts = r.rs_send.shape[2]
    part_rows = rows // parts
    order = arrival_order(t, n)
    is_mid = (t > 0) & (t < n - 1)
    pairs_o = [(2 * y + x, 2 * y + 1 - x, 2), (2 * (1 - y) + x, 2 * (1 - y) + 1 - x, 2)]
    pairs_o += [(2 * y + x, 2 * (1 - y) + x, 4), (2 * y + 1 - x, 2 * (1 - y) + 1 - x, 4)]

    loads = {
        name: pltpu.make_async_copy(getattr(r, name), getattr(r, name + "_b"), r.in_sem.at[i])
        for i, name in enumerate(BACK_INS)
    }
    load_wo = [pltpu.make_async_copy(r.wo_h.at[s], r.wo.at[s], r.wo_sem.at[s]) for s in range(n)]
    load_x = [pltpu.make_async_copy(r.x_h.at[s], r.wo.at[s, pl.ds(0, rows)], r.x_sem.at[s]) for s in range(n)]
    half = r.s3.shape[3]
    load_s3 = []
    for w in range(3):
        for k in range(2):
            load_s3.append(pltpu.make_async_copy(r.tot_h.at[w, 2 * k + 1], r.s3.at[w, k], r.s3_sem.at[0, w, k]))
            landing = r.wo.at[w, pl.ds(rows, rows), pl.ds(k * half, half)]
            other = r.two_h.at[w, 2 * k + 1] if w < 2 else r.late_two.at[2 * k + 1]
            load_s3.append(pltpu.make_async_copy(other, landing, r.s3_sem.at[1, w, k]))

    def late_stage(k):
        src, dst = r.late_h.at[k], r.late_two.at[k]
        return copy_to(src, dst, r.lt_send.at[k], r.lt_recv.at[k], dp=d ^ (2, 2, 4, 4)[k])

    for name in ("fi", "mid", "cot"):
        loads[name].start()
    for copy in load_wo:
        copy.start()
    for name in BACK_INS[3:]:
        loads[name].start()
    for copy in load_s3[::2]:
        copy.start()
    group_barrier(range(1, 8), n, d, t)
    for k in (1, 3, 0, 2):
        late_stage(k).start()

    for name in ("fi", "mid", "cot"):
        loads[name].wait()

    def norm_back_part(grad, values, gain_ref):
        inverse = lax.rsqrt(jnp.mean(values * values, axis=-1, keepdims=True) + NORM_EPS)
        scaled = values * inverse
        weighted = grad * gain_ref[...].astype(F32)
        back = inverse * (weighted - scaled * jnp.mean(weighted * scaled, axis=-1, keepdims=True))
        return back, grad * scaled

    def gain_along_dp(mask):
        return copy_to(
            r.gain_st.at[d ^ mask, pl.ds(0, 8)],
            r.gain_dp.at[mask - 1],
            r.gd_send.at[mask - 1],
            r.gd_recv.at[mask - 1],
            dp=d ^ mask,
        )

    gain_sum = jnp.zeros((8, width), F32)
    for first in range(0, rows, 64):
        part = slice(first, first + 64)
        back, gain_part = norm_back_part(r.fi_b[part, :], r.mid_b[part, :], r.gain_f)
        gain_sum = gain_sum + jnp.sum(gain_part.reshape(8, 8, width), axis=0)
        total = r.cot_b[part, :].astype(F32) + back
        r.fi_b[part, :] = total
        r.bg[part, :] = total.astype(BF)
    for c in range(8):
        r.gain_st[c, 0:8, :] = gain_sum[:, c * chunk : (c + 1) * chunk]
    for mask in range(1, 8):
        gain_along_dp(mask).start()

    def rows_of(s):
        return pl.ds(pl.multiple_of(s * rows, rows), rows)

    def heads_back(k):
        s = lax.rem(t + k, n)
        return copy_to(r.mg.at[s], r.do.at[rows_of(t)], r.mg_send.at[k - 1], r.mg_recv.at[k - 1], tensor=s)

    for copy in load_wo:
        copy.wait()
    for k in range(1, n):
        s = lax.rem(t + k, n)
        r.mg[s] = mm_bt(r.bg[...], r.wo[s]).astype(BF)
        heads_back(k).start()
    r.do[rows_of(t), :] = mm_bt(r.bg[...], r.wo[t]).astype(BF)

    for copy in load_s3[1:8:2] + load_x:
        copy.start()

    def ffn_three(w, k):
        return copy_to(r.s3.at[w, k], r.three_h.at[w, k], r.th_send.at[w, k], r.th_recv.at[w, k], dp=d ^ (4, 2)[k])

    def start_ffn_three(w):
        for k in range(2):
            for copy in load_s3[4 * w + 2 * k : 4 * w + 2 * k + 2]:
                copy.wait()
            other = r.wo[w, rows : 2 * rows, k * half : (k + 1) * half]
            r.s3[w, k] = (r.s3[w, k].astype(F32) + other.astype(F32)).astype(BF)
            ffn_three(w, k).start()

    start_ffn_three(0)
    start_ffn_three(1)

    ones, twos, threes = (r.one_o, r.one_p), (r.two_o, r.two_p), (r.three_o, r.three_p)

    def stage_one(i, j):
        cols = pl.ds(0, ones[i].shape[2])
        src = r.give.at[lax.rem(j, 2), :, cols]
        return copy_to(src, ones[i].at[j], r.one_send.at[i, j], r.one_recv.at[i, j], dp=d ^ 1)

    def halves(i, k):
        size = ones[i].shape[2] // 2
        return pl.ds((k // 2) * size, size)

    def stage_two(i, k):
        src = ones[i].at[pairs_o[k][1]].at[:, halves(i, k)]
        return copy_to(src, twos[i].at[k], r.stw_send.at[i, k], r.stw_recv.at[i, k], dp=d ^ pairs_o[k][2])

    def stage_three(i, k):
        j = (2 * (1 - y) + x, 2 * y + 1 - x)[k]
        src = ones[i].at[j].at[:, halves(i, 2 * k)]
        return copy_to(src, threes[i].at[k], r.sth_send.at[i, k], r.sth_recv.at[i, k], dp=d ^ (4, 2)[k])

    def start_three(i):
        for k in range(2):
            stage_two(i, 2 * k + 1).wait_recv()
            j = (2 * (1 - y) + x, 2 * y + 1 - x)[k]
            piece = ones[i].at[j].at[:, halves(i, 2 * k)]
            piece[...] = (piece[...].astype(F32) + twos[i][2 * k + 1].astype(F32)).astype(BF)
            stage_three(i, k).start()

    def final_half(i, k):
        stage_two(i, 2 * k).wait_recv()
        stage_three(i, k).wait_recv()
        total = ones[i].at[2 * y + x].at[:, halves(i, 2 * k)][...].astype(F32)
        return total + twos[i][2 * k].astype(F32) + threes[i][k].astype(F32)

    def dp_start(i, terms):
        def give(j, carry):
            @pl.when(j >= 2)
            def _():
                stage_one(i, j - 2).wait_send()

            for cols, value in terms(2 * j + 1 - core):
                r.give[lax.rem(j, 2), :, cols] = value.astype(BF)
            stage_one(i, j).start()
            return carry

        def keep(j, carry):
            stage_one(i, j).wait_recv()
            for cols, value in terms(2 * j + core):
                piece = ones[i].at[j].at[:, cols]
                piece[...] = (piece[...].astype(F32) + value).astype(BF)
            return carry

        lax.fori_loop(0, 4, give, 0)
        lax.fori_loop(0, 4, keep, 0)
        for j in (2, 3):
            stage_one(i, j).wait_send()
        for k in (1, 3, 0, 2):
            stage_two(i, k).start()

    loads["mixed"].wait()

    def out_terms(c):
        grads = r.bg[:, pl.ds(pl.multiple_of(c * chunk, chunk), chunk)]
        for s in range(n):
            yield slice(s * q_cols, (s + 1) * q_cols), mm_at(grads, r.mixed_b[s])

    dp_start(0, out_terms)

    for name in BACK_INS[3:]:
        if name != "mixed":
            loads[name].wait()
    for k in range(2):
        late_stage(2 * k + 1).wait_recv()
        load_s3[9 + 2 * k].start()
    for k in range(1, n):
        heads_back(k).wait_recv()
    start_ffn_three(2)

    def turn_back(grad, part):
        return (grad * r.cos_b[part, :] - pltpu.roll(grad, HD // 2, 1) * r.sin_b[part, :]).astype(BF)

    for b in range(tokens // BLK - 1, -1, -1):
        for g in range(kv_cols // HD):
            attend_back_block(
                g,
                b,
                r.q_b,
                r.k_b,
                r.v_b,
                r.m_b,
                r.lse_b,
                r.do,
                turn_back,
                r.bias,
                r.dqkv,
                r.dk_acc,
                r.dv_acc,
            )

    def scatter(s, c, to_right):
        k, slot = (0, s - 1) if to_right else (1, n - 2 - s)
        piece = pl.ds(c * part_rows, part_rows)
        return copy_to(
            r.wo.at[s, pl.ds(rows + c * part_rows, part_rows)],
            r.got.at[k, slot, piece],
            r.rs_send.at[k, slot, c],
            r.rs_recv.at[k, slot, c],
            tensor=t + 1 if to_right else t - 1,
        )

    for i in range(n - 1, -1, -1):
        s = order[i]
        here = rows_of(s)
        for first in range(0, width, 512):
            cols = slice(first, first + 512)
            term = mm_bt(r.dqkv[here, :q_cols], r.wq_b[cols, :])
            term = term + mm_bt(r.dqkv[here, q_cols : q_cols + kv_cols], r.wk_b[cols, :])
            term = term + mm_bt(r.dqkv[here, q_cols + kv_cols :], r.wv_b[cols, :])
            if i:
                r.wo[s, rows : 2 * rows, cols] = term.astype(BF)
            else:
                r.mid_b[:, cols] = term
        if i == n - 1:
            for c in range(parts):
                pl.when(t == 0)(lambda: scatter(n - 1, c, True).start())
                pl.when(t == n - 1)(lambda: scatter(0, c, False).start())

    def next_sends(i):
        for c in range(parts):

            @pl.when(t == 0)
            def _():
                scatter(i + 1, c, True).wait_send()
                scatter(i, c, True).start()

            @pl.when(t == n - 1)
            def _():
                scatter(n - 2 - i, c, False).wait_send()
                scatter(n - 1 - i, c, False).start()

    from_left = t * 2 < n - 1

    def pass_on(index, near):
        for c in range(parts):
            piece = pl.ds(c * part_rows, part_rows)
            for to_right in (True, False):
                s = index if to_right else n - 1 - index
                way = 0 if to_right else 1
                has_source = t > 0 if to_right else t < n - 1
                now = from_left == (to_right == near)

                @pl.when(has_source & now & (s > t if to_right else s < t))
                def _():
                    scatter(s, c, to_right).wait_recv()
                    term = r.wo.at[s, pl.ds(rows + c * part_rows, part_rows)]
                    term[...] = (term[...].astype(F32) + r.got[way, index - 1, piece].astype(F32)).astype(BF)
                    scatter(s, c, to_right).start()

    def take_own():
        for to_right in (True, False):
            way = 0 if to_right else 1
            has_source = t > 0 if to_right else t < n - 1
            for index in range(1, n):
                s = index if to_right else n - 1 - index

                @pl.when(has_source & (s == t))
                def _():
                    for c in range(parts):
                        scatter(s, c, to_right).wait_recv()
                    r.mid_b[...] += r.got[way, index - 1].astype(F32)

    for copy in load_x:
        copy.wait()

    def project_terms(c):
        cols = pl.ds(pl.multiple_of(c * chunk, chunk), chunk)
        normed = r.wo[:, 0:rows, cols].reshape(tokens, chunk)
        for first in range(0, all_cols, 512):
            part = slice(first, first + 512)
            yield part, mm_at(normed, r.dqkv[:, part])

    dp_start(1, project_terms)
    start_three(0)
    next_sends(2)
    pass_on(3, True)
    start_three(1)
    next_sends(1)
    pass_on(3, False)
    pass_on(2, True)
    for k in range(1, n):
        heads_back(k).wait_send()

    def out_piece(k):
        s = lax.rem(t + k, n)
        return copy_to(r.mg.at[s], r.zr.at[k - 1], r.z_send.at[k - 1], r.z_recv.at[k - 1], tensor=s)

    per_half = n // 2
    for k in range(2):
        total = final_half(0, k)
        for i in range(per_half):
            s = k * per_half + i
            value = total[:, i * q_cols : (i + 1) * q_cols]
            r.mg[s] = value.astype(BF)

            @pl.when(s == t)
            def _():
                r.out_grad[...] = value

    for k in range(1, n):
        out_piece(k).start()
    mine = pl.ds(pl.multiple_of(d * chunk, chunk), chunk)
    size = all_cols // 2
    gain_terms = jnp.zeros((8, chunk), F32)
    for k in range(2):
        value = final_half(1, k)
        r.project_grad[:, k * size : (k + 1) * size] = value
        weight = r.wq_b[mine, :] if k == 0 else jnp.concatenate([r.wk_b[mine, :], r.wv_b[mine, :]], axis=1)
        gain_terms = gain_terms + lax.dot_general(
            jnp.ones((8, size), F32),
            value * weight.astype(F32),
            (((1,), (1,)), ((), ())),
            precision=lax.Precision.HIGHEST,
            preferred_element_type=F32,
        )
    r.gain_st[8, 0:8, :] = gain_terms
    total = r.gain_st[d, 0:8]
    for mask in range(1, 8):
        gain_along_dp(mask).wait_recv()
        total = total + r.gain_dp[mask - 1]
    r.gain_st[8, 8:16, :] = total

    def gain_along_line(k):
        s = lax.rem(t + k, n)
        return copy_to(r.gain_st.at[8], r.gain_line.at[k - 1], r.gl_send.at[k - 1], r.gl_recv.at[k - 1], tensor=s)

    for k in range(1, n):
        gain_along_line(k).start()
    take_own()
    for first in range(0, rows, 64):
        part = slice(first, first + 64)
        back, unused = norm_back_part(r.mid_b[part, :], r.hid_b[part, :].astype(F32), r.gain_a)
        r.input_grad[part, :] = (r.fi_b[part, :] + back).astype(BF)
    for k in range(1, n):
        out_piece(k).wait_recv()
        r.out_grad[...] += r.zr[k - 1].astype(F32)
    total = r.gain_st[8]
    for k in range(1, n):
        gain_along_line(k).wait_recv()
        total = total + r.gain_line[k - 1]
    r.gain_grad[0:1, :] = total[0:1] / r.gain_a[:, mine].astype(F32)
    r.gain_grad[1:2, :] = jnp.sum(total[8:16], axis=0, keepdims=True)
    for k in range(1, n):
        gain_along_line(k).wait_send()
    for mask in range(1, 8):
        gain_along_dp(mask).wait_send()

    for k in range(1, n):
        out_piece(k).wait_send()
    for k in range(4):
        late_stage(k).wait_send()
    for k in (0, 2):
        late_stage(k).wait_recv()
    for w in range(3):
        for k in range(2):
            ffn_three(w, k).wait()
    for i in range(2):
        for k in range(4):
            stage_two(i, k).wait_send()
        for k in range(2):
            stage_three(i, k).wait_send()
    for s in range(n):
        for to_right in (True, False):
            goes_on = t < n - 1 if to_right else t > 0

            @pl.when(goes_on & (s > t if to_right else s < t) & (is_mid | (s == (t + 1 if to_right else t - 1))))
            def _():
                for c in range(parts):
                    scatter(s, c, to_right).wait_send()


def back_call(n, arrays, gain_a, gain_f, bias, x_all, w_out_all, totals, twos, late):
    rows, width = arrays["hid"].shape
    q_cols, kv_cols = arrays["q"].shape[1], arrays["k"].shape[1]
    all_cols = q_cols + 2 * kv_cols
    tokens = n * rows
    chunk = width // 8
    parts = rows // 64
    any_spec = pl.BlockSpec(memory_space=pl.ANY)
    vmem_spec = pl.BlockSpec(memory_space=pltpu.VMEM)
    dma = pltpu.SemaphoreType.DMA
    shape = jax.ShapeDtypeStruct
    return pl.pallas_call(
        functools.partial(back_kernel, n),
        out_shape=[
            shape((rows, width), BF),
            shape((chunk, all_cols), F32),
            shape((chunk, q_cols), F32),
            shape((8, chunk), F32),
            shape((3, 2, chunk, width // 2), BF),
            shape((4, chunk, width // 2), BF),
        ],
        in_specs=[any_spec] * len(BACK_INS) + [vmem_spec] * 3 + [any_spec] * 5,
        out_specs=[vmem_spec] * 4 + [any_spec] * 2,
        scratch_shapes=[pltpu.VMEM(arrays[name].shape, arrays[name].dtype) for name in BACK_INS]
        + [
            pltpu.VMEM((n, q_cols, width), BF),
            pltpu.VMEM((rows, width), BF),
            pltpu.VMEM((n, rows, q_cols), BF),
            pltpu.VMEM((tokens, q_cols), BF),
            pltpu.VMEM((tokens, all_cols), BF),
            pltpu.VMEM((tokens, kv_cols), F32),
            pltpu.VMEM((tokens, kv_cols), F32),
            pltpu.VMEM((2, n - 1, rows, width), BF),
            pltpu.VMEM((4, chunk, n * q_cols), BF),
            pltpu.VMEM((4, chunk, all_cols), BF),
            pltpu.VMEM((4, chunk, n * q_cols // 2), BF),
            pltpu.VMEM((4, chunk, all_cols // 2), BF),
            pltpu.VMEM((2, chunk, n * q_cols // 2), BF),
            pltpu.VMEM((2, chunk, all_cols // 2), BF),
            pltpu.VMEM((3, 2, chunk, width // 2), BF),
            pltpu.VMEM((2, chunk, n * q_cols), BF),
            pltpu.VMEM((n - 1, chunk, q_cols), BF),
            pltpu.VMEM((9, 16, chunk), F32),
            pltpu.VMEM((7, 8, chunk), F32),
            pltpu.VMEM((n - 1, 16, chunk), F32),
            dma((len(BACK_INS),)),
            dma((n,)),
            dma((n,)),
            dma((2, 3, 2)),
            dma((n - 1,)),
            dma((n - 1,)),
            dma((3, 2)),
            dma((3, 2)),
            dma((2, 4)),
            dma((2, 4)),
            dma((2, 4)),
            dma((2, 4)),
            dma((2, 2)),
            dma((2, 2)),
            dma((n - 1,)),
            dma((n - 1,)),
            dma((2, n - 1, parts)),
            dma((2, n - 1, parts)),
            dma((7,)),
            dma((7,)),
            dma((n - 1,)),
            dma((n - 1,)),
            dma((4,)),
            dma((4,)),
        ],
        compiler_params=pltpu.CompilerParams(
            vmem_limit_bytes=63 * 1024 * 1024, collective_id=3, has_side_effects=True
        ),
        cost_estimate=pl.CostEstimate(flops=1 << 36, bytes_accessed=1 << 26, transcendentals=0),
        name="back",
    )(*[arrays[name] for name in BACK_INS], gain_a, gain_f, bias, x_all, w_out_all, totals, twos, late)


def finish_kernel(tot, two, late, three, proj, out, ig, oo, gate, up, down, wq, wk, wv, wo, ig_out, oo_out):
    def total(w):
        other = two[w, 0] if w < 2 else late[0]
        return tot[w, 0].astype(F32) + other.astype(F32) + three[w, 0].astype(F32)

    down[...] = total(0).T
    gate[...] = total(1)
    up[...] = total(2)
    wo[...] = out[...].T
    ig_out[...] = ig[...]
    oo_out[...] = oo[...]

    @pl.when(pl.program_id(0) == 0)
    def _():
        wq[...] = proj[...]

    @pl.when(pl.program_id(0) == 1)
    def _():
        wk[...] = proj[:, : wk.shape[1]]
        wv[...] = proj[:, wk.shape[1] :]


def finish_call(totals, twos, late, threes, project_grad, out_grad, input_grad, output):
    chunk, half = totals.shape[2:]
    rows, width = input_grad.shape
    all_cols, q_cols = project_grad.shape[1], out_grad.shape[1]
    kv_cols = (all_cols - q_cols) // 2
    shape, spec = jax.ShapeDtypeStruct, pl.BlockSpec
    side = lambda k: (0, k)
    below = lambda k: (k, 0)
    fixed = lambda k: (0, 0)
    return pl.pallas_call(
        finish_kernel,
        grid=(2,),
        in_specs=[
            spec((3, 1, chunk, half), lambda k: (0, 2 * k, 0, 0)),
            spec((2, 1, chunk, half), lambda k: (0, 2 * k, 0, 0)),
            spec((1, chunk, half), lambda k: (2 * k, 0, 0)),
            spec((3, 1, chunk, half), lambda k: (0, k, 0, 0)),
            spec((chunk, all_cols // 2), side),
            spec((chunk, q_cols // 2), side),
            spec((rows, width // 2), side),
            spec((rows, width // 2), side),
        ],
        out_specs=[
            spec((chunk, half), side),
            spec((chunk, half), side),
            spec((half, chunk), below),
            spec((chunk, q_cols), fixed),
            spec((chunk, kv_cols), fixed),
            spec((chunk, kv_cols), fixed),
            spec((q_cols // 2, chunk), below),
            spec((rows, width // 2), side),
            spec((rows, width // 2), side),
        ],
        out_shape=[
            shape((chunk, 2 * half), F32),
            shape((chunk, 2 * half), F32),
            shape((2 * half, chunk), F32),
            shape((chunk, q_cols), F32),
            shape((chunk, kv_cols), F32),
            shape((chunk, kv_cols), F32),
            shape((q_cols, chunk), F32),
            shape((rows, width), BF),
            shape((rows, width), BF),
        ],
        compiler_params=pltpu.CompilerParams(vmem_limit_bytes=VMEM_LIMIT),
        name="finish",
    )(totals, twos, late, threes, project_grad, out_grad, input_grad, output)


def ffn_kernel(
    n,
    own_ref,
    cot_ref,
    wg_hbm,
    wu_hbm,
    wd_hbm,
    h_out,
    gg_out,
    ug_out,
    n_out,
    fb_out,
    fi_out,
    wg_ref,
    wu_ref,
    wd_ref,
    n_buf,
    c_buf,
    st_buf,
    fi_part,
    got,
    fb_acc,
    fi_acc,
    w_sem,
    c_sem,
    st_sem,
    n_sem,
    ag_send,
    ag_recv,
    rs_send,
    rs_recv,
):
    t, d = lax.axis_index("tensor"), lax.axis_index("dp")
    rows, width = own_ref.shape
    units = wg_ref.shape[1]
    tile = min(512, units)
    tiles = units // tile
    parts = rs_send.shape[2]
    part_rows = rows // parts
    order = arrival_order(t, n)
    is_mid = (t > 0) & (t < n - 1)

    def load_weights(j):
        cols = pl.ds(j * tile, tile)
        return [
            pltpu.make_async_copy(wg_hbm.at[:, cols], wg_ref.at[:, cols], w_sem.at[0, j]),
            pltpu.make_async_copy(wu_hbm.at[:, cols], wu_ref.at[:, cols], w_sem.at[1, j]),
            pltpu.make_async_copy(wd_hbm.at[cols, :], wd_ref.at[cols, :], w_sem.at[2, j]),
        ]

    def load_cot(i):
        return pltpu.make_async_copy(cot_ref.at[order[i]], c_buf.at[i % 2], c_sem.at[i % 2])

    def gather(s, to_right, src=None):
        return copy_to(
            n_buf.at[s] if src is None else src,
            n_buf.at[s],
            ag_send.at[0 if to_right else 1, s],
            ag_recv.at[s],
            tensor=t + 1 if to_right else t - 1,
        )

    def keep_rows(i):
        return pltpu.make_async_copy(own_ref if i == 0 else n_buf.at[order[i]], n_out.at[order[i]], n_sem.at[i])

    def scatter(s, c, to_right):
        k, slot = (0, s - 1) if to_right else (1, n - 2 - s)
        piece = pl.ds(c * part_rows, part_rows)
        return copy_to(
            fi_part.at[s, piece],
            got.at[k, slot, piece],
            rs_send.at[k, slot, c],
            rs_recv.at[k, slot, c],
            tensor=t + 1 if to_right else t - 1,
        )

    for copy in load_weights(0):
        copy.start()
    load_cot(0).start()
    group_barrier([], n, d, t)
    pl.when(t < n - 1)(lambda: gather(t, True, own_ref).start())
    pl.when(t > 0)(lambda: gather(t, False, own_ref).start())
    for j in range(1, tiles):
        for copy in load_weights(j):
            copy.start()
    keep_rows(0).start()

    def arrive(i):
        s = order[i]
        gather(s, True).wait_recv()
        pl.when((s < t) & (t < n - 1))(lambda: gather(s, True).start())
        pl.when((s > t) & (t > 0))(lambda: gather(s, False).start())
        keep_rows(i).start()

    def stage_out(i):
        return [
            pltpu.make_async_copy(
                st_buf.at[i % 2, k, :, pl.ds(0, out.shape[2])], out.at[order[i]], st_sem.at[k, i % 2]
            )
            for k, out in enumerate((h_out, gg_out, ug_out, fb_out))
        ]

    for i in range(n):
        s = order[i]
        slot = i % 2
        if i == 1:
            arrive(1)
            if n > 2:
                pl.when(is_mid)(functools.partial(arrive, 2))
        elif i > 1:
            pl.when(jnp.logical_not(is_mid))(functools.partial(arrive, i))
        if i + 1 < n:
            load_cot(i + 1).start()
        load_cot(i).wait()
        if i >= 2:
            for copy in stage_out(i - 2):
                copy.wait()
        x_ref = own_ref if i == 0 else n_buf.at[s]
        fb_acc[...] = jnp.zeros_like(fb_acc)
        fi_acc[...] = jnp.zeros_like(fi_acc)

        def one_tile(j, carry):
            if i == 0:
                for copy in load_weights(j):
                    copy.wait()
            if 2 <= i < n - 1:
                pl.when(is_mid & (j == tiles // 2))(functools.partial(arrive, i + 1))
            cols = pl.ds(pl.multiple_of(j * tile, tile), tile)
            x = x_ref[...]
            wg, wu, wd = wg_ref[:, cols], wu_ref[:, cols], wd_ref[cols, :]
            gate = mm(x, wg)
            up = mm(x, wu)
            act_grad = mm_bt(c_buf[slot], wd)
            sig = jax.nn.sigmoid(gate)
            silu = gate * sig
            h = (silu * up).astype(BF)
            gg = (act_grad * up * (sig * (1.0 + gate * (1.0 - sig)))).astype(BF)
            ug = (act_grad * silu).astype(BF)
            for k, value in enumerate((h, gg, ug)):
                st_buf[slot, k, :, cols] = value
            for k in range(0, width, 512):
                piece = slice(k, k + 512)
                fb_acc[:, piece] += mm(h, wd_ref[cols, piece])
                fi_acc[:, piece] += mm_bt(gg, wg_ref[piece, cols]) + mm_bt(ug, wu_ref[piece, cols])
            return carry

        lax.fori_loop(0, tiles, one_tile, 0)
        st_buf[slot, 3, :, :width] = fb_acc[...].astype(BF)
        for copy in stage_out(i):
            copy.start()
        if i == 0:
            fi_out[...] = fi_acc[...]
        else:
            fi_part[s] = fi_acc[...].astype(BF)

            @pl.when(t == 0)
            def _():
                for c in range(parts):
                    scatter(i, c, True).start()

            @pl.when(t == n - 1)
            def _():
                for c in range(parts):
                    scatter(n - 1 - i, c, False).start()

    def pass_on(index, c):
        piece = pl.ds(c * part_rows, part_rows)
        for to_right in (True, False):
            s = index if to_right else n - 1 - index
            k = 0 if to_right else 1
            has_source = t > 0 if to_right else t < n - 1
            beyond = s > t if to_right else s < t

            @pl.when(has_source & beyond)
            def _():
                scatter(s, c, to_right).wait_recv()
                total = fi_part[s, piece].astype(F32) + got[k, index - 1, piece].astype(F32)
                fi_part[s, piece] = total.astype(BF)
                scatter(s, c, to_right).start()

            @pl.when(has_source & (s == t))
            def _():
                scatter(s, c, to_right).wait_recv()
                fi_out[piece] += got[k, index - 1, piece].astype(F32)

    for i in range(max(0, n - 2), n):
        for copy in stage_out(i):
            copy.wait()
    for index in range(1, n):
        for c in range(parts):
            pass_on(index, c)
    for i in range(n):
        keep_rows(i).wait()
    for s in range(n):
        for to_right in (True, False):
            goes_on = t < n - 1 if to_right else t > 0

            @pl.when(goes_on & (s <= t if to_right else s >= t))
            def _():
                gather(s, to_right).wait_send()

            @pl.when(goes_on & (s > t if to_right else s < t))
            def _():
                for c in range(parts):
                    scatter(s, c, to_right).wait_send()


def ffn_call(n, own_rows, cot_all, w_gate, w_up, w_down):
    rows, width = own_rows.shape
    units = w_gate.shape[1]
    tile = min(512, units)
    tiles = units // tile
    parts = max(1, rows // 64)
    tall = jax.ShapeDtypeStruct((n, rows, units), BF)
    wide = jax.ShapeDtypeStruct((n, rows, width), BF)
    any_spec = pl.BlockSpec(memory_space=pl.ANY)
    vmem_spec = pl.BlockSpec(memory_space=pltpu.VMEM)
    dma = pltpu.SemaphoreType.DMA
    return pl.pallas_call(
        functools.partial(ffn_kernel, n),
        out_shape=[tall, tall, tall, wide, wide, jax.ShapeDtypeStruct((rows, width), F32)],
        in_specs=[vmem_spec] + [any_spec] * 4,
        out_specs=[any_spec] * 5 + [vmem_spec],
        scratch_shapes=[
            pltpu.VMEM((width, units), BF),
            pltpu.VMEM((width, units), BF),
            pltpu.VMEM((units, width), BF),
            pltpu.VMEM((n, rows, width), BF),
            pltpu.VMEM((2, rows, width), BF),
            pltpu.VMEM((2, 4, rows, max(units, width)), BF),
            pltpu.VMEM((n, rows, width), BF),
            pltpu.VMEM((2, n - 1, rows, width), BF),
            pltpu.VMEM((rows, width), F32),
            pltpu.VMEM((rows, width), F32),
            dma((3, tiles)),
            dma((2,)),
            dma((4, 2)),
            dma((n,)),
            dma((2, n)),
            dma((n,)),
            dma((2, n - 1, parts)),
            dma((2, n - 1, parts)),
        ],
        compiler_params=pltpu.CompilerParams(
            vmem_limit_bytes=63 * 1024 * 1024, collective_id=4, has_side_effects=True
        ),
        cost_estimate=pl.CostEstimate(
            flops=12 * n * rows * width * units, bytes_accessed=6 * width * units, transcendentals=0
        ),
        name="ffn_plain",
    )(own_rows, cot_all, w_gate, w_up, w_down)


MID_NAMES = (
    ("own", "cot_in", "wg_h", "wu_h", "wd_h", "middle_h"),
    ("cot", "h_out", "tot", "two", "late", "fi_out", "output"),
    ("wg", "wu", "wd", "n_buf", "gu", "h_st", "c_buf", "part", "land", "acc"),
    ("w_sem", "own_sem", "c_sem", "h_sem", "re_sem", "tot_sem", "out_sem", "ready"),
    ("ag_send", "ag_recv", "ct_send", "ct_recv", "rs_send", "rs_recv"),
    ("one_send", "one_recv", "two_send", "two_recv", "late_sem"),
)


def middle_kernel(n, *refs):
    names = [name for group in MID_NAMES for name in group]
    r = types.SimpleNamespace(**dict(zip(names, refs, strict=True)))
    t, d = lax.axis_index("tensor"), lax.axis_index("dp")
    rows, width = r.own.shape
    units = r.wg.shape[1]
    tokens = n * rows
    tile = 512
    tiles = units // tile
    parts = r.rs_send.shape[3]
    part_rows = rows // parts
    order = arrival_order(t, n)
    is_mid = (t > 0) & (t < n - 1)
    is_end = jnp.logical_not(is_mid)
    core, x, y = lax.rem(d, 2), lax.rem(d // 2, 2), d // 4
    chunk = width // 8
    halves = units // 2

    def load_weights(j):
        cols = pl.ds(j * tile, tile)
        return [
            pltpu.make_async_copy(r.wg_h.at[:, cols], r.wg.at[:, cols], r.w_sem.at[0, j]),
            pltpu.make_async_copy(r.wu_h.at[:, cols], r.wu.at[:, cols], r.w_sem.at[1, j]),
            pltpu.make_async_copy(r.wd_h.at[cols, :], r.wd.at[cols, :], r.w_sem.at[2, j]),
        ]

    def line(buf, send_sem, recv_sem, s, to_right, src=None):
        return copy_to(
            buf.at[s] if src is None else src,
            buf.at[s],
            send_sem.at[0 if to_right else 1, s],
            recv_sem.at[s],
            tensor=t + 1 if to_right else t - 1,
        )

    gather = functools.partial(line, r.n_buf, r.ag_send, r.ag_recv)
    gather_cot = functools.partial(line, r.cot, r.ct_send, r.ct_recv)
    own_rows = pltpu.make_async_copy(r.own, r.n_buf.at[t], r.own_sem.at[0])

    def load_cot(i):
        return pltpu.make_async_copy(r.cot.at[order[i]], r.c_buf.at[i % 2], r.c_sem.at[i % 2])

    def keep_h(i):
        return pltpu.make_async_copy(r.h_st, r.h_out.at[order[i]], r.h_sem.at[0])

    def scatter(q, s, c, to_right):
        k, index = (0, s - 1) if to_right else (1, n - 2 - s)
        piece = pl.ds(c * part_rows, part_rows)
        to = t + 1 if to_right else t - 1
        slot = s if to_right else jnp.where(to == s, n, s)
        return copy_to(
            r.part.at[q, s, piece],
            r.land.at[q, slot, piece],
            r.rs_send.at[q, k, index, c],
            r.rs_recv.at[q, k, index, c],
            tensor=to,
        )

    own_rows.start()
    for copy in load_weights(0):
        copy.start()
    load_cot(0).start()
    group_barrier([1, 2, 4], n, d, t)
    own_rows.wait()
    pl.when(t < n - 1)(lambda: gather(t, True).start())
    pl.when(t > 0)(lambda: gather(t, False).start())
    for j in range(1, tiles):
        for copy in load_weights(j):
            copy.start()

    def arrive(which, i):
        s = order[i]
        which(s, True).wait_recv()
        pl.when((s < t) & (t < n - 1))(lambda: which(s, True).start())
        pl.when((s > t) & (t > 0))(lambda: which(s, False).start())

    def end_sends(q, i, chunks):
        @pl.when(t == 0)
        def _():
            for c in chunks:
                scatter(q, i, c, True).start()

        @pl.when(t == n - 1)
        def _():
            for c in chunks:
                scatter(q, n - 1 - i, c, False).start()

    def forward(i):
        s = order[i]
        if i:
            keep_h(i - 1).wait()
        r.acc[...] = jnp.zeros_like(r.acc)

        def one_tile(j, carry):
            if i == 0:
                for copy in load_weights(j):
                    copy.wait()
            if 2 <= i < n - 1:
                pl.when(is_mid & (j == tiles // 2))(functools.partial(arrive, gather, i + 1))
            cols = pl.ds(pl.multiple_of(j * tile, tile), tile)
            rows_in = r.n_buf[s]
            gate = mm(rows_in, r.wg[:, cols])
            up = mm(rows_in, r.wu[:, cols])
            sig = jax.nn.sigmoid(gate)
            silu = gate * sig
            h = (silu * up).astype(BF)
            r.h_st[:, cols] = h
            r.gu[0, s, :, cols] = (up * (sig * (1.0 + gate * (1.0 - sig)))).astype(BF)
            r.gu[1, s, :, cols] = silu.astype(BF)
            for k in range(0, width, 512):
                piece = slice(k, k + 512)
                r.acc[:, piece] += mm(h, r.wd[cols, piece])
            return carry

        lax.fori_loop(0, tiles, one_tile, 0)
        keep_h(i).start()
        r.part[0, s] = r.acc[...].astype(BF)
        if i:
            end_sends(0, i, range(parts))

    def backward(i, chunks):
        s = order[i]
        r.acc[...] = jnp.zeros_like(r.acc)
        load_cot(i).wait()

        def one_tile(j, carry):
            cols = pl.ds(pl.multiple_of(j * tile, tile), tile)
            act_grad = mm_bt(r.c_buf[i % 2], r.wd[cols, :])
            gg = (act_grad * r.gu[0, s, :, cols].astype(F32)).astype(BF)
            ug = (act_grad * r.gu[1, s, :, cols].astype(F32)).astype(BF)
            r.gu[0, s, :, cols] = gg
            r.gu[1, s, :, cols] = ug
            for k in range(0, width, 512):
                piece = slice(k, k + 512)
                r.acc[:, piece] += mm_bt(gg, r.wg[piece, cols]) + mm_bt(ug, r.wu[piece, cols])
            return carry

        lax.fori_loop(0, tiles, one_tile, 0)
        r.part[1, s] = r.acc[...].astype(BF)
        if i:
            end_sends(1, i, chunks)

    from_left = t * 2 < n - 1

    def pass_on(q, index, near):
        for c in range(parts):
            piece = pl.ds(c * part_rows, part_rows)
            for to_right in (True, False):
                s = index if to_right else n - 1 - index
                has_source = t > 0 if to_right else t < n - 1
                now = from_left == (to_right == near)

                @pl.when(has_source & now & (s > t if to_right else s < t))
                def _():
                    scatter(q, s, c, to_right).wait_recv()
                    total = r.part[q, s, piece].astype(F32) + r.land[q, s, piece].astype(F32)
                    r.part[q, s, piece] = total.astype(BF)
                    scatter(q, s, c, to_right).start()

    everything = range(parts)
    forward(0)
    load_cot(1).start()
    backward(0, everything)
    arrive(gather, 1)
    pl.when(is_mid)(functools.partial(arrive, gather, 2))
    pl.when(is_mid)(lambda: load_cot(2).start())
    forward(1)
    backward(1, everything)
    pl.when(is_end)(functools.partial(arrive, gather, 2))
    forward(2)
    @pl.when(is_mid)
    def _():
        gather_cot(t - 1, True).start()
        gather_cot(t + 1, False).start()

    pl.when(is_mid)(functools.partial(backward, 2, everything))
    pl.when(is_end)(functools.partial(arrive, gather, 3))
    forward(3)

    @pl.when(is_end)
    def _():
        arrive(gather_cot, 2)
        load_cot(2).start()
        backward(2, everything)

    arrive(gather_cot, 3)
    load_cot(3).start()
    backward(3, (0, 1))
    keep_h(3).wait()

    first, second = pl.ds(0, tokens), pl.ds(tokens, tokens)
    reload = []
    for k, (src, dst, base) in enumerate(((r.h_out, r.wg, 0), (r.cot, r.wu, tokens))):
        for s in range(n):
            place = dst.at[pl.ds(base + s * rows, rows)]
            reload.append(pltpu.make_async_copy(src.at[s], place, r.re_sem.at[k, s]))
    for copy in reload:
        copy.start()
    pl.semaphore_signal(r.ready, inc=1, device_id={"dp": d ^ 1}, device_id_type=pl.DeviceIdType.MESH)
    pl.semaphore_wait(r.ready, 1)

    def block(w, j):
        if w == 2:
            return r.wg.at[pl.ds(tokens + j * chunk, chunk)]
        return r.wd.at[pl.ds((w * 4 + j) * chunk, chunk)]

    def lhs(w, j, who):
        cols = pl.ds(pl.multiple_of((2 * j + who) * chunk, chunk), chunk)
        if w == 0:
            return r.wu[second, cols]
        return r.n_buf[:, :, cols].reshape(tokens, chunk)

    def rhs(w, part):
        if w == 0:
            return r.wg[first, part]
        return r.gu[w - 1, :, :, part].reshape(tokens, part.stop - part.start)

    def stage_one(w, j):
        return copy_to(r.c_buf.at[lax.rem(j, 2)], block(w, j), r.one_send.at[w, j], r.one_recv.at[w, j], dp=d ^ 1)

    def stage_two(w, k):
        j = (2 * y + 1 - x, 2 * (1 - y) + 1 - x, 2 * (1 - y) + x, 2 * (1 - y) + 1 - x)[k]
        cols = pl.ds((k // 2) * halves, halves)
        return copy_to(
            block(w, j).at[:, cols], r.two.at[w, k], r.two_send.at[w, k], r.two_recv.at[w, k], dp=d ^ (2, 2, 4, 4)[k]
        )

    def keep_late(k):
        j = (2 * y + 1 - x, 2 * (1 - y) + 1 - x, 2 * (1 - y) + x, 2 * (1 - y) + 1 - x)[k]
        cols = pl.ds((k // 2) * halves, halves)
        return pltpu.make_async_copy(block(2, j).at[:, cols], r.late.at[k], r.late_sem.at[k])

    def keep_total(w, k):
        j = (2 * y + x, 2 * (1 - y) + x, 2 * y + x, 2 * y + 1 - x)[k]
        cols = pl.ds((k // 2) * halves, halves)
        return pltpu.make_async_copy(block(w, j).at[:, cols], r.tot.at[w, k], r.tot_sem.at[w, k])

    for w in range(3):
        if w == 0:
            for copy in reload:
                copy.wait()

        def give(j, carry):
            @pl.when(j >= 2)
            def _():
                stage_one(w, j - 2).wait_send()

            grads = lhs(w, j, 1 - core)
            for k in range(0, units, 512):
                part = slice(k, k + 512)
                r.c_buf[lax.rem(j, 2), :, part] = mm_at(grads, rhs(w, part)).astype(BF)
            stage_one(w, j).start()
            return carry

        def keep(j, carry):
            stage_one(w, j).wait_recv()
            grads = lhs(w, j, core)
            for k in range(0, units, 512):
                part = slice(k, k + 512)
                piece = block(w, j).at[:, part]
                piece[...] = (piece[...].astype(F32) + mm_at(grads, rhs(w, part))).astype(BF)
            return carry

        lax.fori_loop(0, 4, give, 0)
        if w == 0:
            end_sends(1, 3, (2,))
        lax.fori_loop(0, 4, keep, 0)
        if w == 0:
            end_sends(1, 3, (3,))
        for j in (2, 3):
            stage_one(w, j).wait_send()
        for k in range(4):
            if w < 2:
                stage_two(w, k).start()
            else:
                keep_late(k).start()
            keep_total(w, k).start()
        if w == 0:
            pass_on(0, 2, True)
    pass_on(0, 3, True)
    pass_on(0, 3, False)
    pass_on(1, 2, True)
    pass_on(1, 3, True)
    pass_on(1, 3, False)

    def total_of(q):
        r.acc[...] += r.part[q, t].astype(F32)
        for to_right in (True, False):
            has_source = t > 0 if to_right else t < n - 1

            @pl.when(has_source)
            def _():
                for s in range(n):

                    @pl.when(s == t)
                    def _():
                        for c in range(parts):
                            scatter(q, s, c, to_right).wait_recv()

                slot = t if to_right else n
                r.acc[...] += r.land[q, slot].astype(F32)

    add_middle = pltpu.make_async_copy(r.middle_h, r.acc, r.out_sem.at[0])
    add_middle.start()
    add_middle.wait()
    total_of(0)
    r.h_st[...] = r.acc[...].astype(BF)
    keep_output = pltpu.make_async_copy(r.h_st, r.output, r.out_sem.at[0])
    keep_output.start()
    r.acc[...] = jnp.zeros_like(r.acc)
    total_of(1)
    keep_fi = pltpu.make_async_copy(r.acc, r.fi_out, r.out_sem.at[1])
    keep_fi.start()
    keep_output.wait()
    keep_fi.wait()

    for w in range(3):
        for k in range(4):
            keep_total(w, k).wait()
            if w < 2:
                stage_two(w, k).wait()
            else:
                keep_late(k).wait()
    for s in range(n):
        for to_right in (True, False):
            goes_on = t < n - 1 if to_right else t > 0

            @pl.when(goes_on & (s <= t if to_right else s >= t))
            def _():
                gather(s, to_right).wait_send()

            @pl.when(goes_on & (s < t if to_right else s > t))
            def _():
                gather_cot(s, to_right).wait_send()

            @pl.when(goes_on & (s > t if to_right else s < t))
            def _():
                for q in range(2):
                    for c in range(parts):
                        scatter(q, s, c, to_right).wait_send()


def middle_call(n, own_rows, cot_part, w_gate, w_up, w_down, middle):
    rows, width = own_rows.shape
    units = w_gate.shape[1]
    parts = rows // 64
    shape = jax.ShapeDtypeStruct
    wide = shape((n, rows, width), BF)
    piece = (4, width // 8, units // 2)
    any_spec = pl.BlockSpec(memory_space=pl.ANY)
    dma = pltpu.SemaphoreType.DMA
    return pl.pallas_call(
        functools.partial(middle_kernel, n),
        out_shape=[wide, shape((n, rows, units), BF), shape((3, *piece), BF), shape((2, *piece), BF), shape(piece, BF)]
        + [shape((rows, width), F32), shape((rows, width), BF)],
        in_specs=[any_spec] * 6,
        out_specs=[any_spec] * 7,
        input_output_aliases={1: 0},
        scratch_shapes=[
            pltpu.VMEM((width, units), BF),
            pltpu.VMEM((width, units), BF),
            pltpu.VMEM((units, width), BF),
            pltpu.VMEM((n, rows, width), BF),
            pltpu.VMEM((2, n, rows, units), BF),
            pltpu.VMEM((rows, units), BF),
            pltpu.VMEM((2, rows, width), BF),
            pltpu.VMEM((2, n, rows, width), BF),
            pltpu.VMEM((2, n + 1, rows, width), BF),
            pltpu.VMEM((rows, width), F32),
            dma((3, units // 512)),
            dma((1,)),
            dma((2,)),
            dma((1,)),
            dma((2, n)),
            dma((3, 4)),
            dma((2,)),
            pltpu.SemaphoreType.REGULAR,
            dma((2, n)),
            dma((n,)),
            dma((2, n)),
            dma((n,)),
            dma((2, 2, n - 1, parts)),
            dma((2, 2, n - 1, parts)),
            dma((3, 4)),
            dma((3, 4)),
            dma((3, 4)),
            dma((3, 4)),
            dma((4,)),
        ],
        compiler_params=pltpu.CompilerParams(
            vmem_limit_bytes=64 * 1024 * 1024 - 65536, collective_id=1, has_side_effects=True
        ),
        cost_estimate=pl.CostEstimate(
            flops=18 * n * rows * width * units, bytes_accessed=6 * width * units, transcendentals=0
        ),
        name="middle",
    )(own_rows, cot_part, w_gate, w_up, w_down, middle)


def full_call(kernel, out_shapes, args, scratch=(), flops=0, name=None):
    spec = pl.BlockSpec(memory_space=pltpu.VMEM)
    return pl.pallas_call(
        kernel,
        out_shape=out_shapes,
        in_specs=[spec] * len(args),
        out_specs=[spec] * len(out_shapes),
        scratch_shapes=list(scratch),
        compiler_params=pltpu.CompilerParams(vmem_limit_bytes=VMEM_LIMIT),
        cost_estimate=pl.CostEstimate(flops=flops, bytes_accessed=flops // 400, transcendentals=0),
        name=name,
    )(*args)


def normalize(rows_wide, gain_wide):
    inverse = lax.rsqrt(jnp.mean(rows_wide * rows_wide, axis=-1, keepdims=True) + NORM_EPS)
    scaled_rows = rows_wide * inverse
    return scaled_rows, inverse, (scaled_rows * gain_wide).astype(BF)


def norm_back(normed_grad, scaled_rows, inverse, gain_wide):
    weighted = normed_grad * gain_wide
    return inverse * (weighted - scaled_rows * jnp.mean(weighted * scaled_rows, axis=-1, keepdims=True))


def pairs(n, bit):
    return [(i, i ^ bit) for i in range(n)]


def pick(array, index, axis):
    return lax.dynamic_index_in_dim(array, index, axis, keepdims=False)


def dp_scatter(give, keep, n_dp):
    me = lax.axis_index("dp")
    total = keep + lax.ppermute(give, "dp", pairs(n_dp, 1))
    if n_dp != 8:
        bit = 2
        while total.shape[0] > 1:
            parts = total.reshape(-1, 2, *total.shape[1:])
            mine = (me // bit) % 2
            total = pick(parts, mine, 1) + lax.ppermute(pick(parts, 1 - mine, 1), "dp", pairs(n_dp, bit))
            bit *= 2
        return total[0].astype(F32)
    x, y = (me // 2) % 2, me // 4
    cols = total.shape[-1] // 2
    parts = total.reshape(2, 2, *total.shape[1:])
    a, b = parts[..., :cols], parts[..., cols:]
    got_a = lax.ppermute(pick(a, 1 - x, 1), "dp", pairs(n_dp, 2))
    got_b = lax.ppermute(pick(b, 1 - y, 0), "dp", pairs(n_dp, 4))
    a = pick(a, x, 1) + got_a
    b = pick(b, y, 0) + got_b
    got_a = lax.ppermute(pick(a, 1 - y, 0), "dp", pairs(n_dp, 4))
    got_b = lax.ppermute(pick(b, 1 - x, 0), "dp", pairs(n_dp, 2))
    a = pick(a, y, 0).astype(F32) + got_a.astype(F32)
    b = pick(b, x, 0).astype(F32) + got_b.astype(F32)
    return jnp.concatenate([a, b], axis=-1)


def core_split(rows, n_dp):
    tokens, width = rows.shape
    core = lax.axis_index("dp") % 2
    parts = rows.reshape(tokens, n_dp // 2, 2, width // n_dp)
    return [pick(parts, c, 2).reshape(tokens, width // 2) for c in (1 - core, core)]


def grad_scatter(split_rows, cols, n_dp):
    give, keep = [
        mm_at(part, cols).astype(BF).reshape(n_dp // 2, 2 * part.shape[1] // n_dp, cols.shape[1])
        for part in split_rows
    ]
    return dp_scatter(give, keep, n_dp)


def after(value, *others):
    return lax.optimization_barrier((value, *others))[0]


def shards(n_dp, n_t, hidden_in, gain_attn, w_query, w_key, w_value, w_out, gain_ffn, w_gate, w_up, w_down, segments, parents, cotangent):
    tokens = segments.shape[0]
    own, width = hidden_in.shape
    q_cols, kv_cols, units = w_query.shape[1], w_key.shape[1], w_gate.shape[1]
    heads = q_cols // HD
    me_t = lax.axis_index("tensor")
    me_dp = lax.axis_index("dp")
    gain_attn_wide = gain_attn.astype(F32)
    gain_ffn_wide = gain_ffn.astype(F32)

    def ring(value, shift):
        return lax.ppermute(value, "tensor", [(i, (i + shift) % n_t) for i in range(n_t)])

    ancestry, depth = tree_tables(segments, parents)
    cosine, sine = rope_tables(depth)
    bias = jnp.where(jnp.repeat(ancestry, BLK, axis=1) > 0.5, 0.0, NEG)
    fused = n_dp == 8 and n_t == 4 and units == width and q_cols == 2 * own and tokens * 2 == width
    x_all, cot_all, w_out_all, queries, keys, values, mixed, lse, mixed_own, middle, normed_ffn = attn_call(
        n_dp, n_t, fused, hidden_in, cotangent, gain_attn[None], gain_ffn[None], w_query, w_key, w_value, w_out, cosine, sine, bias
    )
    x_all = x_all.reshape(tokens, width)
    w_out_all = w_out_all.reshape(n_t * q_cols, width)
    rows_wide = hidden_in.astype(F32)
    if fused:
        unused_cot, unused_h, totals, twos, late, ffn_in_grad, output = middle_call(
            n_t, normed_ffn, cot_all, w_gate, w_up, w_down, middle
        )
        arrays = dict(
            fi=ffn_in_grad,
            mid=middle,
            cot=cotangent,
            hid=hidden_in,
            q=queries,
            k=keys,
            v=values,
            m=mixed,
            lse=lse,
            cos=cosine,
            sin=sine,
            mixed=mixed_own,
            wq=w_query,
            wk=w_key,
            wv=w_value,
        )
        input_grad, project_wgrad, out_grad, gain_grads, threes, late_twos = back_call(
            n_t,
            arrays,
            gain_attn[None],
            gain_ffn[None],
            bias,
            x_all.reshape(n_t, own, width),
            w_out_all.reshape(n_t, q_cols, width),
            totals,
            twos,
            late,
        )
        w_gate_grad, w_up_grad, w_down_grad, w_query_grad, w_key_grad, w_value_grad, w_out_grad, input_grad, output = (
            finish_call(totals, twos, late_twos, threes, project_wgrad, out_grad, input_grad, output)
        )
        gain_attn_grad, gain_ffn_grad = gain_grads[0], gain_grads[1]
    else:
        w_project = jnp.concatenate([w_query, w_key, w_value], axis=1)
        h_all, gg_all, ug_all, n_all, fb_part, ffn_in_grad = ffn_call(n_t, normed_ffn, cot_all, w_gate, w_up, w_down)
        fb_sum = lax.psum_scatter(fb_part.reshape(tokens, width), "tensor", scatter_dimension=0, tiled=True)
        output = (middle + fb_sum.astype(F32)).astype(BF)
        h_all, gg_all, ug_all = [a.reshape(tokens, units) for a in (h_all, gg_all, ug_all)]
        cot_split = core_split(cot_all.reshape(tokens, width), n_dp)
        normed_split = core_split(n_all.reshape(tokens, width), n_dp)
        w_down_grad = grad_scatter(cot_split, h_all, n_dp).T
        w_gate_grad = grad_scatter(normed_split, gg_all, n_dp)
        w_up_grad = grad_scatter(normed_split, ug_all, n_dp)

        scaled_attn, inverse_attn, _ = normalize(rows_wide, gain_attn_wide)
        scaled_ffn, inverse_ffn, _ = normalize(middle, gain_ffn_wide)
        middle_grad = cotangent.astype(F32) + norm_back(ffn_in_grad, scaled_ffn, inverse_ffn, gain_ffn_wide)
        branch_grad = middle_grad.astype(BF)
        mixed_grads = mm_bt(branch_grad, w_out_all).astype(BF).reshape(own, n_t, q_cols)
        mixed_grads = [pick(mixed_grads, (me_t + n_t - d) % n_t, 1) for d in range(n_t)]
        mixed_grads = [mixed_grads[0]] + [ring(mixed_grads[d], n_t - d) for d in range(1, n_t)]
        mixed_grad = jnp.roll(jnp.concatenate(mixed_grads, axis=0), me_t * own, axis=0)

        (project_grad,) = full_call(
            attn_bwd_kernel,
            [jax.ShapeDtypeStruct((tokens, q_cols + 2 * kv_cols), BF)],
            (queries, keys, values, mixed, lse, mixed_grad, cosine, sine, bias),
            scratch=[pltpu.VMEM((tokens, kv_cols), F32)] * 2,
            flops=10 * heads * tokens * tokens * HD,
            name="attn_bwd",
        )
        dq, dk, dv = (
            project_grad[:, :q_cols],
            project_grad[:, q_cols : q_cols + kv_cols],
            project_grad[:, q_cols + kv_cols :],
        )
        attn_in_part = mm_bt(project_grad, w_project).astype(BF)
        attn_in_grad = lax.psum_scatter(attn_in_part, "tensor", scatter_dimension=0, tiled=True).astype(F32)

        mixed_wide = jnp.moveaxis(mixed_own, 0, 1).reshape(own, n_t * q_cols)
        out_grad = grad_scatter(core_split(branch_grad, n_dp), mixed_wide, n_dp)
        out_parts = out_grad.reshape(-1, n_t, q_cols)
        w_out_grad = pick(out_parts, me_t, 1)
        for d in range(1, n_t):
            piece = pick(out_parts, (me_t + d) % n_t, 1).astype(BF)
            w_out_grad = w_out_grad + ring(piece, d).astype(F32)
        w_out_grad = w_out_grad.T

        project_wgrad = grad_scatter(core_split(x_all, n_dp), project_grad, n_dp)
        w_query_grad = project_wgrad[:, :q_cols]
        w_key_grad = project_wgrad[:, q_cols : q_cols + kv_cols]
        w_value_grad = project_wgrad[:, q_cols + kv_cols :]

        input_grad = (middle_grad + norm_back(attn_in_grad, scaled_attn, inverse_attn, gain_attn_wide)).astype(BF)

        def own_rows(array):
            return lax.dynamic_slice_in_dim(array, me_dp * (width // n_dp), width // n_dp, 0).astype(F32)

        gain_sums = jnp.stack(
            [
                jnp.sum(own_rows(w_project) * project_wgrad, axis=1),
                jnp.sum(own_rows(w_gate) * w_gate_grad, axis=1) + jnp.sum(own_rows(w_up) * w_up_grad, axis=1),
            ]
        )
        bit = 1
        while bit < n_t:
            gain_sums = gain_sums + lax.ppermute(gain_sums, "tensor", pairs(n_t, bit))
            bit *= 2
        gain_attn_grad = gain_sums[0] / own_rows(gain_attn)
        gain_ffn_grad = gain_sums[1] / own_rows(gain_ffn)

    return (
        output,
        input_grad,
        gain_attn_grad,
        w_query_grad,
        w_key_grad,
        w_value_grad,
        w_out_grad,
        gain_ffn_grad,
        w_gate_grad,
        w_up_grad,
        w_down_grad,
    )


def solution(mesh):
    return jax.shard_map(
        functools.partial(shards, mesh.shape["dp"], mesh.shape["tensor"]),
        mesh=mesh,
        in_specs=(
            P(("dp", "tensor"), None),
            P(),
            P(None, "tensor"),
            P(None, "tensor"),
            P(None, "tensor"),
            P("tensor", None),
            P(),
            P(None, "tensor"),
            P(None, "tensor"),
            P("tensor", None),
            P("dp"),
            P("dp"),
            P(("dp", "tensor"), None),
        ),
        out_specs=(
            P(("dp", "tensor"), None),
            P(("dp", "tensor"), None),
            P("dp"),
            P("dp", "tensor"),
            P("dp", "tensor"),
            P("dp", "tensor"),
            P("tensor", "dp"),
            P("dp"),
            P("dp", "tensor"),
            P("dp", "tensor"),
            P("tensor", "dp"),
        ),
        check_vma=False,
    )
```

```python
import functools
import math
import types

import jax
import jax.numpy as jnp
from jax import lax
from jax.experimental import pallas as pl
from jax.experimental.pallas import tpu as pltpu
from jax.sharding import PartitionSpec as P

HD = 128
BLK = 128
NORM_EPS = 1e-05
ROPE_BASE = 1000000.0
SCALE = HD ** (-0.5)
SCALE2 = SCALE * math.log2(math.e)
NEG = -1e30
BF = jnp.bfloat16
F32 = jnp.float32
VMEM_LIMIT = 56 * 1024 * 1024


def mm(a, b):
    return jnp.dot(a, b, preferred_element_type=F32)


def mm_bt(a, b):
    return lax.dot_general(a, b, (((1,), (1,)), ((), ())), preferred_element_type=F32)


def mm_at(a, b):
    return lax.dot_general(a, b, (((0,), (0,)), ((), ())), preferred_element_type=F32)


def tree_tables(segment_ids, parent_ids):
    block_count = parent_ids.shape[0]
    first_ids = segment_ids.reshape(block_count, -1)[:, 0]
    block_iota = jnp.arange(block_count, dtype=jnp.int32)
    same_tree = first_ids[:, None] == first_ids[None, :]
    tree_start = jnp.min(jnp.where(same_tree, block_iota[None, :], block_count), axis=1)
    parent_block = tree_start + parent_ids
    step = (block_iota[None, :] == parent_block[:, None]) | (
        block_iota[None, :] == block_iota[:, None]
    )
    for _ in range(3):
        step = jnp.any(step[:, :, None] & step[None, :, :], axis=1)
    ancestry = step.astype(F32)
    return ancestry, jnp.sum(ancestry, axis=1) - 1.0


def rope_tables(depth):
    token_total = depth.shape[0] * BLK
    offsets = (jnp.arange(token_total, dtype=jnp.int32) % BLK).astype(F32)
    places = jnp.repeat(depth, BLK) * BLK + offsets
    freq_index = jnp.arange(HD // 2, dtype=jnp.int32).astype(F32)
    inverse_freq = ROPE_BASE ** (-2.0 * freq_index / HD)
    angles = places[:, None] * inverse_freq[None, :]
    cosine, sine = jnp.cos(angles), jnp.sin(angles)
    return jnp.concatenate([cosine, cosine], axis=1), jnp.concatenate([-sine, sine], axis=1)


def head_cols(h):
    return slice(h * HD, (h + 1) * HD)


def causal_tile(rep):
    rows = lax.broadcasted_iota(jnp.int32, (BLK, BLK), 0)
    cols = lax.broadcasted_iota(jnp.int32, (BLK, BLK), 1)
    tile = cols <= rows
    return jnp.concatenate([tile] * rep, axis=0) if rep > 1 else tile


def stack_heads(ref, rows, first, rep):
    parts = [ref[rows, head_cols(first + i)] for i in range(rep)]
    return jnp.concatenate(parts, axis=0) if rep > 1 else parts[0]


def attend_block(b, q_ref, k_ref, v_ref, bias_ref, m_ref, lse_ref, causal, rep):
    rows = slice(b * BLK, (b + 1) * BLK)
    past = slice(0, b * BLK)
    for g in range(k_ref.shape[1] // HD):
        q = stack_heads(q_ref, rows, g * rep, rep)
        s_diag = jnp.where(causal, mm_bt(q, k_ref[rows, head_cols(g)]) * SCALE2, NEG)
        top = jnp.max(s_diag, axis=1, keepdims=True)
        if b:
            s_past = mm_bt(q, k_ref[past, head_cols(g)]) * SCALE2 + bias_ref[b : b + 1, past]
            top = jnp.maximum(top, jnp.max(s_past, axis=1, keepdims=True))
        e_diag = jnp.exp2(s_diag - top)
        mass = jnp.sum(e_diag, axis=1, keepdims=True)
        out = mm(e_diag.astype(BF), v_ref[rows, head_cols(g)])
        if b:
            e_past = jnp.exp2(s_past - top)
            mass = mass + jnp.sum(e_past, axis=1, keepdims=True)
            out = out + mm(e_past.astype(BF), v_ref[past, head_cols(g)])
        out = (out / mass).astype(BF)
        lse = top + jnp.log2(mass)
        for i in range(rep):
            h = g * rep + i
            m_ref[rows, head_cols(h)] = out[i * BLK : (i + 1) * BLK]
            lse_ref[rows, h : h + 1] = lse[i * BLK : (i + 1) * BLK]


def copy_to(src, dst, send_sem, recv_sem, **where):
    return pltpu.make_async_remote_copy(
        src_ref=src,
        dst_ref=dst,
        send_sem=send_sem,
        recv_sem=recv_sem,
        device_id=where,
        device_id_type=pl.DeviceIdType.MESH,
    )


def group_barrier(masks, n, d, t):
    barrier = pltpu.get_barrier_semaphore()
    for k in range(1, n):
        pl.semaphore_signal(
            barrier, inc=1, device_id={"tensor": lax.rem(t + k, n)}, device_id_type=pl.DeviceIdType.MESH
        )
    for mask in masks:
        pl.semaphore_signal(barrier, inc=1, device_id={"dp": d ^ mask}, device_id_type=pl.DeviceIdType.MESH)
    pl.semaphore_wait(barrier, n - 1 + len(masks))


def attn_kernel(
    n_dp,
    n,
    one_hop,
    hidden_ref,
    cot_ref,
    gain_a_ref,
    gain_f_ref,
    wq_hbm,
    wk_hbm,
    wv_hbm,
    wo_hbm,
    cos_ref,
    sin_ref,
    bias_ref,
    x_out,
    cot_out,
    wo_out,
    q_ref,
    k_ref,
    v_ref,
    m_ref,
    lse_ref,
    mixed_ref,
    middle_ref,
    normed_ref,
    own_buf,
    x_buf,
    wq_ref,
    wk_ref,
    wv_ref,
    wo_ref,
    w_sem,
    x_sem,
    misc_sem,
    ag_send,
    ag_recv,
    cot_send,
    cot_recv,
    wz_send,
    wz_recv,
    wp_send,
    wp_recv,
    wc_send,
    wc_recv,
    m_send,
    m_recv,
):
    t, d = lax.axis_index("tensor"), lax.axis_index("dp")
    rows, width = hidden_ref.shape
    q_cols = wq_ref.shape[1]
    heads, kv_heads = q_cols // HD, wk_ref.shape[1] // HD
    rep = heads // kv_heads
    share = q_cols // n_dp
    half = q_cols // 2
    order = arrival_order(t, n)
    is_mid = (t > 0) & (t < n - 1)
    core, plane = lax.rem(d, 2), d // 2
    masks = list(range(2, n_dp, 2))

    load_w = [
        pltpu.make_async_copy(src, dst, w_sem.at[i])
        for i, (src, dst) in enumerate(((wq_hbm, wq_ref), (wk_hbm, wk_ref), (wv_hbm, wv_ref)))
    ]
    own_wo = pltpu.make_async_copy(wo_hbm, wo_ref.at[t], misc_sem.at[0])
    own_cot = pltpu.make_async_copy(cot_ref, cot_out.at[t], misc_sem.at[1])
    for copy in load_w:
        copy.start()
    own_wo.start()
    own_cot.start()

    def norm(values, gain_ref):
        inverse = lax.rsqrt(jnp.mean(values * values, axis=-1, keepdims=True) + NORM_EPS)
        return (values * inverse * gain_ref[...].astype(F32)).astype(BF)

    for r in range(0, rows, 64):
        part = slice(r, r + 64)
        own_buf[part, :] = norm(hidden_ref[part, :].astype(F32), gain_a_ref)
    group_barrier([1, *masks], n, d, t)

    def line_copy(buf, send_sem, recv_sem, s, to_right, src=None):
        return copy_to(
            buf.at[s] if src is None else src,
            buf.at[s],
            send_sem.at[0 if to_right else 1, s],
            recv_sem.at[s],
            tensor=t + 1 if to_right else t - 1,
        )

    gather_x = functools.partial(line_copy, x_buf, ag_send, ag_recv)
    gather_cot = functools.partial(line_copy, cot_out, cot_send, cot_recv)

    def first_hop(gather, src):
        pl.when(t < n - 1)(lambda: gather(t, True, src).start())
        pl.when(t > 0)(lambda: gather(t, False, src).start())

    def arrive(gather, i):
        s = order[i]
        gather(s, True).wait_recv()
        pl.when((s < t) & (t < n - 1))(lambda: gather(s, True).start())
        pl.when((s > t) & (t > 0))(lambda: gather(s, False).start())

    def keep_rows(i):
        return pltpu.make_async_copy(own_buf if i == 0 else x_buf.at[order[i]], x_out.at[order[i]], x_sem.at[i])

    my_rows = pl.ds(pl.multiple_of(core * half + plane * share, 16), share)
    my_half = pl.ds(pl.multiple_of(core * half, 16), half)

    def wo_line(k):
        return copy_to(
            wo_hbm.at[my_rows],
            wo_ref.at[t, my_rows],
            wz_send.at[k - 1],
            wz_recv.at[k - 1],
            tensor=lax.rem(t + k, n),
        )

    def wo_plane(k, j):
        s = lax.rem(t + n - k, n)
        return copy_to(
            wo_ref.at[s, my_rows],
            wo_ref.at[s, my_rows],
            wp_send.at[k - 1, j],
            wp_recv.at[k - 1, j],
            dp=d ^ masks[j],
        )

    def wo_core(k):
        s = lax.rem(t + n - k, n)
        return copy_to(
            wo_ref.at[s, my_half], wo_ref.at[s, my_half], wc_send.at[k - 1], wc_recv.at[k - 1], dp=d ^ 1
        )

    first_hop(gather_x, own_buf)
    for k in range(1, n):
        wo_line(k).start()
    keep_rows(0).start()

    for copy in load_w:
        copy.wait()
    for i in range(n):
        s = order[i]
        if i == 1:
            arrive(gather_x, 1)
            if n > 2:
                pl.when(is_mid)(lambda: arrive(gather_x, 2))
        elif i > 1:
            if i > 2:
                arrive(gather_x, i)
            else:
                pl.when(jnp.logical_not(is_mid))(lambda: arrive(gather_x, 2))
        if i:
            keep_rows(i).start()
        x = own_buf[...] if i == 0 else x_buf[s]
        here = pl.ds(pl.multiple_of(s * rows, rows), rows)
        cosine, sine = cos_ref[here, :], sin_ref[here, :]
        for w_ref, out_ref, count in ((wq_ref, q_ref, heads), (wk_ref, k_ref, kv_heads)):
            raw = mm(x, w_ref[...])
            for h in range(count):
                u = raw[:, head_cols(h)]
                out_ref[here, head_cols(h)] = (u * cosine + pltpu.roll(u, HD // 2, 1) * sine).astype(BF)
        v_ref[here, :] = mm(x, wv_ref[...]).astype(BF)
        if i == 1:
            for k in range(1, n):
                wo_line(k).wait_recv()
                for j in range(len(masks)):
                    wo_plane(k, j).start()
        if i == n - 1:
            first_hop(gather_cot, cot_ref)
            for k in range(1, n):
                for j in range(len(masks)):
                    wo_plane(k, j).wait_recv()
                wo_core(k).start()

    def heads_to(r):
        here = pl.ds(r * rows, rows)
        return copy_to(m_ref.at[here], mixed_ref.at[t], m_send.at[r], m_recv.at[t], tensor=r)

    causal = causal_tile(rep)
    for b in range(n * rows // BLK):
        attend_block(b, q_ref, k_ref, v_ref, bias_ref, m_ref, lse_ref, causal, rep)
        if (b + 1) * BLK % rows == 0:
            r = (b + 1) * BLK // rows - 1
            pl.when(t != r)(lambda: heads_to(r).start())

            @pl.when(t == r)
            def _():
                mixed_ref[r] = m_ref[r * rows : (r + 1) * rows, :]

    if n > 2 and not one_hop:

        @pl.when(is_mid)
        def _():
            arrive(gather_cot, 1)
            arrive(gather_cot, 2)

    own_wo.wait()
    for k in range(1, n):
        s = lax.rem(t + n - k, n)
        copy_to(m_ref.at[pl.ds(0, rows)], mixed_ref.at[s], m_send.at[0], m_recv.at[s], tensor=s).wait_recv()
        wo_core(k).wait_recv()
    keep_wo = pltpu.make_async_copy(wo_ref, wo_out, misc_sem.at[0])
    keep_wo.start()
    for r in range(0, rows, 128):
        part = slice(r, r + 128)
        total = hidden_ref[part, :].astype(F32)
        for s in range(n):
            total = total + mm(mixed_ref[s, part, :], wo_ref[s])
        middle_ref[part, :] = total
        normed_ref[part, :] = norm(total, gain_f_ref)

    if one_hop:
        pl.when(t > 0)(lambda: gather_cot(t - 1, True).wait_recv())
        pl.when(t < n - 1)(lambda: gather_cot(t + 1, False).wait_recv())
    else:
        for i in range(1, n):
            if i > 2:
                arrive(gather_cot, i)
            else:
                pl.when(jnp.logical_not(is_mid))(functools.partial(arrive, gather_cot, i))
    own_cot.wait()
    keep_wo.wait()
    for i in range(n):
        keep_rows(i).wait()
    for k in range(1, n):
        wo_line(k).wait_send()
        wo_core(k).wait_send()
        for j in range(len(masks)):
            wo_plane(k, j).wait_send()
    if one_hop:
        pl.when(t < n - 1)(lambda: gather_cot(t, True).wait_send())
        pl.when(t > 0)(lambda: gather_cot(t, False).wait_send())
    for s in range(n):
        pl.when(t != s)(lambda: heads_to(s).wait_send())
        for to_right in (True, False):
            goes_on = t < n - 1 if to_right else t > 0

            @pl.when(goes_on & (s <= t if to_right else s >= t))
            def _():
                gather_x(s, to_right).wait_send()
                if not one_hop:
                    gather_cot(s, to_right).wait_send()


def attn_call(n_dp, n, one_hop, hidden, cot, gain_a, gain_f, wq, wk, wv, wo, cosine, sine, bias):
    rows, width = hidden.shape
    q_cols, kv_cols = wq.shape[1], wk.shape[1]
    tokens = n * rows
    any_spec = pl.BlockSpec(memory_space=pl.ANY)
    vmem_spec = pl.BlockSpec(memory_space=pltpu.VMEM)
    dma = pltpu.SemaphoreType.DMA
    masks = n_dp // 2 - 1
    shape = jax.ShapeDtypeStruct
    return pl.pallas_call(
        functools.partial(attn_kernel, n_dp, n, one_hop),
        out_shape=[
            shape((n, rows, width), BF),
            shape((n, rows, width), BF),
            shape((n, q_cols, width), BF),
            shape((tokens, q_cols), BF),
            shape((tokens, kv_cols), BF),
            shape((tokens, kv_cols), BF),
            shape((tokens, q_cols), BF),
            shape((tokens, HD), F32),
            shape((n, rows, q_cols), BF),
            shape((rows, width), F32),
            shape((rows, width), BF),
        ],
        in_specs=[vmem_spec, any_spec, vmem_spec, vmem_spec] + [any_spec] * 4 + [vmem_spec] * 3,
        out_specs=[any_spec] * 3 + [vmem_spec] * 8,
        scratch_shapes=[
            pltpu.VMEM((rows, width), BF),
            pltpu.VMEM((n, rows, width), BF),
            pltpu.VMEM((width, q_cols), BF),
            pltpu.VMEM((width, kv_cols), BF),
            pltpu.VMEM((width, kv_cols), BF),
            pltpu.VMEM((n, q_cols, width), BF),
            dma((3,)),
            dma((n,)),
            dma((2,)),
            dma((2, n)),
            dma((n,)),
            dma((2, n)),
            dma((n,)),
            dma((n - 1,)),
            dma((n - 1,)),
            dma((n - 1, masks)),
            dma((n - 1, masks)),
            dma((n - 1,)),
            dma((n - 1,)),
            dma((n,)),
            dma((n,)),
        ],
        compiler_params=pltpu.CompilerParams(
            vmem_limit_bytes=VMEM_LIMIT, collective_id=2, has_side_effects=True
        ),
        cost_estimate=pl.CostEstimate(
            flops=2 * tokens * width * (q_cols + 2 * kv_cols), bytes_accessed=1 << 25, transcendentals=0
        ),
        name="attn",
    )(hidden, cot, gain_a, gain_f, wq, wk, wv, wo, cosine, sine, bias)


def arrival_order(t, n):
    near = jnp.minimum(t, n - 1 - t)
    order = [t]
    for i in range(1, n):
        both = t - (i + 1) // 2 if i % 2 else t + i // 2
        one_side = jnp.where(t > n - 1 - t, t - (i - near), t + (i - near))
        order.append(jnp.where(i <= 2 * near, both, one_side))
    return order


def attend_back_block(g, b, q_ref, k_ref, v_ref, o_ref, lse_ref, do_ref, turn_back, bias_ref, d_ref, dk_acc, dv_acc):
    heads, kv_heads = q_ref.shape[1] // HD, k_ref.shape[1] // HD
    rep = heads // kv_heads
    last = q_ref.shape[0] // BLK - 1
    causal = causal_tile(rep)
    rows = slice(b * BLK, (b + 1) * BLK)
    q = stack_heads(q_ref, rows, g * rep, rep)
    do = stack_heads(do_ref, rows, g * rep, rep)
    o = stack_heads(o_ref, rows, g * rep, rep)
    lse = [lse_ref[rows, h : h + 1] for h in range(g * rep, (g + 1) * rep)]
    lse = jnp.concatenate(lse, axis=0) if rep > 1 else lse[0]
    delta = jnp.sum(do.astype(F32) * o.astype(F32), axis=1, keepdims=True)
    k_d = k_ref[rows, head_cols(g)]
    p = jnp.where(causal, jnp.exp2(mm_bt(q, k_d) * SCALE2 - lse), 0.0)
    ds = (p * (mm_bt(do, v_ref[rows, head_cols(g)]) - delta)).astype(BF)
    dq = mm(ds, k_d)
    dk = mm_at(ds, q)
    dv = mm_at(p.astype(BF), do)
    if b < last:
        dk = dk + dk_acc[rows, head_cols(g)]
        dv = dv + dv_acc[rows, head_cols(g)]
    d_ref[rows, head_cols(heads + g)] = turn_back(dk * SCALE, rows)
    d_ref[rows, head_cols(heads + kv_heads + g)] = dv.astype(BF)
    if b:
        past = slice(0, b * BLK)
        k_p = k_ref[past, head_cols(g)]
        p = jnp.exp2(mm_bt(q, k_p) * SCALE2 + (bias_ref[b : b + 1, past] - lse))
        ds = (p * (mm_bt(do, v_ref[past, head_cols(g)]) - delta)).astype(BF)
        dq = dq + mm(ds, k_p)
        dk = mm_at(ds, q)
        dv = mm_at(p.astype(BF), do)
        if b < last:
            dk = dk + dk_acc[past, head_cols(g)]
            dv = dv + dv_acc[past, head_cols(g)]
        dk_acc[past, head_cols(g)] = dk
        dv_acc[past, head_cols(g)] = dv
    dq = dq * SCALE
    for i in range(rep):
        d_ref[rows, head_cols(g * rep + i)] = turn_back(dq[i * BLK : (i + 1) * BLK], rows)


def attn_bwd_kernel(q_ref, k_ref, v_ref, o_ref, lse_ref, do_ref, cos_ref, sin_ref, bias_ref, d_ref, dk_acc, dv_acc):
    def turn_back(grad, rows):
        return (grad * cos_ref[rows, :] - pltpu.roll(grad, HD // 2, 1) * sin_ref[rows, :]).astype(BF)

    for b in range(q_ref.shape[0] // BLK - 1, -1, -1):
        for g in range(k_ref.shape[1] // HD):
            attend_back_block(
                g, b, q_ref, k_ref, v_ref, o_ref, lse_ref, do_ref, turn_back, bias_ref, d_ref, dk_acc, dv_acc
            )


BACK_INS = ("fi", "mid", "cot", "hid", "q", "k", "v", "m", "lse", "cos", "sin", "mixed", "wq", "wk", "wv")
BACK_NAMES = (
    BACK_INS,
    ("gain_a", "gain_f", "bias", "x_h", "wo_h", "tot_h", "two_h", "late_h", "far_h"),
    ("input_grad", "project_grad", "out_grad", "gain_grad", "three_h", "late_two", "far_add"),
    tuple(name + "_b" for name in BACK_INS),
    ("wo", "bg", "mg", "do", "dqkv", "dk_acc", "dv_acc", "got", "one_o", "one_p", "two_o", "two_p"),
    ("three_o", "three_p", "s3", "give", "zr", "gain_st", "gain_dp", "gain_line", "far_land"),
    ("in_sem", "wo_sem", "x_sem", "s3_sem", "mg_send", "mg_recv", "th_send", "th_recv", "one_send", "one_recv"),
    ("stw_send", "stw_recv", "sth_send", "sth_recv", "z_send", "z_recv", "rs_send", "rs_recv"),
    ("gd_send", "gd_recv", "gl_send", "gl_recv", "lt_send", "lt_recv"),
    ("late_sem", "far_sem", "far_send", "far_recv"),
)


def back_kernel(n, *refs):
    names = [name for group in BACK_NAMES for name in group]
    r = types.SimpleNamespace(**dict(zip(names, refs, strict=True)))
    t, d = lax.axis_index("tensor"), lax.axis_index("dp")
    rows, width = r.bg.shape
    q_cols, kv_cols = r.q_b.shape[1], r.k_b.shape[1]
    all_cols = q_cols + 2 * kv_cols
    tokens = n * rows
    core, x, y = lax.rem(d, 2), lax.rem(d // 2, 2), d // 4
    chunk = width // 8
    parts = r.rs_send.shape[2]
    part_rows = rows // parts
    order = arrival_order(t, n)
    is_mid = (t > 0) & (t < n - 1)
    from_left = t * 2 < n - 1
    pairs_o = [(2 * y + x, 2 * y + 1 - x, 2), (2 * (1 - y) + x, 2 * (1 - y) + 1 - x, 2)]
    pairs_o += [(2 * y + x, 2 * (1 - y) + x, 4), (2 * y + 1 - x, 2 * (1 - y) + 1 - x, 4)]

    loads = {
        name: pltpu.make_async_copy(getattr(r, name), getattr(r, name + "_b"), r.in_sem.at[i])
        for i, name in enumerate(BACK_INS)
    }
    load_wo = [pltpu.make_async_copy(r.wo_h.at[s], r.wo.at[s], r.wo_sem.at[s]) for s in range(n)]
    load_x = [pltpu.make_async_copy(r.x_h.at[s], r.wo.at[s, pl.ds(0, rows)], r.x_sem.at[s]) for s in range(n)]
    half = r.s3.shape[3]
    load_tot, load_two = {}, {}
    for w in range(3):
        for k in range(2):
            load_tot[w, k] = [pltpu.make_async_copy(r.tot_h.at[w, 2 * k + 1], r.s3.at[w, k], r.s3_sem.at[0, w, k])]
            if w < 2:
                landing = r.wo.at[w, pl.ds(rows, rows), pl.ds(k * half, half)]
                load_two[w, k] = [pltpu.make_async_copy(r.two_h.at[w, 2 * k + 1], landing, r.s3_sem.at[1, w, k])]
            else:
                load_two[w, k] = [
                    pltpu.make_async_copy(
                        r.late_two.at[2 * k + 1, :, pl.ds(i * q_cols, q_cols)], r.mg.at[2 * k + i], r.late_sem.at[k, i]
                    )
                    for i in range(2)
                ]

    def late_stage(i):
        k = i if i < 4 else 2 * (i - 4)
        src, dst = r.late_h.at[i], r.late_two.at[i]
        return copy_to(src, dst, r.lt_send.at[i], r.lt_recv.at[i], dp=d ^ (2, 2, 4, 4)[k])

    def far_copy(i, c, src=None):
        piece = pl.ds(c * part_rows, part_rows)
        return copy_to(
            r.far_land.at[piece] if src is None else src.at[i, piece],
            r.far_land.at[piece],
            r.far_send.at[i, c],
            r.far_recv.at[i, c],
            tensor=t + 1 if i else t - 1,
        )

    load_far = pltpu.make_async_copy(r.far_h.at[jnp.where(from_left, 0, 1)], r.bg, r.far_sem.at[0])
    for name in ("fi", "mid", "cot"):
        loads[name].start()
    for copy in load_wo:
        copy.start()
    for name in BACK_INS[3:]:
        loads[name].start()
    for w in range(3):
        for k in range(2):
            load_tot[w, k][0].start()
    group_barrier(range(1, 8), n, d, t)
    for k in (1, 3, 0, 2):
        late_stage(k).start()

    for name in ("fi", "mid", "cot"):
        loads[name].wait()

    def norm_back_part(grad, values, gain_ref):
        inverse = lax.rsqrt(jnp.mean(values * values, axis=-1, keepdims=True) + NORM_EPS)
        scaled = values * inverse
        weighted = grad * gain_ref[...].astype(F32)
        back = inverse * (weighted - scaled * jnp.mean(weighted * scaled, axis=-1, keepdims=True))
        return back, grad * scaled

    def gain_along_dp(mask):
        return copy_to(
            r.gain_st.at[d ^ mask, pl.ds(0, 8)],
            r.gain_dp.at[mask - 1],
            r.gd_send.at[mask - 1],
            r.gd_recv.at[mask - 1],
            dp=d ^ mask,
        )

    gain_sum = jnp.zeros((8, width), F32)
    for first in range(0, rows, 64):
        part = slice(first, first + 64)
        back, gain_part = norm_back_part(r.fi_b[part, :], r.mid_b[part, :], r.gain_f)
        gain_sum = gain_sum + jnp.sum(gain_part.reshape(8, 8, width), axis=0)
        total = r.cot_b[part, :].astype(F32) + back
        r.fi_b[part, :] = total
        r.bg[part, :] = total.astype(BF)
    for c in range(8):
        r.gain_st[c, 0:8, :] = gain_sum[:, c * chunk : (c + 1) * chunk]
    for mask in range(1, 8):
        gain_along_dp(mask).start()

    def rows_of(s):
        return pl.ds(pl.multiple_of(s * rows, rows), rows)

    def heads_back(k):
        s = lax.rem(t + k, n)
        return copy_to(r.mg.at[s], r.do.at[rows_of(t)], r.mg_send.at[k - 1], r.mg_recv.at[k - 1], tensor=s)

    for copy in load_wo:
        copy.wait()
    for k in range(1, n):
        s = lax.rem(t + k, n)
        r.mg[s] = mm_bt(r.bg[...], r.wo[s]).astype(BF)
        heads_back(k).start()
    r.do[rows_of(t), :] = mm_bt(r.bg[...], r.wo[t]).astype(BF)

    for w in range(2):
        for k in range(2):
            load_two[w, k][0].start()
    for copy in load_x:
        copy.start()

    def ffn_three(w, k):
        return copy_to(r.s3.at[w, k], r.three_h.at[w, k], r.th_send.at[w, k], r.th_recv.at[w, k], dp=d ^ (4, 2)[k])

    def start_ffn_three(w):
        for k in range(2):
            for copy in load_tot[w, k] + load_two[w, k]:
                copy.wait()
            if w < 2:
                other = r.wo[w, rows : 2 * rows, k * half : (k + 1) * half]
            else:
                other = jnp.concatenate([r.mg[2 * k], r.mg[2 * k + 1]], axis=1)
            r.s3[w, k] = (r.s3[w, k].astype(F32) + other.astype(F32)).astype(BF)
            ffn_three(w, k).start()

    start_ffn_three(0)
    start_ffn_three(1)

    ones, twos, threes = (r.one_o, r.one_p), (r.two_o, r.two_p), (r.three_o, r.three_p)

    def stage_one(i, j):
        cols = pl.ds(0, ones[i].shape[2])
        src = r.give.at[lax.rem(j, 2), :, cols]
        return copy_to(src, ones[i].at[j], r.one_send.at[i, j], r.one_recv.at[i, j], dp=d ^ 1)

    def halves(i, k):
        size = ones[i].shape[2] // 2
        return pl.ds((k // 2) * size, size)

    def stage_two(i, k):
        src = ones[i].at[pairs_o[k][1]].at[:, halves(i, k)]
        return copy_to(src, twos[i].at[k], r.stw_send.at[i, k], r.stw_recv.at[i, k], dp=d ^ pairs_o[k][2])

    def stage_three(i, k):
        j = (2 * (1 - y) + x, 2 * y + 1 - x)[k]
        src = ones[i].at[j].at[:, halves(i, 2 * k)]
        return copy_to(src, threes[i].at[k], r.sth_send.at[i, k], r.sth_recv.at[i, k], dp=d ^ (4, 2)[k])

    def start_three(i):
        for k in range(2):
            stage_two(i, 2 * k + 1).wait_recv()
            j = (2 * (1 - y) + x, 2 * y + 1 - x)[k]
            piece = ones[i].at[j].at[:, halves(i, 2 * k)]
            piece[...] = (piece[...].astype(F32) + twos[i][2 * k + 1].astype(F32)).astype(BF)
            stage_three(i, k).start()

    def final_half(i, k):
        stage_two(i, 2 * k).wait_recv()
        stage_three(i, k).wait_recv()
        total = ones[i].at[2 * y + x].at[:, halves(i, 2 * k)][...].astype(F32)
        return total + twos[i][2 * k].astype(F32) + threes[i][k].astype(F32)

    def dp_start(i, terms):
        def give(j, carry):
            @pl.when(j >= 2)
            def _():
                stage_one(i, j - 2).wait_send()

            for cols, value in terms(2 * j + 1 - core):
                r.give[lax.rem(j, 2), :, cols] = value.astype(BF)
            stage_one(i, j).start()
            return carry

        def keep(j, carry):
            stage_one(i, j).wait_recv()
            for cols, value in terms(2 * j + core):
                piece = ones[i].at[j].at[:, cols]
                piece[...] = (piece[...].astype(F32) + value).astype(BF)
            return carry

        lax.fori_loop(0, 4, give, 0)
        lax.fori_loop(0, 4, keep, 0)
        for j in (2, 3):
            stage_one(i, j).wait_send()
        for k in (1, 3, 0, 2):
            stage_two(i, k).start()

    loads["mixed"].wait()

    def out_terms(c):
        grads = r.bg[:, pl.ds(pl.multiple_of(c * chunk, chunk), chunk)]
        for s in range(n):
            yield slice(s * q_cols, (s + 1) * q_cols), mm_at(grads, r.mixed_b[s])

    dp_start(0, out_terms)
    load_far.start()

    for name in BACK_INS[3:]:
        if name != "mixed":
            loads[name].wait()
    for k in range(1, n):
        heads_back(k).wait_recv()
    for c in range(parts):
        pl.when(is_mid & from_left)(lambda: far_copy(1, c, r.far_h).start())
        pl.when(is_mid & jnp.logical_not(from_left))(lambda: far_copy(0, c, r.far_h).start())

    def turn_back(grad, part):
        return (grad * r.cos_b[part, :] - pltpu.roll(grad, HD // 2, 1) * r.sin_b[part, :]).astype(BF)

    for b in range(tokens // BLK - 1, -1, -1):
        for g in range(kv_cols // HD):
            attend_back_block(
                g,
                b,
                r.q_b,
                r.k_b,
                r.v_b,
                r.m_b,
                r.lse_b,
                r.do,
                turn_back,
                r.bias,
                r.dqkv,
                r.dk_acc,
                r.dv_acc,
            )

    def scatter(s, c, to_right):
        k, slot = (0, s - 1) if to_right else (1, n - 2 - s)
        piece = pl.ds(c * part_rows, part_rows)
        return copy_to(
            r.wo.at[s, pl.ds(rows + c * part_rows, part_rows)],
            r.got.at[k, slot, piece],
            r.rs_send.at[k, slot, c],
            r.rs_recv.at[k, slot, c],
            tensor=t + 1 if to_right else t - 1,
        )

    for i in range(n - 1, -1, -1):
        s = order[i]
        here = rows_of(s)
        for first in range(0, width, 512):
            cols = slice(first, first + 512)
            term = mm_bt(r.dqkv[here, :q_cols], r.wq_b[cols, :])
            term = term + mm_bt(r.dqkv[here, q_cols : q_cols + kv_cols], r.wk_b[cols, :])
            term = term + mm_bt(r.dqkv[here, q_cols + kv_cols :], r.wv_b[cols, :])
            if i:
                r.wo[s, rows : 2 * rows, cols] = term.astype(BF)
            else:
                r.mid_b[:, cols] = term
        if i == n - 1:
            for c in range(parts):
                pl.when(t == 0)(lambda: scatter(n - 1, c, True).start())
                pl.when(t == n - 1)(lambda: scatter(0, c, False).start())

    def next_sends(i):
        for c in range(parts):

            @pl.when(t == 0)
            def _():
                scatter(i + 1, c, True).wait_send()
                scatter(i, c, True).start()

            @pl.when(t == n - 1)
            def _():
                scatter(n - 2 - i, c, False).wait_send()
                scatter(n - 1 - i, c, False).start()

    def pass_on(index, near):
        for c in range(parts):
            piece = pl.ds(c * part_rows, part_rows)
            for to_right in (True, False):
                s = index if to_right else n - 1 - index
                way = 0 if to_right else 1
                has_source = t > 0 if to_right else t < n - 1
                now = from_left == (to_right == near)

                @pl.when(has_source & now & (s > t if to_right else s < t))
                def _():
                    scatter(s, c, to_right).wait_recv()
                    term = r.wo.at[s, pl.ds(rows + c * part_rows, part_rows)]
                    term[...] = (term[...].astype(F32) + r.got[way, index - 1, piece].astype(F32)).astype(BF)
                    scatter(s, c, to_right).start()

    def take_own():
        for to_right in (True, False):
            way = 0 if to_right else 1
            has_source = t > 0 if to_right else t < n - 1
            for index in range(1, n):
                s = index if to_right else n - 1 - index

                @pl.when(has_source & (s == t))
                def _():
                    for c in range(parts):
                        scatter(s, c, to_right).wait_recv()
                    r.mid_b[...] += r.got[way, index - 1].astype(F32)

    for copy in load_x:
        copy.wait()

    def project_terms(c):
        cols = pl.ds(pl.multiple_of(c * chunk, chunk), chunk)
        normed = r.wo[:, 0:rows, cols].reshape(tokens, chunk)
        for first in range(0, all_cols, 512):
            part = slice(first, first + 512)
            yield part, mm_at(normed, r.dqkv[:, part])

    def far_on():
        for i in range(2):
            for c in range(parts):
                piece = pl.ds(c * part_rows, part_rows)

                @pl.when(is_mid & (from_left == (i == 0)))
                def _():
                    far_copy(i, c).wait_recv()
                    total = r.far_land[piece].astype(F32) + r.bg[piece].astype(F32)
                    r.far_land[piece] = total.astype(BF)
                    far_copy(i, c).start()

    for k in range(1, n):
        heads_back(k).wait_send()
    for k in range(2):
        late_stage(2 * k + 1).wait_recv()
        for copy in load_two[2, k]:
            copy.start()
    dp_start(1, project_terms)
    start_ffn_three(2)
    start_three(0)
    load_far.wait()
    next_sends(2)
    pass_on(3, True)
    start_three(1)
    for i in (4, 5):
        late_stage(i).start()
    far_on()
    next_sends(1)
    pass_on(3, False)
    pass_on(2, True)

    def out_piece(k):
        s = lax.rem(t + k, n)
        return copy_to(r.mg.at[s], r.zr.at[k - 1], r.z_send.at[k - 1], r.z_recv.at[k - 1], tensor=s)

    per_half = n // 2
    for k in range(2):
        total = final_half(0, k)
        for i in range(per_half):
            s = k * per_half + i
            value = total[:, i * q_cols : (i + 1) * q_cols]
            r.mg[s] = value.astype(BF)

            @pl.when(s == t)
            def _():
                r.out_grad[...] = value

    for k in range(1, n):
        out_piece(k).start()
    mine = pl.ds(pl.multiple_of(d * chunk, chunk), chunk)
    size = all_cols // 2
    gain_terms = jnp.zeros((8, chunk), F32)
    for k in range(2):
        value = final_half(1, k)
        r.project_grad[:, k * size : (k + 1) * size] = value
        weight = r.wq_b[mine, :] if k == 0 else jnp.concatenate([r.wk_b[mine, :], r.wv_b[mine, :]], axis=1)
        gain_terms = gain_terms + lax.dot_general(
            jnp.ones((8, size), F32),
            value * weight.astype(F32),
            (((1,), (1,)), ((), ())),
            precision=lax.Precision.HIGHEST,
            preferred_element_type=F32,
        )
    r.gain_st[8, 0:8, :] = gain_terms
    total = r.gain_st[d, 0:8]
    for mask in range(1, 8):
        gain_along_dp(mask).wait_recv()
        total = total + r.gain_dp[mask - 1]
    r.gain_st[8, 8:16, :] = total

    def gain_along_line(k):
        s = lax.rem(t + k, n)
        return copy_to(r.gain_st.at[8], r.gain_line.at[k - 1], r.gl_send.at[k - 1], r.gl_recv.at[k - 1], tensor=s)

    for k in range(1, n):
        gain_along_line(k).start()
    take_own()
    for first in range(0, rows, 64):
        part = slice(first, first + 64)
        back, unused = norm_back_part(r.mid_b[part, :], r.hid_b[part, :].astype(F32), r.gain_a)
        r.input_grad[part, :] = (r.fi_b[part, :] + back).astype(BF)
    for k in range(1, n):
        out_piece(k).wait_recv()
        r.out_grad[...] += r.zr[k - 1].astype(F32)
    total = r.gain_st[8]
    for k in range(1, n):
        gain_along_line(k).wait_recv()
        total = total + r.gain_line[k - 1]
    r.gain_grad[0:1, :] = total[0:1] / r.gain_a[:, mine].astype(F32)
    r.gain_grad[1:2, :] = jnp.sum(total[8:16], axis=0, keepdims=True)
    for k in range(1, n):
        gain_along_line(k).wait_send()
    for mask in range(1, 8):
        gain_along_dp(mask).wait_send()

    for k in range(1, n):
        out_piece(k).wait_send()
    for i in range(6):
        late_stage(i).wait_send()
    for i in (0, 2, 4, 5):
        late_stage(i).wait_recv()
    for i, last in ((0, 0), (1, n - 1)):

        @pl.when(t == last)
        def _():
            for c in range(parts):
                far_copy(i, c).wait_recv()

        @pl.when(is_mid)
        def _():
            for c in range(parts):
                far_copy(i, c).wait_send()

    @pl.when(is_mid)
    def _():
        r.far_land[...] = jnp.zeros_like(r.far_land)

    keep_far = pltpu.make_async_copy(r.far_land, r.far_add, r.far_sem.at[0])
    keep_far.start()
    keep_far.wait()
    for w in range(3):
        for k in range(2):
            ffn_three(w, k).wait()
    for i in range(2):
        for k in range(4):
            stage_two(i, k).wait_send()
        for k in range(2):
            stage_three(i, k).wait_send()
    for s in range(n):
        for to_right in (True, False):
            goes_on = t < n - 1 if to_right else t > 0

            @pl.when(goes_on & (s > t if to_right else s < t) & (is_mid | (s == (t + 1 if to_right else t - 1))))
            def _():
                for c in range(parts):
                    scatter(s, c, to_right).wait_send()


def back_call(n, arrays, gain_a, gain_f, bias, x_all, w_out_all, totals, twos, late, far):
    rows, width = arrays["hid"].shape
    q_cols, kv_cols = arrays["q"].shape[1], arrays["k"].shape[1]
    all_cols = q_cols + 2 * kv_cols
    tokens = n * rows
    chunk = width // 8
    parts = rows // 64
    any_spec = pl.BlockSpec(memory_space=pl.ANY)
    vmem_spec = pl.BlockSpec(memory_space=pltpu.VMEM)
    dma = pltpu.SemaphoreType.DMA
    shape = jax.ShapeDtypeStruct
    return pl.pallas_call(
        functools.partial(back_kernel, n),
        out_shape=[
            shape((rows, width), BF),
            shape((chunk, all_cols), F32),
            shape((chunk, q_cols), F32),
            shape((8, chunk), F32),
            shape((3, 2, chunk, width // 2), BF),
            shape((6, chunk, width // 2), BF),
            shape((rows, width), BF),
        ],
        in_specs=[any_spec] * len(BACK_INS) + [vmem_spec] * 3 + [any_spec] * 6,
        out_specs=[vmem_spec] * 4 + [any_spec] * 3,
        scratch_shapes=[pltpu.VMEM(arrays[name].shape, arrays[name].dtype) for name in BACK_INS]
        + [
            pltpu.VMEM((n, q_cols, width), BF),
            pltpu.VMEM((rows, width), BF),
            pltpu.VMEM((n, rows, q_cols), BF),
            pltpu.VMEM((tokens, q_cols), BF),
            pltpu.VMEM((tokens, all_cols), BF),
            pltpu.VMEM((tokens, kv_cols), F32),
            pltpu.VMEM((tokens, kv_cols), F32),
            pltpu.VMEM((2, n - 1, rows, width), BF),
            pltpu.VMEM((4, chunk, n * q_cols), BF),
            pltpu.VMEM((4, chunk, all_cols), BF),
            pltpu.VMEM((4, chunk, n * q_cols // 2), BF),
            pltpu.VMEM((4, chunk, all_cols // 2), BF),
            pltpu.VMEM((2, chunk, n * q_cols // 2), BF),
            pltpu.VMEM((2, chunk, all_cols // 2), BF),
            pltpu.VMEM((3, 2, chunk, width // 2), BF),
            pltpu.VMEM((2, chunk, n * q_cols), BF),
            pltpu.VMEM((n - 1, chunk, q_cols), BF),
            pltpu.VMEM((9, 16, chunk), F32),
            pltpu.VMEM((7, 8, chunk), F32),
            pltpu.VMEM((n - 1, 16, chunk), F32),
            pltpu.VMEM((rows, width), BF),
            dma((len(BACK_INS),)),
            dma((n,)),
            dma((n,)),
            dma((2, 3, 2)),
            dma((n - 1,)),
            dma((n - 1,)),
            dma((3, 2)),
            dma((3, 2)),
            dma((2, 4)),
            dma((2, 4)),
            dma((2, 4)),
            dma((2, 4)),
            dma((2, 2)),
            dma((2, 2)),
            dma((n - 1,)),
            dma((n - 1,)),
            dma((2, n - 1, parts)),
            dma((2, n - 1, parts)),
            dma((7,)),
            dma((7,)),
            dma((n - 1,)),
            dma((n - 1,)),
            dma((6,)),
            dma((6,)),
            dma((2, 2)),
            dma((1,)),
            dma((2, parts)),
            dma((2, parts)),
        ],
        compiler_params=pltpu.CompilerParams(
            vmem_limit_bytes=64 * 1024 * 1024 - 65536, collective_id=3, has_side_effects=True
        ),
        cost_estimate=pl.CostEstimate(flops=1 << 36, bytes_accessed=1 << 26, transcendentals=0),
        name="back",
    )(*[arrays[name] for name in BACK_INS], gain_a, gain_f, bias, x_all, w_out_all, totals, twos, late, far)


def finish_kernel(tot, two, near, late, three, proj, out, ig, base, far, gate, up, down, wq, wk, wv, wo, ig_out, oo_out):
    def total(w):
        other = (two[0, 0], near[0], late[0])[w]
        return tot[w, 0].astype(F32) + other.astype(F32) + three[w, 0].astype(F32)

    down[...] = total(0).T
    gate[...] = total(1)
    up[...] = total(2)
    wo[...] = out[...].T
    ig_out[...] = ig[...]
    oo_out[...] = (base[...] + far[...].astype(F32)).astype(BF)

    @pl.when(pl.program_id(0) == 0)
    def _():
        wq[...] = proj[...]

    @pl.when(pl.program_id(0) == 1)
    def _():
        wk[...] = proj[:, : wk.shape[1]]
        wv[...] = proj[:, wk.shape[1] :]


def finish_call(totals, twos, late, threes, project_grad, out_grad, input_grad, base, far):
    chunk, half = totals.shape[2:]
    rows, width = input_grad.shape
    all_cols, q_cols = project_grad.shape[1], out_grad.shape[1]
    kv_cols = (all_cols - q_cols) // 2
    shape, spec = jax.ShapeDtypeStruct, pl.BlockSpec
    side = lambda k: (0, k)
    below = lambda k: (k, 0)
    fixed = lambda k: (0, 0)
    return pl.pallas_call(
        finish_kernel,
        grid=(2,),
        in_specs=[
            spec((3, 1, chunk, half), lambda k: (0, 2 * k, 0, 0)),
            spec((1, 1, chunk, half), lambda k: (0, 2 * k, 0, 0)),
            spec((1, chunk, half), lambda k: (4 + k, 0, 0)),
            spec((1, chunk, half), lambda k: (2 * k, 0, 0)),
            spec((3, 1, chunk, half), lambda k: (0, k, 0, 0)),
            spec((chunk, all_cols // 2), side),
            spec((chunk, q_cols // 2), side),
            spec((rows, width // 2), side),
            spec((rows, width // 2), side),
            spec((rows, width // 2), side),
        ],
        out_specs=[
            spec((chunk, half), side),
            spec((chunk, half), side),
            spec((half, chunk), below),
            spec((chunk, q_cols), fixed),
            spec((chunk, kv_cols), fixed),
            spec((chunk, kv_cols), fixed),
            spec((q_cols // 2, chunk), below),
            spec((rows, width // 2), side),
            spec((rows, width // 2), side),
        ],
        out_shape=[
            shape((chunk, 2 * half), F32),
            shape((chunk, 2 * half), F32),
            shape((2 * half, chunk), F32),
            shape((chunk, q_cols), F32),
            shape((chunk, kv_cols), F32),
            shape((chunk, kv_cols), F32),
            shape((q_cols, chunk), F32),
            shape((rows, width), BF),
            shape((rows, width), BF),
        ],
        compiler_params=pltpu.CompilerParams(vmem_limit_bytes=VMEM_LIMIT),
        name="finish",
    )(totals, twos, late, late, threes, project_grad, out_grad, input_grad, base, far)


def ffn_kernel(
    n,
    own_ref,
    cot_ref,
    wg_hbm,
    wu_hbm,
    wd_hbm,
    h_out,
    gg_out,
    ug_out,
    n_out,
    fb_out,
    fi_out,
    wg_ref,
    wu_ref,
    wd_ref,
    n_buf,
    c_buf,
    st_buf,
    fi_part,
    got,
    fb_acc,
    fi_acc,
    w_sem,
    c_sem,
    st_sem,
    n_sem,
    ag_send,
    ag_recv,
    rs_send,
    rs_recv,
):
    t, d = lax.axis_index("tensor"), lax.axis_index("dp")
    rows, width = own_ref.shape
    units = wg_ref.shape[1]
    tile = min(512, units)
    tiles = units // tile
    parts = rs_send.shape[2]
    part_rows = rows // parts
    order = arrival_order(t, n)
    is_mid = (t > 0) & (t < n - 1)

    def load_weights(j):
        cols = pl.ds(j * tile, tile)
        return [
            pltpu.make_async_copy(wg_hbm.at[:, cols], wg_ref.at[:, cols], w_sem.at[0, j]),
            pltpu.make_async_copy(wu_hbm.at[:, cols], wu_ref.at[:, cols], w_sem.at[1, j]),
            pltpu.make_async_copy(wd_hbm.at[cols, :], wd_ref.at[cols, :], w_sem.at[2, j]),
        ]

    def load_cot(i):
        return pltpu.make_async_copy(cot_ref.at[order[i]], c_buf.at[i % 2], c_sem.at[i % 2])

    def gather(s, to_right, src=None):
        return copy_to(
            n_buf.at[s] if src is None else src,
            n_buf.at[s],
            ag_send.at[0 if to_right else 1, s],
            ag_recv.at[s],
            tensor=t + 1 if to_right else t - 1,
        )

    def keep_rows(i):
        return pltpu.make_async_copy(own_ref if i == 0 else n_buf.at[order[i]], n_out.at[order[i]], n_sem.at[i])

    def scatter(s, c, to_right):
        k, slot = (0, s - 1) if to_right else (1, n - 2 - s)
        piece = pl.ds(c * part_rows, part_rows)
        return copy_to(
            fi_part.at[s, piece],
            got.at[k, slot, piece],
            rs_send.at[k, slot, c],
            rs_recv.at[k, slot, c],
            tensor=t + 1 if to_right else t - 1,
        )

    for copy in load_weights(0):
        copy.start()
    load_cot(0).start()
    group_barrier([], n, d, t)
    pl.when(t < n - 1)(lambda: gather(t, True, own_ref).start())
    pl.when(t > 0)(lambda: gather(t, False, own_ref).start())
    for j in range(1, tiles):
        for copy in load_weights(j):
            copy.start()
    keep_rows(0).start()

    def arrive(i):
        s = order[i]
        gather(s, True).wait_recv()
        pl.when((s < t) & (t < n - 1))(lambda: gather(s, True).start())
        pl.when((s > t) & (t > 0))(lambda: gather(s, False).start())
        keep_rows(i).start()

    def stage_out(i):
        return [
            pltpu.make_async_copy(
                st_buf.at[i % 2, k, :, pl.ds(0, out.shape[2])], out.at[order[i]], st_sem.at[k, i % 2]
            )
            for k, out in enumerate((h_out, gg_out, ug_out, fb_out))
        ]

    for i in range(n):
        s = order[i]
        slot = i % 2
        if i == 1:
            arrive(1)
            if n > 2:
                pl.when(is_mid)(functools.partial(arrive, 2))
        elif i > 1:
            pl.when(jnp.logical_not(is_mid))(functools.partial(arrive, i))
        if i + 1 < n:
            load_cot(i + 1).start()
        load_cot(i).wait()
        if i >= 2:
            for copy in stage_out(i - 2):
                copy.wait()
        x_ref = own_ref if i == 0 else n_buf.at[s]
        fb_acc[...] = jnp.zeros_like(fb_acc)
        fi_acc[...] = jnp.zeros_like(fi_acc)

        def one_tile(j, carry):
            if i == 0:
                for copy in load_weights(j):
                    copy.wait()
            if 2 <= i < n - 1:
                pl.when(is_mid & (j == tiles // 2))(functools.partial(arrive, i + 1))
            cols = pl.ds(pl.multiple_of(j * tile, tile), tile)
            x = x_ref[...]
            wg, wu, wd = wg_ref[:, cols], wu_ref[:, cols], wd_ref[cols, :]
            gate = mm(x, wg)
            up = mm(x, wu)
            act_grad = mm_bt(c_buf[slot], wd)
            sig = jax.nn.sigmoid(gate)
            silu = gate * sig
            h = (silu * up).astype(BF)
            gg = (act_grad * up * (sig * (1.0 + gate * (1.0 - sig)))).astype(BF)
            ug = (act_grad * silu).astype(BF)
            for k, value in enumerate((h, gg, ug)):
                st_buf[slot, k, :, cols] = value
            for k in range(0, width, 512):
                piece = slice(k, k + 512)
                fb_acc[:, piece] += mm(h, wd_ref[cols, piece])
                fi_acc[:, piece] += mm_bt(gg, wg_ref[piece, cols]) + mm_bt(ug, wu_ref[piece, cols])
            return carry

        lax.fori_loop(0, tiles, one_tile, 0)
        st_buf[slot, 3, :, :width] = fb_acc[...].astype(BF)
        for copy in stage_out(i):
            copy.start()
        if i == 0:
            fi_out[...] = fi_acc[...]
        else:
            fi_part[s] = fi_acc[...].astype(BF)

            @pl.when(t == 0)
            def _():
                for c in range(parts):
                    scatter(i, c, True).start()

            @pl.when(t == n - 1)
            def _():
                for c in range(parts):
                    scatter(n - 1 - i, c, False).start()

    def pass_on(index, c):
        piece = pl.ds(c * part_rows, part_rows)
        for to_right in (True, False):
            s = index if to_right else n - 1 - index
            k = 0 if to_right else 1
            has_source = t > 0 if to_right else t < n - 1
            beyond = s > t if to_right else s < t

            @pl.when(has_source & beyond)
            def _():
                scatter(s, c, to_right).wait_recv()
                total = fi_part[s, piece].astype(F32) + got[k, index - 1, piece].astype(F32)
                fi_part[s, piece] = total.astype(BF)
                scatter(s, c, to_right).start()

            @pl.when(has_source & (s == t))
            def _():
                scatter(s, c, to_right).wait_recv()
                fi_out[piece] += got[k, index - 1, piece].astype(F32)

    for i in range(max(0, n - 2), n):
        for copy in stage_out(i):
            copy.wait()
    for index in range(1, n):
        for c in range(parts):
            pass_on(index, c)
    for i in range(n):
        keep_rows(i).wait()
    for s in range(n):
        for to_right in (True, False):
            goes_on = t < n - 1 if to_right else t > 0

            @pl.when(goes_on & (s <= t if to_right else s >= t))
            def _():
                gather(s, to_right).wait_send()

            @pl.when(goes_on & (s > t if to_right else s < t))
            def _():
                for c in range(parts):
                    scatter(s, c, to_right).wait_send()


def ffn_call(n, own_rows, cot_all, w_gate, w_up, w_down):
    rows, width = own_rows.shape
    units = w_gate.shape[1]
    tile = min(512, units)
    tiles = units // tile
    parts = max(1, rows // 64)
    tall = jax.ShapeDtypeStruct((n, rows, units), BF)
    wide = jax.ShapeDtypeStruct((n, rows, width), BF)
    any_spec = pl.BlockSpec(memory_space=pl.ANY)
    vmem_spec = pl.BlockSpec(memory_space=pltpu.VMEM)
    dma = pltpu.SemaphoreType.DMA
    return pl.pallas_call(
        functools.partial(ffn_kernel, n),
        out_shape=[tall, tall, tall, wide, wide, jax.ShapeDtypeStruct((rows, width), F32)],
        in_specs=[vmem_spec] + [any_spec] * 4,
        out_specs=[any_spec] * 5 + [vmem_spec],
        scratch_shapes=[
            pltpu.VMEM((width, units), BF),
            pltpu.VMEM((width, units), BF),
            pltpu.VMEM((units, width), BF),
            pltpu.VMEM((n, rows, width), BF),
            pltpu.VMEM((2, rows, width), BF),
            pltpu.VMEM((2, 4, rows, max(units, width)), BF),
            pltpu.VMEM((n, rows, width), BF),
            pltpu.VMEM((2, n - 1, rows, width), BF),
            pltpu.VMEM((rows, width), F32),
            pltpu.VMEM((rows, width), F32),
            dma((3, tiles)),
            dma((2,)),
            dma((4, 2)),
            dma((n,)),
            dma((2, n)),
            dma((n,)),
            dma((2, n - 1, parts)),
            dma((2, n - 1, parts)),
        ],
        compiler_params=pltpu.CompilerParams(
            vmem_limit_bytes=63 * 1024 * 1024, collective_id=4, has_side_effects=True
        ),
        cost_estimate=pl.CostEstimate(
            flops=12 * n * rows * width * units, bytes_accessed=6 * width * units, transcendentals=0
        ),
        name="ffn_plain",
    )(own_rows, cot_all, w_gate, w_up, w_down)


MID_NAMES = (
    ("own", "cot_in", "wg_h", "wu_h", "wd_h", "middle_h"),
    ("cot", "h_out", "tot", "two", "late", "fi_out", "base", "far"),
    ("wg", "wu", "wd", "n_buf", "gu", "h_st", "c_buf", "part", "land", "acc"),
    ("w_sem", "own_sem", "c_sem", "h_sem", "re_sem", "tot_sem", "out_sem", "ready"),
    ("ag_send", "ag_recv", "ct_send", "ct_recv", "rs_send", "rs_recv"),
    ("one_send", "one_recv", "two_send", "two_recv", "late_sem", "far_sem"),
)


def middle_kernel(n, *refs):
    names = [name for group in MID_NAMES for name in group]
    r = types.SimpleNamespace(**dict(zip(names, refs, strict=True)))
    t, d = lax.axis_index("tensor"), lax.axis_index("dp")
    rows, width = r.own.shape
    units = r.wg.shape[1]
    tokens = n * rows
    tile = 512
    tiles = units // tile
    parts = r.rs_send.shape[3]
    part_rows = rows // parts
    order = arrival_order(t, n)
    is_mid = (t > 0) & (t < n - 1)
    is_end = jnp.logical_not(is_mid)
    core, x, y = lax.rem(d, 2), lax.rem(d // 2, 2), d // 4
    chunk = width // 8
    halves = units // 2

    def load_weights(j):
        cols = pl.ds(j * tile, tile)
        return [
            pltpu.make_async_copy(r.wg_h.at[:, cols], r.wg.at[:, cols], r.w_sem.at[0, j]),
            pltpu.make_async_copy(r.wu_h.at[:, cols], r.wu.at[:, cols], r.w_sem.at[1, j]),
            pltpu.make_async_copy(r.wd_h.at[cols, :], r.wd.at[cols, :], r.w_sem.at[2, j]),
        ]

    def line(buf, send_sem, recv_sem, s, to_right, src=None):
        return copy_to(
            buf.at[s] if src is None else src,
            buf.at[s],
            send_sem.at[0 if to_right else 1, s],
            recv_sem.at[s],
            tensor=t + 1 if to_right else t - 1,
        )

    gather = functools.partial(line, r.n_buf, r.ag_send, r.ag_recv)
    gather_cot = functools.partial(line, r.cot, r.ct_send, r.ct_recv)
    own_rows = pltpu.make_async_copy(r.own, r.n_buf.at[t], r.own_sem.at[0])

    def load_cot(i):
        return pltpu.make_async_copy(r.cot.at[order[i]], r.c_buf.at[i % 2], r.c_sem.at[i % 2])

    def keep_h(i):
        return pltpu.make_async_copy(r.h_st, r.h_out.at[order[i]], r.h_sem.at[0])

    def scatter(q, s, c, to_right):
        k, index = (0, s - 1) if to_right else (1, n - 2 - s)
        piece = pl.ds(c * part_rows, part_rows)
        to = t + 1 if to_right else t - 1
        slot = s if to_right else jnp.where(to == s, n, s)
        return copy_to(
            r.part.at[q, s, piece],
            r.land.at[q, slot, piece],
            r.rs_send.at[q, k, index, c],
            r.rs_recv.at[q, k, index, c],
            tensor=to,
        )

    own_rows.start()
    for copy in load_weights(0):
        copy.start()
    load_cot(0).start()
    group_barrier([1, 2, 4], n, d, t)
    own_rows.wait()
    pl.when(t < n - 1)(lambda: gather(t, True).start())
    pl.when(t > 0)(lambda: gather(t, False).start())
    for j in range(1, tiles):
        for copy in load_weights(j):
            copy.start()

    def arrive(which, i):
        s = order[i]
        which(s, True).wait_recv()
        pl.when((s < t) & (t < n - 1))(lambda: which(s, True).start())
        pl.when((s > t) & (t > 0))(lambda: which(s, False).start())

    def end_sends(q, i, chunks):
        @pl.when(t == 0)
        def _():
            for c in chunks:
                scatter(q, i, c, True).start()

        @pl.when(t == n - 1)
        def _():
            for c in chunks:
                scatter(q, n - 1 - i, c, False).start()

    def forward(i):
        s = order[i]
        if i:
            keep_h(i - 1).wait()
        r.acc[...] = jnp.zeros_like(r.acc)

        def one_tile(j, carry):
            if i == 0:
                for copy in load_weights(j):
                    copy.wait()
            if 2 <= i < n - 1:
                pl.when(is_mid & (j == tiles // 2))(functools.partial(arrive, gather, i + 1))
            cols = pl.ds(pl.multiple_of(j * tile, tile), tile)
            rows_in = r.n_buf[s]
            gate = mm(rows_in, r.wg[:, cols])
            up = mm(rows_in, r.wu[:, cols])
            sig = jax.nn.sigmoid(gate)
            silu = gate * sig
            h = (silu * up).astype(BF)
            r.h_st[:, cols] = h
            r.gu[0, s, :, cols] = (up * (sig * (1.0 + gate * (1.0 - sig)))).astype(BF)
            r.gu[1, s, :, cols] = silu.astype(BF)
            for k in range(0, width, 512):
                piece = slice(k, k + 512)
                r.acc[:, piece] += mm(h, r.wd[cols, piece])
            return carry

        lax.fori_loop(0, tiles, one_tile, 0)
        keep_h(i).start()
        r.part[0, s] = r.acc[...].astype(BF)
        if 0 < i < n - 1:
            end_sends(0, i, range(parts))

    def backward(i, chunks):
        s = order[i]
        r.acc[...] = jnp.zeros_like(r.acc)
        load_cot(i).wait()

        def one_tile(j, carry):
            cols = pl.ds(pl.multiple_of(j * tile, tile), tile)
            act_grad = mm_bt(r.c_buf[i % 2], r.wd[cols, :])
            gg = (act_grad * r.gu[0, s, :, cols].astype(F32)).astype(BF)
            ug = (act_grad * r.gu[1, s, :, cols].astype(F32)).astype(BF)
            r.gu[0, s, :, cols] = gg
            r.gu[1, s, :, cols] = ug
            for k in range(0, width, 512):
                piece = slice(k, k + 512)
                r.acc[:, piece] += mm_bt(gg, r.wg[piece, cols]) + mm_bt(ug, r.wu[piece, cols])
            return carry

        lax.fori_loop(0, tiles, one_tile, 0)
        r.part[1, s] = r.acc[...].astype(BF)
        if i:
            end_sends(1, i, chunks)

    from_left = t * 2 < n - 1

    def pass_on(q, index, near):
        for c in range(parts):
            piece = pl.ds(c * part_rows, part_rows)
            for to_right in (True, False):
                s = index if to_right else n - 1 - index
                has_source = t > 0 if to_right else t < n - 1
                now = from_left == (to_right == near)

                @pl.when(has_source & now & (s > t if to_right else s < t))
                def _():
                    scatter(q, s, c, to_right).wait_recv()
                    total = r.part[q, s, piece].astype(F32) + r.land[q, s, piece].astype(F32)
                    r.part[q, s, piece] = total.astype(BF)
                    scatter(q, s, c, to_right).start()

    everything = range(parts)
    forward(0)
    load_cot(1).start()
    backward(0, everything)
    arrive(gather, 1)
    pl.when(is_mid)(functools.partial(arrive, gather, 2))
    pl.when(is_mid)(lambda: load_cot(2).start())
    forward(1)
    backward(1, everything)
    pl.when(is_end)(functools.partial(arrive, gather, 2))
    forward(2)
    @pl.when(is_mid)
    def _():
        gather_cot(t - 1, True).start()
        gather_cot(t + 1, False).start()

    pl.when(is_mid)(functools.partial(backward, 2, everything))
    pl.when(is_end)(functools.partial(arrive, gather, 3))
    forward(3)

    @pl.when(is_end)
    def _():
        arrive(gather_cot, 2)
        load_cot(2).start()
        backward(2, everything)

    arrive(gather_cot, 3)
    load_cot(3).start()
    backward(3, (0, 1))
    keep_h(3).wait()

    first, second = pl.ds(0, tokens), pl.ds(tokens, tokens)
    reload = []
    for k, (src, dst, base) in enumerate(((r.h_out, r.wg, 0), (r.cot, r.wu, tokens))):
        for s in range(n):
            place = dst.at[pl.ds(base + s * rows, rows)]
            reload.append(pltpu.make_async_copy(src.at[s], place, r.re_sem.at[k, s]))
    for copy in reload:
        copy.start()
    pl.semaphore_signal(r.ready, inc=1, device_id={"dp": d ^ 1}, device_id_type=pl.DeviceIdType.MESH)
    pl.semaphore_wait(r.ready, 1)

    def block(w, j):
        if w == 2:
            return r.wg.at[pl.ds(tokens + j * chunk, chunk)]
        return r.wd.at[pl.ds((w * 4 + j) * chunk, chunk)]

    def lhs(w, j, who):
        cols = pl.ds(pl.multiple_of((2 * j + who) * chunk, chunk), chunk)
        if w == 0:
            return r.wu[second, cols]
        return r.n_buf[:, :, cols].reshape(tokens, chunk)

    def rhs(w, part):
        if w == 0:
            return r.wg[first, part]
        return r.gu[w - 1, :, :, part].reshape(tokens, part.stop - part.start)

    def stage_one(w, j):
        return copy_to(r.c_buf.at[lax.rem(j, 2)], block(w, j), r.one_send.at[w, j], r.one_recv.at[w, j], dp=d ^ 1)

    def stage_two(w, k):
        j = (2 * y + 1 - x, 2 * (1 - y) + 1 - x, 2 * (1 - y) + x, 2 * (1 - y) + 1 - x)[k]
        cols = pl.ds((k // 2) * halves, halves)
        return copy_to(
            block(w, j).at[:, cols], r.two.at[w, k], r.two_send.at[w, k], r.two_recv.at[w, k], dp=d ^ (2, 2, 4, 4)[k]
        )

    def keep_late(i):
        k = i if i < 4 else 2 * (i - 4)
        j = (2 * y + 1 - x, 2 * (1 - y) + 1 - x, 2 * (1 - y) + x, 2 * (1 - y) + 1 - x)[k]
        cols = pl.ds((k // 2) * halves, halves)
        return pltpu.make_async_copy(block(2 if i < 4 else 1, j).at[:, cols], r.late.at[i], r.late_sem.at[i])

    def leave(w, k):
        if w == 0 or (w == 1 and k % 2):
            return stage_two(w, k)
        return keep_late(k if w == 2 else 4 + k // 2)

    def keep_total(w, k):
        j = (2 * y + x, 2 * (1 - y) + x, 2 * y + x, 2 * y + 1 - x)[k]
        cols = pl.ds((k // 2) * halves, halves)
        return pltpu.make_async_copy(block(w, j).at[:, cols], r.tot.at[w, k], r.tot_sem.at[w, k])

    for w in range(3):
        if w == 0:
            for copy in reload:
                copy.wait()

        def give(j, carry):
            @pl.when(j >= 2)
            def _():
                stage_one(w, j - 2).wait_send()

            grads = lhs(w, j, 1 - core)
            for k in range(0, units, 512):
                part = slice(k, k + 512)
                r.c_buf[lax.rem(j, 2), :, part] = mm_at(grads, rhs(w, part)).astype(BF)
            stage_one(w, j).start()
            return carry

        def keep(j, carry):
            stage_one(w, j).wait_recv()
            grads = lhs(w, j, core)
            for k in range(0, units, 512):
                part = slice(k, k + 512)
                piece = block(w, j).at[:, part]
                piece[...] = (piece[...].astype(F32) + mm_at(grads, rhs(w, part))).astype(BF)
            return carry

        lax.fori_loop(0, 4, give, 0)
        if w == 0:
            end_sends(1, 3, (2,))
        lax.fori_loop(0, 4, keep, 0)
        if w == 0:
            end_sends(1, 3, (3,))
        for j in (2, 3):
            stage_one(w, j).wait_send()
        for k in range(4):
            leave(w, k).start()
            keep_total(w, k).start()
        if w == 0:
            pass_on(0, 2, True)
        if w == 1:
            end_sends(0, n - 1, everything)
    def total_of(q):
        r.acc[...] += r.part[q, t].astype(F32)
        for to_right in (True, False):
            has_source = (t > 0 if to_right else t < n - 1) if q else is_mid

            @pl.when(has_source)
            def _():
                for s in range(n):

                    @pl.when(s == t)
                    def _():
                        for c in range(parts):
                            scatter(q, s, c, to_right).wait_recv()

                slot = t if to_right else n
                r.acc[...] += r.land[q, slot].astype(F32)

    add_middle = pltpu.make_async_copy(r.middle_h, r.acc, r.out_sem.at[0])
    add_middle.start()
    add_middle.wait()
    total_of(0)
    keep_base = pltpu.make_async_copy(r.acc, r.base, r.out_sem.at[0])
    keep_base.start()
    pass_on(1, 2, True)
    pass_on(1, 3, True)
    pass_on(1, 3, False)
    keep_base.wait()

    for to_right in (True, False):
        s = n - 1 if to_right else 0

        @pl.when(is_mid & (from_left == to_right))
        def _():
            for c in range(parts):
                scatter(0, s, c, to_right).wait_recv()
            r.part[0, s] = (r.part[0, s].astype(F32) + r.land[0, s].astype(F32)).astype(BF)

    keep_far = [pltpu.make_async_copy(r.part.at[0, s], r.far.at[i], r.far_sem.at[i]) for i, s in ((0, 0), (1, n - 1))]
    for copy in keep_far:
        copy.start()

    r.acc[...] = jnp.zeros_like(r.acc)
    total_of(1)
    keep_fi = pltpu.make_async_copy(r.acc, r.fi_out, r.out_sem.at[1])
    keep_fi.start()
    keep_fi.wait()
    for copy in keep_far:
        copy.wait()
    for w in range(3):
        for k in range(4):
            keep_total(w, k).wait()
            leave(w, k).wait()
    for s in range(n):
        for to_right in (True, False):
            goes_on = t < n - 1 if to_right else t > 0

            @pl.when(goes_on & (s <= t if to_right else s >= t))
            def _():
                gather(s, to_right).wait_send()

            @pl.when(goes_on & (s < t if to_right else s > t))
            def _():
                gather_cot(s, to_right).wait_send()

            @pl.when(goes_on & (s > t if to_right else s < t))
            def _():
                for c in range(parts):
                    scatter(1, s, c, to_right).wait_send()
                    if 0 < s < n - 1:
                        scatter(0, s, c, to_right).wait_send()
                    else:
                        pl.when(is_end)(lambda: scatter(0, s, c, to_right).wait_send())


def middle_call(n, own_rows, cot_part, w_gate, w_up, w_down, middle):
    rows, width = own_rows.shape
    units = w_gate.shape[1]
    parts = rows // 64
    shape = jax.ShapeDtypeStruct
    wide = shape((n, rows, width), BF)
    piece = (4, width // 8, units // 2)
    any_spec = pl.BlockSpec(memory_space=pl.ANY)
    dma = pltpu.SemaphoreType.DMA
    return pl.pallas_call(
        functools.partial(middle_kernel, n),
        out_shape=[wide, shape((n, rows, units), BF), shape((3, *piece), BF), shape((2, *piece), BF)]
        + [shape((6, *piece[1:]), BF), shape((rows, width), F32), shape((rows, width), F32)]
        + [shape((2, rows, width), BF)],
        in_specs=[any_spec] * 6,
        out_specs=[any_spec] * 8,
        input_output_aliases={1: 0},
        scratch_shapes=[
            pltpu.VMEM((width, units), BF),
            pltpu.VMEM((width, units), BF),
            pltpu.VMEM((units, width), BF),
            pltpu.VMEM((n, rows, width), BF),
            pltpu.VMEM((2, n, rows, units), BF),
            pltpu.VMEM((rows, units), BF),
            pltpu.VMEM((2, rows, width), BF),
            pltpu.VMEM((2, n, rows, width), BF),
            pltpu.VMEM((2, n + 1, rows, width), BF),
            pltpu.VMEM((rows, width), F32),
            dma((3, units // 512)),
            dma((1,)),
            dma((2,)),
            dma((1,)),
            dma((2, n)),
            dma((3, 4)),
            dma((2,)),
            pltpu.SemaphoreType.REGULAR,
            dma((2, n)),
            dma((n,)),
            dma((2, n)),
            dma((n,)),
            dma((2, 2, n - 1, parts)),
            dma((2, 2, n - 1, parts)),
            dma((3, 4)),
            dma((3, 4)),
            dma((3, 4)),
            dma((3, 4)),
            dma((6,)),
            dma((2,)),
        ],
        compiler_params=pltpu.CompilerParams(
            vmem_limit_bytes=64 * 1024 * 1024 - 65536, collective_id=1, has_side_effects=True
        ),
        cost_estimate=pl.CostEstimate(
            flops=18 * n * rows * width * units, bytes_accessed=6 * width * units, transcendentals=0
        ),
        name="middle",
    )(own_rows, cot_part, w_gate, w_up, w_down, middle)


def full_call(kernel, out_shapes, args, scratch=(), flops=0, name=None):
    spec = pl.BlockSpec(memory_space=pltpu.VMEM)
    return pl.pallas_call(
        kernel,
        out_shape=out_shapes,
        in_specs=[spec] * len(args),
        out_specs=[spec] * len(out_shapes),
        scratch_shapes=list(scratch),
        compiler_params=pltpu.CompilerParams(vmem_limit_bytes=VMEM_LIMIT),
        cost_estimate=pl.CostEstimate(flops=flops, bytes_accessed=flops // 400, transcendentals=0),
        name=name,
    )(*args)


def normalize(rows_wide, gain_wide):
    inverse = lax.rsqrt(jnp.mean(rows_wide * rows_wide, axis=-1, keepdims=True) + NORM_EPS)
    scaled_rows = rows_wide * inverse
    return scaled_rows, inverse, (scaled_rows * gain_wide).astype(BF)


def norm_back(normed_grad, scaled_rows, inverse, gain_wide):
    weighted = normed_grad * gain_wide
    return inverse * (weighted - scaled_rows * jnp.mean(weighted * scaled_rows, axis=-1, keepdims=True))


def pairs(n, bit):
    return [(i, i ^ bit) for i in range(n)]


def pick(array, index, axis):
    return lax.dynamic_index_in_dim(array, index, axis, keepdims=False)


def dp_scatter(give, keep, n_dp):
    me = lax.axis_index("dp")
    total = keep + lax.ppermute(give, "dp", pairs(n_dp, 1))
    if n_dp != 8:
        bit = 2
        while total.shape[0] > 1:
            parts = total.reshape(-1, 2, *total.shape[1:])
            mine = (me // bit) % 2
            total = pick(parts, mine, 1) + lax.ppermute(pick(parts, 1 - mine, 1), "dp", pairs(n_dp, bit))
            bit *= 2
        return total[0].astype(F32)
    x, y = (me // 2) % 2, me // 4
    cols = total.shape[-1] // 2
    parts = total.reshape(2, 2, *total.shape[1:])
    a, b = parts[..., :cols], parts[..., cols:]
    got_a = lax.ppermute(pick(a, 1 - x, 1), "dp", pairs(n_dp, 2))
    got_b = lax.ppermute(pick(b, 1 - y, 0), "dp", pairs(n_dp, 4))
    a = pick(a, x, 1) + got_a
    b = pick(b, y, 0) + got_b
    got_a = lax.ppermute(pick(a, 1 - y, 0), "dp", pairs(n_dp, 4))
    got_b = lax.ppermute(pick(b, 1 - x, 0), "dp", pairs(n_dp, 2))
    a = pick(a, y, 0).astype(F32) + got_a.astype(F32)
    b = pick(b, x, 0).astype(F32) + got_b.astype(F32)
    return jnp.concatenate([a, b], axis=-1)


def core_split(rows, n_dp):
    tokens, width = rows.shape
    core = lax.axis_index("dp") % 2
    parts = rows.reshape(tokens, n_dp // 2, 2, width // n_dp)
    return [pick(parts, c, 2).reshape(tokens, width // 2) for c in (1 - core, core)]


def grad_scatter(split_rows, cols, n_dp):
    give, keep = [
        mm_at(part, cols).astype(BF).reshape(n_dp // 2, 2 * part.shape[1] // n_dp, cols.shape[1])
        for part in split_rows
    ]
    return dp_scatter(give, keep, n_dp)


def after(value, *others):
    return lax.optimization_barrier((value, *others))[0]


def shards(n_dp, n_t, hidden_in, gain_attn, w_query, w_key, w_value, w_out, gain_ffn, w_gate, w_up, w_down, segments, parents, cotangent):
    tokens = segments.shape[0]
    own, width = hidden_in.shape
    q_cols, kv_cols, units = w_query.shape[1], w_key.shape[1], w_gate.shape[1]
    heads = q_cols // HD
    me_t = lax.axis_index("tensor")
    me_dp = lax.axis_index("dp")
    gain_attn_wide = gain_attn.astype(F32)
    gain_ffn_wide = gain_ffn.astype(F32)

    def ring(value, shift):
        return lax.ppermute(value, "tensor", [(i, (i + shift) % n_t) for i in range(n_t)])

    ancestry, depth = tree_tables(segments, parents)
    cosine, sine = rope_tables(depth)
    bias = jnp.where(jnp.repeat(ancestry, BLK, axis=1) > 0.5, 0.0, NEG)
    fused = n_dp == 8 and n_t == 4 and units == width and q_cols == 2 * own and tokens * 2 == width
    x_all, cot_all, w_out_all, queries, keys, values, mixed, lse, mixed_own, middle, normed_ffn = attn_call(
        n_dp, n_t, fused, hidden_in, cotangent, gain_attn[None], gain_ffn[None], w_query, w_key, w_value, w_out, cosine, sine, bias
    )
    x_all = x_all.reshape(tokens, width)
    w_out_all = w_out_all.reshape(n_t * q_cols, width)
    rows_wide = hidden_in.astype(F32)
    if fused:
        unused_cot, unused_h, totals, twos, late, ffn_in_grad, base, far = middle_call(
            n_t, normed_ffn, cot_all, w_gate, w_up, w_down, middle
        )
        arrays = dict(
            fi=ffn_in_grad,
            mid=middle,
            cot=cotangent,
            hid=hidden_in,
            q=queries,
            k=keys,
            v=values,
            m=mixed,
            lse=lse,
            cos=cosine,
            sin=sine,
            mixed=mixed_own,
            wq=w_query,
            wk=w_key,
            wv=w_value,
        )
        input_grad, project_wgrad, out_grad, gain_grads, threes, late_twos, far_sum = back_call(
            n_t,
            arrays,
            gain_attn[None],
            gain_ffn[None],
            bias,
            x_all.reshape(n_t, own, width),
            w_out_all.reshape(n_t, q_cols, width),
            totals,
            twos,
            late,
            far,
        )
        w_gate_grad, w_up_grad, w_down_grad, w_query_grad, w_key_grad, w_value_grad, w_out_grad, input_grad, output = (
            finish_call(totals, twos, late_twos, threes, project_wgrad, out_grad, input_grad, base, far_sum)
        )
        gain_attn_grad, gain_ffn_grad = gain_grads[0], gain_grads[1]
    else:
        w_project = jnp.concatenate([w_query, w_key, w_value], axis=1)
        h_all, gg_all, ug_all, n_all, fb_part, ffn_in_grad = ffn_call(n_t, normed_ffn, cot_all, w_gate, w_up, w_down)
        fb_sum = lax.psum_scatter(fb_part.reshape(tokens, width), "tensor", scatter_dimension=0, tiled=True)
        output = (middle + fb_sum.astype(F32)).astype(BF)
        h_all, gg_all, ug_all = [a.reshape(tokens, units) for a in (h_all, gg_all, ug_all)]
        cot_split = core_split(cot_all.reshape(tokens, width), n_dp)
        normed_split = core_split(n_all.reshape(tokens, width), n_dp)
        w_down_grad = grad_scatter(cot_split, h_all, n_dp).T
        w_gate_grad = grad_scatter(normed_split, gg_all, n_dp)
        w_up_grad = grad_scatter(normed_split, ug_all, n_dp)

        scaled_attn, inverse_attn, _ = normalize(rows_wide, gain_attn_wide)
        scaled_ffn, inverse_ffn, _ = normalize(middle, gain_ffn_wide)
        middle_grad = cotangent.astype(F32) + norm_back(ffn_in_grad, scaled_ffn, inverse_ffn, gain_ffn_wide)
        branch_grad = middle_grad.astype(BF)
        mixed_grads = mm_bt(branch_grad, w_out_all).astype(BF).reshape(own, n_t, q_cols)
        mixed_grads = [pick(mixed_grads, (me_t + n_t - d) % n_t, 1) for d in range(n_t)]
        mixed_grads = [mixed_grads[0]] + [ring(mixed_grads[d], n_t - d) for d in range(1, n_t)]
        mixed_grad = jnp.roll(jnp.concatenate(mixed_grads, axis=0), me_t * own, axis=0)

        (project_grad,) = full_call(
            attn_bwd_kernel,
            [jax.ShapeDtypeStruct((tokens, q_cols + 2 * kv_cols), BF)],
            (queries, keys, values, mixed, lse, mixed_grad, cosine, sine, bias),
            scratch=[pltpu.VMEM((tokens, kv_cols), F32)] * 2,
            flops=10 * heads * tokens * tokens * HD,
            name="attn_bwd",
        )
        dq, dk, dv = (
            project_grad[:, :q_cols],
            project_grad[:, q_cols : q_cols + kv_cols],
            project_grad[:, q_cols + kv_cols :],
        )
        attn_in_part = mm_bt(project_grad, w_project).astype(BF)
        attn_in_grad = lax.psum_scatter(attn_in_part, "tensor", scatter_dimension=0, tiled=True).astype(F32)

        mixed_wide = jnp.moveaxis(mixed_own, 0, 1).reshape(own, n_t * q_cols)
        out_grad = grad_scatter(core_split(branch_grad, n_dp), mixed_wide, n_dp)
        out_parts = out_grad.reshape(-1, n_t, q_cols)
        w_out_grad = pick(out_parts, me_t, 1)
        for d in range(1, n_t):
            piece = pick(out_parts, (me_t + d) % n_t, 1).astype(BF)
            w_out_grad = w_out_grad + ring(piece, d).astype(F32)
        w_out_grad = w_out_grad.T

        project_wgrad = grad_scatter(core_split(x_all, n_dp), project_grad, n_dp)
        w_query_grad = project_wgrad[:, :q_cols]
        w_key_grad = project_wgrad[:, q_cols : q_cols + kv_cols]
        w_value_grad = project_wgrad[:, q_cols + kv_cols :]

        input_grad = (middle_grad + norm_back(attn_in_grad, scaled_attn, inverse_attn, gain_attn_wide)).astype(BF)

        def own_rows(array):
            return lax.dynamic_slice_in_dim(array, me_dp * (width // n_dp), width // n_dp, 0).astype(F32)

        gain_sums = jnp.stack(
            [
                jnp.sum(own_rows(w_project) * project_wgrad, axis=1),
                jnp.sum(own_rows(w_gate) * w_gate_grad, axis=1) + jnp.sum(own_rows(w_up) * w_up_grad, axis=1),
            ]
        )
        bit = 1
        while bit < n_t:
            gain_sums = gain_sums + lax.ppermute(gain_sums, "tensor", pairs(n_t, bit))
            bit *= 2
        gain_attn_grad = gain_sums[0] / own_rows(gain_attn)
        gain_ffn_grad = gain_sums[1] / own_rows(gain_ffn)

    return (
        output,
        input_grad,
        gain_attn_grad,
        w_query_grad,
        w_key_grad,
        w_value_grad,
        w_out_grad,
        gain_ffn_grad,
        w_gate_grad,
        w_up_grad,
        w_down_grad,
    )


def solution(mesh):
    return jax.shard_map(
        functools.partial(shards, mesh.shape["dp"], mesh.shape["tensor"]),
        mesh=mesh,
        in_specs=(
            P(("dp", "tensor"), None),
            P(),
            P(None, "tensor"),
            P(None, "tensor"),
            P(None, "tensor"),
            P("tensor", None),
            P(),
            P(None, "tensor"),
            P(None, "tensor"),
            P("tensor", None),
            P("dp"),
            P("dp"),
            P(("dp", "tensor"), None),
        ),
        out_specs=(
            P(("dp", "tensor"), None),
            P(("dp", "tensor"), None),
            P("dp"),
            P("dp", "tensor"),
            P("dp", "tensor"),
            P("dp", "tensor"),
            P("tensor", "dp"),
            P("dp"),
            P("dp", "tensor"),
            P("dp", "tensor"),
            P("tensor", "dp"),
        ),
        check_vma=False,
    )
```

```python
import functools
import math
import types

import jax
import jax.numpy as jnp
from jax import lax
from jax.experimental import pallas as pl
from jax.experimental.pallas import tpu as pltpu
from jax.sharding import PartitionSpec as P

HD = 128
BLK = 128
NORM_EPS = 1e-05
ROPE_BASE = 1000000.0
SCALE = HD ** (-0.5)
SCALE2 = SCALE * math.log2(math.e)
NEG = -1e30
BF = jnp.bfloat16
F32 = jnp.float32
VMEM_LIMIT = 56 * 1024 * 1024


def mm(a, b):
    return jnp.dot(a, b, preferred_element_type=F32)


def mm_bt(a, b):
    return lax.dot_general(a, b, (((1,), (1,)), ((), ())), preferred_element_type=F32)


def mm_at(a, b):
    return lax.dot_general(a, b, (((0,), (0,)), ((), ())), preferred_element_type=F32)


def tree_tables(segment_ids, parent_ids):
    block_count = parent_ids.shape[0]
    first_ids = segment_ids.reshape(block_count, -1)[:, 0]
    block_iota = jnp.arange(block_count, dtype=jnp.int32)
    same_tree = first_ids[:, None] == first_ids[None, :]
    tree_start = jnp.min(jnp.where(same_tree, block_iota[None, :], block_count), axis=1)
    parent_block = tree_start + parent_ids
    step = (block_iota[None, :] == parent_block[:, None]) | (
        block_iota[None, :] == block_iota[:, None]
    )
    for _ in range(3):
        step = jnp.any(step[:, :, None] & step[None, :, :], axis=1)
    ancestry = step.astype(F32)
    return ancestry, jnp.sum(ancestry, axis=1) - 1.0


def head_cols(h):
    return slice(h * HD, (h + 1) * HD)


def causal_tile(rep):
    rows = lax.broadcasted_iota(jnp.int32, (BLK, BLK), 0)
    cols = lax.broadcasted_iota(jnp.int32, (BLK, BLK), 1)
    tile = cols <= rows
    return jnp.concatenate([tile] * rep, axis=0) if rep > 1 else tile


def stack_heads(ref, rows, first, rep):
    parts = [ref[rows, head_cols(first + i)] for i in range(rep)]
    return jnp.concatenate(parts, axis=0) if rep > 1 else parts[0]


def attend_block(b, q_ref, k_ref, v_ref, bias_ref, m_ref, lse_ref, causal, rep):
    rows = slice(b * BLK, (b + 1) * BLK)
    past = slice(0, b * BLK)
    for g in range(k_ref.shape[1] // HD):
        q = stack_heads(q_ref, rows, g * rep, rep)
        s_diag = jnp.where(causal, mm_bt(q, k_ref[rows, head_cols(g)]) * SCALE2, NEG)
        top = jnp.max(s_diag, axis=1, keepdims=True)
        if b:
            s_past = mm_bt(q, k_ref[past, head_cols(g)]) * SCALE2 + bias_ref[b : b + 1, past]
            top = jnp.maximum(top, jnp.max(s_past, axis=1, keepdims=True))
        e_diag = jnp.exp2(s_diag - top)
        mass = jnp.sum(e_diag, axis=1, keepdims=True)
        out = mm(e_diag.astype(BF), v_ref[rows, head_cols(g)])
        if b:
            e_past = jnp.exp2(s_past - top)
            mass = mass + jnp.sum(e_past, axis=1, keepdims=True)
            out = out + mm(e_past.astype(BF), v_ref[past, head_cols(g)])
        out = (out / mass).astype(BF)
        lse = top + jnp.log2(mass)
        for i in range(rep):
            h = g * rep + i
            m_ref[rows, head_cols(h)] = out[i * BLK : (i + 1) * BLK]
            lse_ref[rows, h : h + 1] = lse[i * BLK : (i + 1) * BLK]


def copy_to(src, dst, send_sem, recv_sem, **where):
    return pltpu.make_async_remote_copy(
        src_ref=src,
        dst_ref=dst,
        send_sem=send_sem,
        recv_sem=recv_sem,
        device_id=where,
        device_id_type=pl.DeviceIdType.MESH,
    )


def group_barrier(masks, n, d, t):
    barrier = pltpu.get_barrier_semaphore()
    for k in range(1, n):
        pl.semaphore_signal(
            barrier, inc=1, device_id={"tensor": lax.rem(t + k, n)}, device_id_type=pl.DeviceIdType.MESH
        )
    for mask in masks:
        pl.semaphore_signal(barrier, inc=1, device_id={"dp": d ^ mask}, device_id_type=pl.DeviceIdType.MESH)
    pl.semaphore_wait(barrier, n - 1 + len(masks))


def attn_kernel(
    n_dp,
    n,
    one_hop,
    hidden_ref,
    cot_ref,
    gains_ref,
    wq_hbm,
    wk_hbm,
    wv_hbm,
    wo_hbm,
    bias_ref,
    x_out,
    cot_out,
    wo_out,
    q_ref,
    k_ref,
    v_ref,
    m_ref,
    lse_ref,
    mixed_ref,
    middle_ref,
    normed_ref,
    cos_ref,
    sin_ref,
    own_buf,
    x_buf,
    wq_ref,
    wk_ref,
    wv_ref,
    wo_ref,
    w_sem,
    x_sem,
    misc_sem,
    ag_send,
    ag_recv,
    cot_send,
    cot_recv,
    wz_send,
    wz_recv,
    wp_send,
    wp_recv,
    wc_send,
    wc_recv,
    m_send,
    m_recv,
):
    t, d = lax.axis_index("tensor"), lax.axis_index("dp")
    rows, width = hidden_ref.shape
    q_cols = wq_ref.shape[1]
    heads, kv_heads = q_cols // HD, wk_ref.shape[1] // HD
    rep = heads // kv_heads
    share = q_cols // n_dp
    half = q_cols // 2
    order = arrival_order(t, n)
    gain_a_ref, gain_f_ref = gains_ref.at[pl.ds(0, 1)], gains_ref.at[pl.ds(1, 1)]
    is_mid = (t > 0) & (t < n - 1)
    core, plane = lax.rem(d, 2), d // 2
    masks = list(range(2, n_dp, 2))

    load_w = [
        pltpu.make_async_copy(src, dst, w_sem.at[i])
        for i, (src, dst) in enumerate(((wq_hbm, wq_ref), (wk_hbm, wk_ref), (wv_hbm, wv_ref)))
    ]
    own_wo = pltpu.make_async_copy(wo_hbm, wo_ref.at[t], misc_sem.at[0])
    own_cot = pltpu.make_async_copy(cot_ref, cot_out.at[t], misc_sem.at[1])
    for copy in load_w:
        copy.start()
    own_wo.start()
    own_cot.start()

    def norm(values, gain_ref):
        inverse = lax.rsqrt(jnp.mean(values * values, axis=-1, keepdims=True) + NORM_EPS)
        return (values * inverse * gain_ref[...].astype(F32)).astype(BF)

    for r in range(0, rows, 64):
        part = slice(r, r + 64)
        own_buf[part, :] = norm(hidden_ref[part, :].astype(F32), gain_a_ref)
    group_barrier([1, *masks], n, d, t)

    def line_copy(buf, send_sem, recv_sem, s, to_right, src=None):
        return copy_to(
            buf.at[s] if src is None else src,
            buf.at[s],
            send_sem.at[0 if to_right else 1, s],
            recv_sem.at[s],
            tensor=t + 1 if to_right else t - 1,
        )

    gather_x = functools.partial(line_copy, x_buf, ag_send, ag_recv)
    gather_cot = functools.partial(line_copy, cot_out, cot_send, cot_recv)

    def first_hop(gather, src):
        pl.when(t < n - 1)(lambda: gather(t, True, src).start())
        pl.when(t > 0)(lambda: gather(t, False, src).start())

    def arrive(gather, i):
        s = order[i]
        gather(s, True).wait_recv()
        pl.when((s < t) & (t < n - 1))(lambda: gather(s, True).start())
        pl.when((s > t) & (t > 0))(lambda: gather(s, False).start())

    def keep_rows(i):
        return pltpu.make_async_copy(own_buf if i == 0 else x_buf.at[order[i]], x_out.at[order[i]], x_sem.at[i])

    my_rows = pl.ds(pl.multiple_of(core * half + plane * share, 16), share)
    my_half = pl.ds(pl.multiple_of(core * half, 16), half)

    def wo_line(k):
        return copy_to(
            wo_hbm.at[my_rows],
            wo_ref.at[t, my_rows],
            wz_send.at[k - 1],
            wz_recv.at[k - 1],
            tensor=lax.rem(t + k, n),
        )

    def wo_plane(k, j):
        s = lax.rem(t + n - k, n)
        return copy_to(
            wo_ref.at[s, my_rows],
            wo_ref.at[s, my_rows],
            wp_send.at[k - 1, j],
            wp_recv.at[k - 1, j],
            dp=d ^ masks[j],
        )

    def wo_core(k):
        s = lax.rem(t + n - k, n)
        return copy_to(
            wo_ref.at[s, my_half], wo_ref.at[s, my_half], wc_send.at[k - 1], wc_recv.at[k - 1], dp=d ^ 1
        )

    first_hop(gather_x, own_buf)
    for k in range(1, n):
        wo_line(k).start()
    keep_rows(0).start()

    lane = lax.broadcasted_iota(jnp.int32, (BLK, HD), 1)
    low = lane < HD // 2
    index = jnp.where(low, lane, lane - HD // 2).astype(F32)
    frequency = jnp.exp(index * (-2.0 * math.log(ROPE_BASE) / HD))
    offset = lax.broadcasted_iota(jnp.int32, (BLK, HD), 0).astype(F32)
    for b in range(n * rows // BLK):
        angles = (bias_ref[b : b + 1, n * rows :] + offset) * frequency
        sine = jnp.sin(angles)
        cos_ref[b * BLK : (b + 1) * BLK, :] = jnp.cos(angles)
        sin_ref[b * BLK : (b + 1) * BLK, :] = jnp.where(low, -sine, sine)

    for copy in load_w:
        copy.wait()
    for i in range(n):
        s = order[i]
        if i == 1:
            arrive(gather_x, 1)
            if n > 2:
                pl.when(is_mid)(lambda: arrive(gather_x, 2))
        elif i > 1:
            if i > 2:
                arrive(gather_x, i)
            else:
                pl.when(jnp.logical_not(is_mid))(lambda: arrive(gather_x, 2))
        if i:
            keep_rows(i).start()
        x = own_buf[...] if i == 0 else x_buf[s]
        here = pl.ds(pl.multiple_of(s * rows, rows), rows)
        cosine, sine = cos_ref[here, :], sin_ref[here, :]
        for w_ref, out_ref, count in ((wq_ref, q_ref, heads), (wk_ref, k_ref, kv_heads)):
            raw = mm(x, w_ref[...])
            for h in range(count):
                u = raw[:, head_cols(h)]
                out_ref[here, head_cols(h)] = (u * cosine + pltpu.roll(u, HD // 2, 1) * sine).astype(BF)
        v_ref[here, :] = mm(x, wv_ref[...]).astype(BF)
        if i == 1:
            for k in range(1, n):
                wo_line(k).wait_recv()
                for j in range(len(masks)):
                    wo_plane(k, j).start()
        if i == n - 1:
            first_hop(gather_cot, cot_ref)
            for k in range(1, n):
                for j in range(len(masks)):
                    wo_plane(k, j).wait_recv()
                wo_core(k).start()

    def heads_to(r):
        here = pl.ds(r * rows, rows)
        return copy_to(m_ref.at[here], mixed_ref.at[t], m_send.at[r], m_recv.at[t], tensor=r)

    causal = causal_tile(rep)
    for b in range(n * rows // BLK):
        attend_block(b, q_ref, k_ref, v_ref, bias_ref, m_ref, lse_ref, causal, rep)
        if (b + 1) * BLK % rows == 0:
            r = (b + 1) * BLK // rows - 1
            pl.when(t != r)(lambda: heads_to(r).start())

            @pl.when(t == r)
            def _():
                mixed_ref[r] = m_ref[r * rows : (r + 1) * rows, :]

    if n > 2 and not one_hop:

        @pl.when(is_mid)
        def _():
            arrive(gather_cot, 1)
            arrive(gather_cot, 2)

    own_wo.wait()
    for k in range(1, n):
        s = lax.rem(t + n - k, n)
        copy_to(m_ref.at[pl.ds(0, rows)], mixed_ref.at[s], m_send.at[0], m_recv.at[s], tensor=s).wait_recv()
        wo_core(k).wait_recv()
    keep_wo = pltpu.make_async_copy(wo_ref, wo_out, misc_sem.at[0])
    keep_wo.start()
    for r in range(0, rows, 128):
        part = slice(r, r + 128)
        total = hidden_ref[part, :].astype(F32)
        for s in range(n):
            total = total + mm(mixed_ref[s, part, :], wo_ref[s])
        middle_ref[part, :] = total
        normed_ref[part, :] = norm(total, gain_f_ref)

    if one_hop:
        pl.when(t > 0)(lambda: gather_cot(t - 1, True).wait_recv())
        pl.when(t < n - 1)(lambda: gather_cot(t + 1, False).wait_recv())
    else:
        for i in range(1, n):
            if i > 2:
                arrive(gather_cot, i)
            else:
                pl.when(jnp.logical_not(is_mid))(functools.partial(arrive, gather_cot, i))
    own_cot.wait()
    keep_wo.wait()
    for i in range(n):
        keep_rows(i).wait()
    for k in range(1, n):
        wo_line(k).wait_send()
        wo_core(k).wait_send()
        for j in range(len(masks)):
            wo_plane(k, j).wait_send()
    if one_hop:
        pl.when(t < n - 1)(lambda: gather_cot(t, True).wait_send())
        pl.when(t > 0)(lambda: gather_cot(t, False).wait_send())
    for s in range(n):
        pl.when(t != s)(lambda: heads_to(s).wait_send())
        for to_right in (True, False):
            goes_on = t < n - 1 if to_right else t > 0

            @pl.when(goes_on & (s <= t if to_right else s >= t))
            def _():
                gather_x(s, to_right).wait_send()
                if not one_hop:
                    gather_cot(s, to_right).wait_send()


def attn_call(n_dp, n, one_hop, hidden, cot, gains, wq, wk, wv, wo, bias):
    rows, width = hidden.shape
    q_cols, kv_cols = wq.shape[1], wk.shape[1]
    tokens = n * rows
    any_spec = pl.BlockSpec(memory_space=pl.ANY)
    vmem_spec = pl.BlockSpec(memory_space=pltpu.VMEM)
    dma = pltpu.SemaphoreType.DMA
    masks = n_dp // 2 - 1
    shape = jax.ShapeDtypeStruct
    return pl.pallas_call(
        functools.partial(attn_kernel, n_dp, n, one_hop),
        out_shape=[
            shape((n, rows, width), BF),
            shape((n, rows, width), BF),
            shape((n, q_cols, width), BF),
            shape((tokens, q_cols), BF),
            shape((tokens, kv_cols), BF),
            shape((tokens, kv_cols), BF),
            shape((tokens, q_cols), BF),
            shape((tokens, HD), F32),
            shape((n, rows, q_cols), BF),
            shape((rows, width), F32),
            shape((rows, width), BF),
            shape((tokens, HD), F32),
            shape((tokens, HD), F32),
        ],
        in_specs=[vmem_spec, any_spec, vmem_spec] + [any_spec] * 4 + [vmem_spec],
        out_specs=[any_spec] * 3 + [vmem_spec] * 10,
        scratch_shapes=[
            pltpu.VMEM((rows, width), BF),
            pltpu.VMEM((n, rows, width), BF),
            pltpu.VMEM((width, q_cols), BF),
            pltpu.VMEM((width, kv_cols), BF),
            pltpu.VMEM((width, kv_cols), BF),
            pltpu.VMEM((n, q_cols, width), BF),
            dma((3,)),
            dma((n,)),
            dma((2,)),
            dma((2, n)),
            dma((n,)),
            dma((2, n)),
            dma((n,)),
            dma((n - 1,)),
            dma((n - 1,)),
            dma((n - 1, masks)),
            dma((n - 1, masks)),
            dma((n - 1,)),
            dma((n - 1,)),
            dma((n,)),
            dma((n,)),
        ],
        compiler_params=pltpu.CompilerParams(
            vmem_limit_bytes=VMEM_LIMIT, collective_id=2, has_side_effects=True
        ),
        cost_estimate=pl.CostEstimate(
            flops=2 * tokens * width * (q_cols + 2 * kv_cols), bytes_accessed=1 << 25, transcendentals=0
        ),
        name="attn",
    )(hidden, cot, gains, wq, wk, wv, wo, bias)


def arrival_order(t, n):
    near = jnp.minimum(t, n - 1 - t)
    order = [t]
    for i in range(1, n):
        both = t - (i + 1) // 2 if i % 2 else t + i // 2
        one_side = jnp.where(t > n - 1 - t, t - (i - near), t + (i - near))
        order.append(jnp.where(i <= 2 * near, both, one_side))
    return order


def attend_back_block(g, b, q_ref, k_ref, v_ref, o_ref, lse_ref, do_ref, turn_back, bias_ref, d_ref, dk_acc, dv_acc):
    heads, kv_heads = q_ref.shape[1] // HD, k_ref.shape[1] // HD
    rep = heads // kv_heads
    last = q_ref.shape[0] // BLK - 1
    causal = causal_tile(rep)
    rows = slice(b * BLK, (b + 1) * BLK)
    q = stack_heads(q_ref, rows, g * rep, rep)
    do = stack_heads(do_ref, rows, g * rep, rep)
    o = stack_heads(o_ref, rows, g * rep, rep)
    lse = [lse_ref[rows, h : h + 1] for h in range(g * rep, (g + 1) * rep)]
    lse = jnp.concatenate(lse, axis=0) if rep > 1 else lse[0]
    delta = jnp.sum(do.astype(F32) * o.astype(F32), axis=1, keepdims=True)
    k_d = k_ref[rows, head_cols(g)]
    p = jnp.where(causal, jnp.exp2(mm_bt(q, k_d) * SCALE2 - lse), 0.0)
    ds = (p * (mm_bt(do, v_ref[rows, head_cols(g)]) - delta)).astype(BF)
    dq = mm(ds, k_d)
    dk = mm_at(ds, q)
    dv = mm_at(p.astype(BF), do)
    if b < last:
        dk = dk + dk_acc[rows, head_cols(g)]
        dv = dv + dv_acc[rows, head_cols(g)]
    d_ref[rows, head_cols(heads + g)] = turn_back(dk * SCALE, rows)
    d_ref[rows, head_cols(heads + kv_heads + g)] = dv.astype(BF)
    if b:
        past = slice(0, b * BLK)
        k_p = k_ref[past, head_cols(g)]
        p = jnp.exp2(mm_bt(q, k_p) * SCALE2 + (bias_ref[b : b + 1, past] - lse))
        ds = (p * (mm_bt(do, v_ref[past, head_cols(g)]) - delta)).astype(BF)
        dq = dq + mm(ds, k_p)
        dk = mm_at(ds, q)
        dv = mm_at(p.astype(BF), do)
        if b < last:
            dk = dk + dk_acc[past, head_cols(g)]
            dv = dv + dv_acc[past, head_cols(g)]
        dk_acc[past, head_cols(g)] = dk
        dv_acc[past, head_cols(g)] = dv
    dq = dq * SCALE
    for i in range(rep):
        d_ref[rows, head_cols(g * rep + i)] = turn_back(dq[i * BLK : (i + 1) * BLK], rows)


def attn_bwd_kernel(q_ref, k_ref, v_ref, o_ref, lse_ref, do_ref, cos_ref, sin_ref, bias_ref, d_ref, dk_acc, dv_acc):
    def turn_back(grad, rows):
        return (grad * cos_ref[rows, :] - pltpu.roll(grad, HD // 2, 1) * sin_ref[rows, :]).astype(BF)

    for b in range(q_ref.shape[0] // BLK - 1, -1, -1):
        for g in range(k_ref.shape[1] // HD):
            attend_back_block(
                g, b, q_ref, k_ref, v_ref, o_ref, lse_ref, do_ref, turn_back, bias_ref, d_ref, dk_acc, dv_acc
            )


BACK_INS = ("fi", "mid", "cot", "hid", "q", "k", "v", "m", "lse", "cos", "sin", "mixed", "wq", "wk", "wv")
BACK_NAMES = (
    BACK_INS,
    ("gains", "bias", "x_h", "wo_h", "tot_h", "two_h", "late_h", "far_h"),
    ("input_grad", "project_grad", "out_grad", "gain_grad", "three_h", "late_two", "far_add"),
    tuple(name + "_b" for name in BACK_INS),
    ("wo", "bg", "mg", "do", "dqkv", "dk_acc", "dv_acc", "got", "one_o", "one_p", "two_o", "two_p"),
    ("three_o", "three_p", "s3", "give", "zr", "gain_st", "gain_dp", "gain_line", "far_land"),
    ("in_sem", "wo_sem", "x_sem", "s3_sem", "mg_send", "mg_recv", "th_send", "th_recv", "one_send", "one_recv"),
    ("stw_send", "stw_recv", "sth_send", "sth_recv", "z_send", "z_recv", "rs_send", "rs_recv"),
    ("gd_send", "gd_recv", "gl_send", "gl_recv", "lt_send", "lt_recv"),
    ("late_sem", "far_sem", "far_send", "far_recv"),
)


def back_kernel(n, *refs):
    names = [name for group in BACK_NAMES for name in group]
    r = types.SimpleNamespace(**dict(zip(names, refs, strict=True)))
    r.gain_a, r.gain_f = r.gains.at[pl.ds(0, 1)], r.gains.at[pl.ds(1, 1)]
    t, d = lax.axis_index("tensor"), lax.axis_index("dp")
    rows, width = r.bg.shape
    q_cols, kv_cols = r.q_b.shape[1], r.k_b.shape[1]
    all_cols = q_cols + 2 * kv_cols
    tokens = n * rows
    core, x, y = lax.rem(d, 2), lax.rem(d // 2, 2), d // 4
    chunk = width // 8
    parts = r.rs_send.shape[2]
    part_rows = rows // parts
    order = arrival_order(t, n)
    is_mid = (t > 0) & (t < n - 1)
    from_left = t * 2 < n - 1
    pairs_o = [(2 * y + x, 2 * y + 1 - x, 2), (2 * (1 - y) + x, 2 * (1 - y) + 1 - x, 2)]
    pairs_o += [(2 * y + x, 2 * (1 - y) + x, 4), (2 * y + 1 - x, 2 * (1 - y) + 1 - x, 4)]

    loads = {
        name: pltpu.make_async_copy(getattr(r, name), getattr(r, name + "_b"), r.in_sem.at[i])
        for i, name in enumerate(BACK_INS)
    }
    load_wo = [pltpu.make_async_copy(r.wo_h.at[s], r.wo.at[s], r.wo_sem.at[s]) for s in range(n)]
    load_x = [pltpu.make_async_copy(r.x_h.at[s], r.wo.at[s, pl.ds(0, rows)], r.x_sem.at[s]) for s in range(n)]
    half = r.s3.shape[3]
    load_tot, load_two = {}, {}
    for w in range(3):
        for k in range(2):
            load_tot[w, k] = [pltpu.make_async_copy(r.tot_h.at[w, 2 * k + 1], r.s3.at[w, k], r.s3_sem.at[0, w, k])]
            if w < 2:
                landing = r.wo.at[w, pl.ds(rows, rows), pl.ds(k * half, half)]
                load_two[w, k] = [pltpu.make_async_copy(r.two_h.at[w, 2 * k + 1], landing, r.s3_sem.at[1, w, k])]
            else:
                load_two[w, k] = [
                    pltpu.make_async_copy(
                        r.late_two.at[2 * k + 1, :, pl.ds(i * q_cols, q_cols)], r.mg.at[2 * k + i], r.late_sem.at[k, i]
                    )
                    for i in range(2)
                ]

    def late_stage(i):
        k = i if i < 4 else 2 * (i - 4)
        src, dst = r.late_h.at[i], r.late_two.at[i]
        return copy_to(src, dst, r.lt_send.at[i], r.lt_recv.at[i], dp=d ^ (2, 2, 4, 4)[k])

    def far_copy(i, c, src=None):
        piece = pl.ds(c * part_rows, part_rows)
        return copy_to(
            r.far_land.at[piece] if src is None else src.at[i, piece],
            r.far_land.at[piece],
            r.far_send.at[i, c],
            r.far_recv.at[i, c],
            tensor=t + 1 if i else t - 1,
        )

    load_far = pltpu.make_async_copy(r.far_h.at[jnp.where(from_left, 0, 1)], r.bg, r.far_sem.at[0])
    for name in ("fi", "mid", "cot"):
        loads[name].start()
    for copy in load_wo:
        copy.start()
    for name in BACK_INS[3:]:
        loads[name].start()
    for w in range(3):
        for k in range(2):
            load_tot[w, k][0].start()
    group_barrier(range(1, 8), n, d, t)
    for k in (1, 3, 0, 2):
        late_stage(k).start()

    for name in ("fi", "mid", "cot"):
        loads[name].wait()

    def norm_back_part(grad, values, gain_ref):
        inverse = lax.rsqrt(jnp.mean(values * values, axis=-1, keepdims=True) + NORM_EPS)
        scaled = values * inverse
        weighted = grad * gain_ref[...].astype(F32)
        back = inverse * (weighted - scaled * jnp.mean(weighted * scaled, axis=-1, keepdims=True))
        return back, grad * scaled

    def gain_along_dp(mask):
        return copy_to(
            r.gain_st.at[d ^ mask, pl.ds(0, 8)],
            r.gain_dp.at[mask - 1],
            r.gd_send.at[mask - 1],
            r.gd_recv.at[mask - 1],
            dp=d ^ mask,
        )

    gain_sum = jnp.zeros((8, width), F32)
    for first in range(0, rows, 64):
        part = slice(first, first + 64)
        back, gain_part = norm_back_part(r.fi_b[part, :], r.mid_b[part, :], r.gain_f)
        gain_sum = gain_sum + jnp.sum(gain_part.reshape(8, 8, width), axis=0)
        total = r.cot_b[part, :].astype(F32) + back
        r.fi_b[part, :] = total
        r.bg[part, :] = total.astype(BF)
    for c in range(8):
        r.gain_st[c, 0:8, :] = gain_sum[:, c * chunk : (c + 1) * chunk]
    for mask in range(1, 8):
        gain_along_dp(mask).start()

    def rows_of(s):
        return pl.ds(pl.multiple_of(s * rows, rows), rows)

    def heads_back(k):
        s = lax.rem(t + k, n)
        return copy_to(r.mg.at[s], r.do.at[rows_of(t)], r.mg_send.at[k - 1], r.mg_recv.at[k - 1], tensor=s)

    for copy in load_wo:
        copy.wait()
    for k in range(1, n):
        s = lax.rem(t + k, n)
        r.mg[s] = mm_bt(r.bg[...], r.wo[s]).astype(BF)
        heads_back(k).start()
    r.do[rows_of(t), :] = mm_bt(r.bg[...], r.wo[t]).astype(BF)

    for w in range(2):
        for k in range(2):
            load_two[w, k][0].start()
    for copy in load_x:
        copy.start()

    def ffn_three(w, k):
        return copy_to(r.s3.at[w, k], r.three_h.at[w, k], r.th_send.at[w, k], r.th_recv.at[w, k], dp=d ^ (4, 2)[k])

    def start_ffn_three(w):
        for k in range(2):
            for copy in load_tot[w, k] + load_two[w, k]:
                copy.wait()
            if w < 2:
                other = r.wo[w, rows : 2 * rows, k * half : (k + 1) * half]
            else:
                other = jnp.concatenate([r.mg[2 * k], r.mg[2 * k + 1]], axis=1)
            r.s3[w, k] = (r.s3[w, k].astype(F32) + other.astype(F32)).astype(BF)
            ffn_three(w, k).start()

    start_ffn_three(0)
    start_ffn_three(1)

    ones, twos, threes = (r.one_o, r.one_p), (r.two_o, r.two_p), (r.three_o, r.three_p)

    def stage_one(i, j):
        cols = pl.ds(0, ones[i].shape[2])
        src = r.give.at[lax.rem(j, 2), :, cols]
        return copy_to(src, ones[i].at[j], r.one_send.at[i, j], r.one_recv.at[i, j], dp=d ^ 1)

    def halves(i, k):
        size = ones[i].shape[2] // 2
        return pl.ds((k // 2) * size, size)

    def stage_two(i, k):
        src = ones[i].at[pairs_o[k][1]].at[:, halves(i, k)]
        return copy_to(src, twos[i].at[k], r.stw_send.at[i, k], r.stw_recv.at[i, k], dp=d ^ pairs_o[k][2])

    def stage_three(i, k):
        j = (2 * (1 - y) + x, 2 * y + 1 - x)[k]
        src = ones[i].at[j].at[:, halves(i, 2 * k)]
        return copy_to(src, threes[i].at[k], r.sth_send.at[i, k], r.sth_recv.at[i, k], dp=d ^ (4, 2)[k])

    def start_three(i):
        for k in range(2):
            stage_two(i, 2 * k + 1).wait_recv()
            j = (2 * (1 - y) + x, 2 * y + 1 - x)[k]
            piece = ones[i].at[j].at[:, halves(i, 2 * k)]
            piece[...] = (piece[...].astype(F32) + twos[i][2 * k + 1].astype(F32)).astype(BF)
            stage_three(i, k).start()

    def final_half(i, k):
        stage_two(i, 2 * k).wait_recv()
        stage_three(i, k).wait_recv()
        total = ones[i].at[2 * y + x].at[:, halves(i, 2 * k)][...].astype(F32)
        return total + twos[i][2 * k].astype(F32) + threes[i][k].astype(F32)

    def dp_start(i, terms):
        def give(j, carry):
            @pl.when(j >= 2)
            def _():
                stage_one(i, j - 2).wait_send()

            for cols, value in terms(2 * j + 1 - core):
                r.give[lax.rem(j, 2), :, cols] = value.astype(BF)
            stage_one(i, j).start()
            return carry

        def keep(j, carry):
            stage_one(i, j).wait_recv()
            for cols, value in terms(2 * j + core):
                piece = ones[i].at[j].at[:, cols]
                piece[...] = (piece[...].astype(F32) + value).astype(BF)
            return carry

        lax.fori_loop(0, 4, give, 0)
        lax.fori_loop(0, 4, keep, 0)
        for j in (2, 3):
            stage_one(i, j).wait_send()
        for k in (1, 3, 0, 2):
            stage_two(i, k).start()

    loads["mixed"].wait()

    def out_terms(c):
        grads = r.bg[:, pl.ds(pl.multiple_of(c * chunk, chunk), chunk)]
        for s in range(n):
            yield slice(s * q_cols, (s + 1) * q_cols), mm_at(grads, r.mixed_b[s])

    dp_start(0, out_terms)
    load_far.start()

    for name in BACK_INS[3:]:
        if name != "mixed":
            loads[name].wait()
    for k in range(1, n):
        heads_back(k).wait_recv()
    for c in range(parts):
        pl.when(is_mid & from_left)(lambda: far_copy(1, c, r.far_h).start())
        pl.when(is_mid & jnp.logical_not(from_left))(lambda: far_copy(0, c, r.far_h).start())

    def turn_back(grad, part):
        return (grad * r.cos_b[part, :] - pltpu.roll(grad, HD // 2, 1) * r.sin_b[part, :]).astype(BF)

    for b in range(tokens // BLK - 1, -1, -1):
        for g in range(kv_cols // HD):
            attend_back_block(
                g,
                b,
                r.q_b,
                r.k_b,
                r.v_b,
                r.m_b,
                r.lse_b,
                r.do,
                turn_back,
                r.bias,
                r.dqkv,
                r.dk_acc,
                r.dv_acc,
            )

    def scatter(s, c, to_right):
        k, slot = (0, s - 1) if to_right else (1, n - 2 - s)
        piece = pl.ds(c * part_rows, part_rows)
        return copy_to(
            r.wo.at[s, pl.ds(rows + c * part_rows, part_rows)],
            r.got.at[k, slot, piece],
            r.rs_send.at[k, slot, c],
            r.rs_recv.at[k, slot, c],
            tensor=t + 1 if to_right else t - 1,
        )

    for i in range(n - 1, -1, -1):
        s = order[i]
        here = rows_of(s)
        for first in range(0, width, 512):
            cols = slice(first, first + 512)
            term = mm_bt(r.dqkv[here, :q_cols], r.wq_b[cols, :])
            term = term + mm_bt(r.dqkv[here, q_cols : q_cols + kv_cols], r.wk_b[cols, :])
            term = term + mm_bt(r.dqkv[here, q_cols + kv_cols :], r.wv_b[cols, :])
            if i:
                r.wo[s, rows : 2 * rows, cols] = term.astype(BF)
            else:
                r.mid_b[:, cols] = term
        if i == n - 1:
            for c in range(parts):
                pl.when(t == 0)(lambda: scatter(n - 1, c, True).start())
                pl.when(t == n - 1)(lambda: scatter(0, c, False).start())

    def next_sends(i):
        for c in range(parts):

            @pl.when(t == 0)
            def _():
                scatter(i + 1, c, True).wait_send()
                scatter(i, c, True).start()

            @pl.when(t == n - 1)
            def _():
                scatter(n - 2 - i, c, False).wait_send()
                scatter(n - 1 - i, c, False).start()

    def pass_on(index, near):
        for c in range(parts):
            piece = pl.ds(c * part_rows, part_rows)
            for to_right in (True, False):
                s = index if to_right else n - 1 - index
                way = 0 if to_right else 1
                has_source = t > 0 if to_right else t < n - 1
                now = from_left == (to_right == near)

                @pl.when(has_source & now & (s > t if to_right else s < t))
                def _():
                    scatter(s, c, to_right).wait_recv()
                    term = r.wo.at[s, pl.ds(rows + c * part_rows, part_rows)]
                    term[...] = (term[...].astype(F32) + r.got[way, index - 1, piece].astype(F32)).astype(BF)
                    scatter(s, c, to_right).start()

    def take_own():
        for to_right in (True, False):
            way = 0 if to_right else 1
            has_source = t > 0 if to_right else t < n - 1
            for index in range(1, n):
                s = index if to_right else n - 1 - index

                @pl.when(has_source & (s == t))
                def _():
                    for c in range(parts):
                        scatter(s, c, to_right).wait_recv()
                    r.mid_b[...] += r.got[way, index - 1].astype(F32)

    for copy in load_x:
        copy.wait()

    def project_terms(c):
        cols = pl.ds(pl.multiple_of(c * chunk, chunk), chunk)
        normed = r.wo[:, 0:rows, cols].reshape(tokens, chunk)
        for first in range(0, all_cols, 512):
            part = slice(first, first + 512)
            yield part, mm_at(normed, r.dqkv[:, part])

    def far_on():
        for i in range(2):
            for c in range(parts):
                piece = pl.ds(c * part_rows, part_rows)

                @pl.when(is_mid & (from_left == (i == 0)))
                def _():
                    far_copy(i, c).wait_recv()
                    total = r.far_land[piece].astype(F32) + r.bg[piece].astype(F32)
                    r.far_land[piece] = total.astype(BF)
                    far_copy(i, c).start()

    for k in range(1, n):
        heads_back(k).wait_send()
    for k in range(2):
        late_stage(2 * k + 1).wait_recv()
        for copy in load_two[2, k]:
            copy.start()
    dp_start(1, project_terms)
    start_ffn_three(2)
    start_three(0)
    load_far.wait()
    next_sends(2)
    pass_on(3, True)
    start_three(1)
    for i in (4, 5):
        late_stage(i).start()
    far_on()
    next_sends(1)
    pass_on(3, False)
    pass_on(2, True)

    def out_piece(k):
        s = lax.rem(t + k, n)
        return copy_to(r.mg.at[s], r.zr.at[k - 1], r.z_send.at[k - 1], r.z_recv.at[k - 1], tensor=s)

    per_half = n // 2
    for k in range(2):
        total = final_half(0, k)
        for i in range(per_half):
            s = k * per_half + i
            value = total[:, i * q_cols : (i + 1) * q_cols]
            r.mg[s] = value.astype(BF)

            @pl.when(s == t)
            def _():
                r.out_grad[...] = value

    for k in range(1, n):
        out_piece(k).start()
    mine = pl.ds(pl.multiple_of(d * chunk, chunk), chunk)
    size = all_cols // 2
    gain_terms = jnp.zeros((8, chunk), F32)
    for k in range(2):
        value = final_half(1, k)
        r.project_grad[:, k * size : (k + 1) * size] = value
        weight = r.wq_b[mine, :] if k == 0 else jnp.concatenate([r.wk_b[mine, :], r.wv_b[mine, :]], axis=1)
        gain_terms = gain_terms + lax.dot_general(
            jnp.ones((8, size), F32),
            value * weight.astype(F32),
            (((1,), (1,)), ((), ())),
            precision=lax.Precision.HIGHEST,
            preferred_element_type=F32,
        )
    r.gain_st[8, 0:8, :] = gain_terms
    total = r.gain_st[d, 0:8]
    for mask in range(1, 8):
        gain_along_dp(mask).wait_recv()
        total = total + r.gain_dp[mask - 1]
    r.gain_st[8, 8:16, :] = total

    def gain_along_line(k):
        s = lax.rem(t + k, n)
        return copy_to(r.gain_st.at[8], r.gain_line.at[k - 1], r.gl_send.at[k - 1], r.gl_recv.at[k - 1], tensor=s)

    for k in range(1, n):
        gain_along_line(k).start()
    take_own()
    for first in range(0, rows, 64):
        part = slice(first, first + 64)
        back, unused = norm_back_part(r.mid_b[part, :], r.hid_b[part, :].astype(F32), r.gain_a)
        r.input_grad[part, :] = (r.fi_b[part, :] + back).astype(BF)
    for k in range(1, n):
        out_piece(k).wait_recv()
        r.out_grad[...] += r.zr[k - 1].astype(F32)
    total = r.gain_st[8]
    for k in range(1, n):
        gain_along_line(k).wait_recv()
        total = total + r.gain_line[k - 1]
    r.gain_grad[0:1, :] = total[0:1] / r.gain_a[:, mine].astype(F32)
    r.gain_grad[1:2, :] = jnp.sum(total[8:16], axis=0, keepdims=True)
    for k in range(1, n):
        gain_along_line(k).wait_send()
    for mask in range(1, 8):
        gain_along_dp(mask).wait_send()

    for k in range(1, n):
        out_piece(k).wait_send()
    for i in range(6):
        late_stage(i).wait_send()
    for i in (0, 2, 4, 5):
        late_stage(i).wait_recv()
    for i, last in ((0, 0), (1, n - 1)):

        @pl.when(t == last)
        def _():
            for c in range(parts):
                far_copy(i, c).wait_recv()

        @pl.when(is_mid)
        def _():
            for c in range(parts):
                far_copy(i, c).wait_send()

    @pl.when(is_mid)
    def _():
        r.far_land[...] = jnp.zeros_like(r.far_land)

    keep_far = pltpu.make_async_copy(r.far_land, r.far_add, r.far_sem.at[0])
    keep_far.start()
    keep_far.wait()
    for w in range(3):
        for k in range(2):
            ffn_three(w, k).wait()
    for i in range(2):
        for k in range(4):
            stage_two(i, k).wait_send()
        for k in range(2):
            stage_three(i, k).wait_send()
    for s in range(n):
        for to_right in (True, False):
            goes_on = t < n - 1 if to_right else t > 0

            @pl.when(goes_on & (s > t if to_right else s < t) & (is_mid | (s == (t + 1 if to_right else t - 1))))
            def _():
                for c in range(parts):
                    scatter(s, c, to_right).wait_send()


def back_call(n, arrays, gains, bias, x_all, w_out_all, totals, twos, late, far):
    rows, width = arrays["hid"].shape
    q_cols, kv_cols = arrays["q"].shape[1], arrays["k"].shape[1]
    all_cols = q_cols + 2 * kv_cols
    tokens = n * rows
    chunk = width // 8
    parts = rows // 64
    any_spec = pl.BlockSpec(memory_space=pl.ANY)
    vmem_spec = pl.BlockSpec(memory_space=pltpu.VMEM)
    dma = pltpu.SemaphoreType.DMA
    shape = jax.ShapeDtypeStruct
    return pl.pallas_call(
        functools.partial(back_kernel, n),
        out_shape=[
            shape((rows, width), BF),
            shape((chunk, all_cols), F32),
            shape((chunk, q_cols), F32),
            shape((8, chunk), F32),
            shape((3, 2, chunk, width // 2), BF),
            shape((6, chunk, width // 2), BF),
            shape((rows, width), BF),
        ],
        in_specs=[any_spec] * len(BACK_INS) + [vmem_spec] * 2 + [any_spec] * 6,
        out_specs=[vmem_spec] * 4 + [any_spec] * 3,
        scratch_shapes=[pltpu.VMEM(arrays[name].shape, arrays[name].dtype) for name in BACK_INS]
        + [
            pltpu.VMEM((n, q_cols, width), BF),
            pltpu.VMEM((rows, width), BF),
            pltpu.VMEM((n, rows, q_cols), BF),
            pltpu.VMEM((tokens, q_cols), BF),
            pltpu.VMEM((tokens, all_cols), BF),
            pltpu.VMEM((tokens, kv_cols), F32),
            pltpu.VMEM((tokens, kv_cols), F32),
            pltpu.VMEM((2, n - 1, rows, width), BF),
            pltpu.VMEM((4, chunk, n * q_cols), BF),
            pltpu.VMEM((4, chunk, all_cols), BF),
            pltpu.VMEM((4, chunk, n * q_cols // 2), BF),
            pltpu.VMEM((4, chunk, all_cols // 2), BF),
            pltpu.VMEM((2, chunk, n * q_cols // 2), BF),
            pltpu.VMEM((2, chunk, all_cols // 2), BF),
            pltpu.VMEM((3, 2, chunk, width // 2), BF),
            pltpu.VMEM((2, chunk, n * q_cols), BF),
            pltpu.VMEM((n - 1, chunk, q_cols), BF),
            pltpu.VMEM((9, 16, chunk), F32),
            pltpu.VMEM((7, 8, chunk), F32),
            pltpu.VMEM((n - 1, 16, chunk), F32),
            pltpu.VMEM((rows, width), BF),
            dma((len(BACK_INS),)),
            dma((n,)),
            dma((n,)),
            dma((2, 3, 2)),
            dma((n - 1,)),
            dma((n - 1,)),
            dma((3, 2)),
            dma((3, 2)),
            dma((2, 4)),
            dma((2, 4)),
            dma((2, 4)),
            dma((2, 4)),
            dma((2, 2)),
            dma((2, 2)),
            dma((n - 1,)),
            dma((n - 1,)),
            dma((2, n - 1, parts)),
            dma((2, n - 1, parts)),
            dma((7,)),
            dma((7,)),
            dma((n - 1,)),
            dma((n - 1,)),
            dma((6,)),
            dma((6,)),
            dma((2, 2)),
            dma((1,)),
            dma((2, parts)),
            dma((2, parts)),
        ],
        compiler_params=pltpu.CompilerParams(
            vmem_limit_bytes=64 * 1024 * 1024 - 65536, collective_id=3, has_side_effects=True
        ),
        cost_estimate=pl.CostEstimate(flops=1 << 36, bytes_accessed=1 << 26, transcendentals=0),
        name="back",
    )(*[arrays[name] for name in BACK_INS], gains, bias, x_all, w_out_all, totals, twos, late, far)


def finish_kernel(tot, two, near, late, three, proj, out, ig, base, far, gate, up, down, wq, wk, wv, wo, ig_out, oo_out):
    def total(w):
        other = (two[0, 0], near[0], late[0])[w]
        return tot[w, 0].astype(F32) + other.astype(F32) + three[w, 0].astype(F32)

    down[...] = total(0).T
    gate[...] = total(1)
    up[...] = total(2)
    wo[...] = out[...].T
    ig_out[...] = ig[...]
    oo_out[...] = (base[...] + far[...].astype(F32)).astype(BF)

    @pl.when(pl.program_id(0) == 0)
    def _():
        wq[...] = proj[...]

    @pl.when(pl.program_id(0) == 1)
    def _():
        wk[...] = proj[:, : wk.shape[1]]
        wv[...] = proj[:, wk.shape[1] :]


def finish_call(totals, twos, late, threes, project_grad, out_grad, input_grad, base, far):
    chunk, half = totals.shape[2:]
    rows, width = input_grad.shape
    all_cols, q_cols = project_grad.shape[1], out_grad.shape[1]
    kv_cols = (all_cols - q_cols) // 2
    shape, spec = jax.ShapeDtypeStruct, pl.BlockSpec
    side = lambda k: (0, k)
    below = lambda k: (k, 0)
    fixed = lambda k: (0, 0)
    return pl.pallas_call(
        finish_kernel,
        grid=(2,),
        in_specs=[
            spec((3, 1, chunk, half), lambda k: (0, 2 * k, 0, 0)),
            spec((1, 1, chunk, half), lambda k: (0, 2 * k, 0, 0)),
            spec((1, chunk, half), lambda k: (4 + k, 0, 0)),
            spec((1, chunk, half), lambda k: (2 * k, 0, 0)),
            spec((3, 1, chunk, half), lambda k: (0, k, 0, 0)),
            spec((chunk, all_cols // 2), side),
            spec((chunk, q_cols // 2), side),
            spec((rows, width // 2), side),
            spec((rows, width // 2), side),
            spec((rows, width // 2), side),
        ],
        out_specs=[
            spec((chunk, half), side),
            spec((chunk, half), side),
            spec((half, chunk), below),
            spec((chunk, q_cols), fixed),
            spec((chunk, kv_cols), fixed),
            spec((chunk, kv_cols), fixed),
            spec((q_cols // 2, chunk), below),
            spec((rows, width // 2), side),
            spec((rows, width // 2), side),
        ],
        out_shape=[
            shape((chunk, 2 * half), F32),
            shape((chunk, 2 * half), F32),
            shape((2 * half, chunk), F32),
            shape((chunk, q_cols), F32),
            shape((chunk, kv_cols), F32),
            shape((chunk, kv_cols), F32),
            shape((q_cols, chunk), F32),
            shape((rows, width), BF),
            shape((rows, width), BF),
        ],
        compiler_params=pltpu.CompilerParams(vmem_limit_bytes=VMEM_LIMIT),
        name="finish",
    )(totals, twos, late, late, threes, project_grad, out_grad, input_grad, base, far)


def ffn_kernel(
    n,
    own_ref,
    cot_ref,
    wg_hbm,
    wu_hbm,
    wd_hbm,
    h_out,
    gg_out,
    ug_out,
    n_out,
    fb_out,
    fi_out,
    wg_ref,
    wu_ref,
    wd_ref,
    n_buf,
    c_buf,
    st_buf,
    fi_part,
    got,
    fb_acc,
    fi_acc,
    w_sem,
    c_sem,
    st_sem,
    n_sem,
    ag_send,
    ag_recv,
    rs_send,
    rs_recv,
):
    t, d = lax.axis_index("tensor"), lax.axis_index("dp")
    rows, width = own_ref.shape
    units = wg_ref.shape[1]
    tile = min(512, units)
    tiles = units // tile
    parts = rs_send.shape[2]
    part_rows = rows // parts
    order = arrival_order(t, n)
    is_mid = (t > 0) & (t < n - 1)

    def load_weights(j):
        cols = pl.ds(j * tile, tile)
        return [
            pltpu.make_async_copy(wg_hbm.at[:, cols], wg_ref.at[:, cols], w_sem.at[0, j]),
            pltpu.make_async_copy(wu_hbm.at[:, cols], wu_ref.at[:, cols], w_sem.at[1, j]),
            pltpu.make_async_copy(wd_hbm.at[cols, :], wd_ref.at[cols, :], w_sem.at[2, j]),
        ]

    def load_cot(i):
        return pltpu.make_async_copy(cot_ref.at[order[i]], c_buf.at[i % 2], c_sem.at[i % 2])

    def gather(s, to_right, src=None):
        return copy_to(
            n_buf.at[s] if src is None else src,
            n_buf.at[s],
            ag_send.at[0 if to_right else 1, s],
            ag_recv.at[s],
            tensor=t + 1 if to_right else t - 1,
        )

    def keep_rows(i):
        return pltpu.make_async_copy(own_ref if i == 0 else n_buf.at[order[i]], n_out.at[order[i]], n_sem.at[i])

    def scatter(s, c, to_right):
        k, slot = (0, s - 1) if to_right else (1, n - 2 - s)
        piece = pl.ds(c * part_rows, part_rows)
        return copy_to(
            fi_part.at[s, piece],
            got.at[k, slot, piece],
            rs_send.at[k, slot, c],
            rs_recv.at[k, slot, c],
            tensor=t + 1 if to_right else t - 1,
        )

    for copy in load_weights(0):
        copy.start()
    load_cot(0).start()
    group_barrier([], n, d, t)
    pl.when(t < n - 1)(lambda: gather(t, True, own_ref).start())
    pl.when(t > 0)(lambda: gather(t, False, own_ref).start())
    for j in range(1, tiles):
        for copy in load_weights(j):
            copy.start()
    keep_rows(0).start()

    def arrive(i):
        s = order[i]
        gather(s, True).wait_recv()
        pl.when((s < t) & (t < n - 1))(lambda: gather(s, True).start())
        pl.when((s > t) & (t > 0))(lambda: gather(s, False).start())
        keep_rows(i).start()

    def stage_out(i):
        return [
            pltpu.make_async_copy(
                st_buf.at[i % 2, k, :, pl.ds(0, out.shape[2])], out.at[order[i]], st_sem.at[k, i % 2]
            )
            for k, out in enumerate((h_out, gg_out, ug_out, fb_out))
        ]

    for i in range(n):
        s = order[i]
        slot = i % 2
        if i == 1:
            arrive(1)
            if n > 2:
                pl.when(is_mid)(functools.partial(arrive, 2))
        elif i > 1:
            pl.when(jnp.logical_not(is_mid))(functools.partial(arrive, i))
        if i + 1 < n:
            load_cot(i + 1).start()
        load_cot(i).wait()
        if i >= 2:
            for copy in stage_out(i - 2):
                copy.wait()
        x_ref = own_ref if i == 0 else n_buf.at[s]
        fb_acc[...] = jnp.zeros_like(fb_acc)
        fi_acc[...] = jnp.zeros_like(fi_acc)

        def one_tile(j, carry):
            if i == 0:
                for copy in load_weights(j):
                    copy.wait()
            if 2 <= i < n - 1:
                pl.when(is_mid & (j == tiles // 2))(functools.partial(arrive, i + 1))
            cols = pl.ds(pl.multiple_of(j * tile, tile), tile)
            x = x_ref[...]
            wg, wu, wd = wg_ref[:, cols], wu_ref[:, cols], wd_ref[cols, :]
            gate = mm(x, wg)
            up = mm(x, wu)
            act_grad = mm_bt(c_buf[slot], wd)
            sig = jax.nn.sigmoid(gate)
            silu = gate * sig
            h = (silu * up).astype(BF)
            gg = (act_grad * up * (sig * (1.0 + gate * (1.0 - sig)))).astype(BF)
            ug = (act_grad * silu).astype(BF)
            for k, value in enumerate((h, gg, ug)):
                st_buf[slot, k, :, cols] = value
            for k in range(0, width, 512):
                piece = slice(k, k + 512)
                fb_acc[:, piece] += mm(h, wd_ref[cols, piece])
                fi_acc[:, piece] += mm_bt(gg, wg_ref[piece, cols]) + mm_bt(ug, wu_ref[piece, cols])
            return carry

        lax.fori_loop(0, tiles, one_tile, 0)
        st_buf[slot, 3, :, :width] = fb_acc[...].astype(BF)
        for copy in stage_out(i):
            copy.start()
        if i == 0:
            fi_out[...] = fi_acc[...]
        else:
            fi_part[s] = fi_acc[...].astype(BF)

            @pl.when(t == 0)
            def _():
                for c in range(parts):
                    scatter(i, c, True).start()

            @pl.when(t == n - 1)
            def _():
                for c in range(parts):
                    scatter(n - 1 - i, c, False).start()

    def pass_on(index, c):
        piece = pl.ds(c * part_rows, part_rows)
        for to_right in (True, False):
            s = index if to_right else n - 1 - index
            k = 0 if to_right else 1
            has_source = t > 0 if to_right else t < n - 1
            beyond = s > t if to_right else s < t

            @pl.when(has_source & beyond)
            def _():
                scatter(s, c, to_right).wait_recv()
                total = fi_part[s, piece].astype(F32) + got[k, index - 1, piece].astype(F32)
                fi_part[s, piece] = total.astype(BF)
                scatter(s, c, to_right).start()

            @pl.when(has_source & (s == t))
            def _():
                scatter(s, c, to_right).wait_recv()
                fi_out[piece] += got[k, index - 1, piece].astype(F32)

    for i in range(max(0, n - 2), n):
        for copy in stage_out(i):
            copy.wait()
    for index in range(1, n):
        for c in range(parts):
            pass_on(index, c)
    for i in range(n):
        keep_rows(i).wait()
    for s in range(n):
        for to_right in (True, False):
            goes_on = t < n - 1 if to_right else t > 0

            @pl.when(goes_on & (s <= t if to_right else s >= t))
            def _():
                gather(s, to_right).wait_send()

            @pl.when(goes_on & (s > t if to_right else s < t))
            def _():
                for c in range(parts):
                    scatter(s, c, to_right).wait_send()


def ffn_call(n, own_rows, cot_all, w_gate, w_up, w_down):
    rows, width = own_rows.shape
    units = w_gate.shape[1]
    tile = min(512, units)
    tiles = units // tile
    parts = max(1, rows // 64)
    tall = jax.ShapeDtypeStruct((n, rows, units), BF)
    wide = jax.ShapeDtypeStruct((n, rows, width), BF)
    any_spec = pl.BlockSpec(memory_space=pl.ANY)
    vmem_spec = pl.BlockSpec(memory_space=pltpu.VMEM)
    dma = pltpu.SemaphoreType.DMA
    return pl.pallas_call(
        functools.partial(ffn_kernel, n),
        out_shape=[tall, tall, tall, wide, wide, jax.ShapeDtypeStruct((rows, width), F32)],
        in_specs=[vmem_spec] + [any_spec] * 4,
        out_specs=[any_spec] * 5 + [vmem_spec],
        scratch_shapes=[
            pltpu.VMEM((width, units), BF),
            pltpu.VMEM((width, units), BF),
            pltpu.VMEM((units, width), BF),
            pltpu.VMEM((n, rows, width), BF),
            pltpu.VMEM((2, rows, width), BF),
            pltpu.VMEM((2, 4, rows, max(units, width)), BF),
            pltpu.VMEM((n, rows, width), BF),
            pltpu.VMEM((2, n - 1, rows, width), BF),
            pltpu.VMEM((rows, width), F32),
            pltpu.VMEM((rows, width), F32),
            dma((3, tiles)),
            dma((2,)),
            dma((4, 2)),
            dma((n,)),
            dma((2, n)),
            dma((n,)),
            dma((2, n - 1, parts)),
            dma((2, n - 1, parts)),
        ],
        compiler_params=pltpu.CompilerParams(
            vmem_limit_bytes=63 * 1024 * 1024, collective_id=4, has_side_effects=True
        ),
        cost_estimate=pl.CostEstimate(
            flops=12 * n * rows * width * units, bytes_accessed=6 * width * units, transcendentals=0
        ),
        name="ffn_plain",
    )(own_rows, cot_all, w_gate, w_up, w_down)


MID_NAMES = (
    ("own", "cot_in", "wg_h", "wu_h", "wd_h", "middle_h"),
    ("cot", "h_out", "tot", "two", "late", "fi_out", "base", "far"),
    ("wg", "wu", "wd", "n_buf", "gu", "h_st", "c_buf", "part", "land", "acc"),
    ("w_sem", "own_sem", "c_sem", "h_sem", "re_sem", "tot_sem", "out_sem", "ready"),
    ("ag_send", "ag_recv", "ct_send", "ct_recv", "rs_send", "rs_recv"),
    ("one_send", "one_recv", "two_send", "two_recv", "late_sem", "far_sem"),
)


def middle_kernel(n, *refs):
    names = [name for group in MID_NAMES for name in group]
    r = types.SimpleNamespace(**dict(zip(names, refs, strict=True)))
    t, d = lax.axis_index("tensor"), lax.axis_index("dp")
    rows, width = r.own.shape
    units = r.wg.shape[1]
    tokens = n * rows
    tile = 512
    tiles = units // tile
    parts = r.rs_send.shape[3]
    part_rows = rows // parts
    order = arrival_order(t, n)
    is_mid = (t > 0) & (t < n - 1)
    is_end = jnp.logical_not(is_mid)
    core, x, y = lax.rem(d, 2), lax.rem(d // 2, 2), d // 4
    chunk = width // 8
    halves = units // 2

    def load_weights(j):
        cols = pl.ds(j * tile, tile)
        return [
            pltpu.make_async_copy(r.wg_h.at[:, cols], r.wg.at[:, cols], r.w_sem.at[0, j]),
            pltpu.make_async_copy(r.wu_h.at[:, cols], r.wu.at[:, cols], r.w_sem.at[1, j]),
            pltpu.make_async_copy(r.wd_h.at[cols, :], r.wd.at[cols, :], r.w_sem.at[2, j]),
        ]

    def line(buf, send_sem, recv_sem, s, to_right, src=None):
        return copy_to(
            buf.at[s] if src is None else src,
            buf.at[s],
            send_sem.at[0 if to_right else 1, s],
            recv_sem.at[s],
            tensor=t + 1 if to_right else t - 1,
        )

    gather = functools.partial(line, r.n_buf, r.ag_send, r.ag_recv)
    gather_cot = functools.partial(line, r.cot, r.ct_send, r.ct_recv)
    own_rows = pltpu.make_async_copy(r.own, r.n_buf.at[t], r.own_sem.at[0])

    def load_cot(i):
        return pltpu.make_async_copy(r.cot.at[order[i]], r.c_buf.at[i % 2], r.c_sem.at[i % 2])

    def keep_h(i):
        return pltpu.make_async_copy(r.h_st, r.h_out.at[order[i]], r.h_sem.at[0])

    def scatter(q, s, c, to_right):
        k, index = (0, s - 1) if to_right else (1, n - 2 - s)
        piece = pl.ds(c * part_rows, part_rows)
        to = t + 1 if to_right else t - 1
        slot = s if to_right else jnp.where(to == s, n, s)
        return copy_to(
            r.part.at[q, s, piece],
            r.land.at[q, slot, piece],
            r.rs_send.at[q, k, index, c],
            r.rs_recv.at[q, k, index, c],
            tensor=to,
        )

    own_rows.start()
    for copy in load_weights(0):
        copy.start()
    load_cot(0).start()
    group_barrier([1, 2, 4], n, d, t)
    own_rows.wait()
    pl.when(t < n - 1)(lambda: gather(t, True).start())
    pl.when(t > 0)(lambda: gather(t, False).start())
    for j in range(1, tiles):
        for copy in load_weights(j):
            copy.start()

    def arrive(which, i):
        s = order[i]
        which(s, True).wait_recv()
        pl.when((s < t) & (t < n - 1))(lambda: which(s, True).start())
        pl.when((s > t) & (t > 0))(lambda: which(s, False).start())

    def end_sends(q, i, chunks):
        @pl.when(t == 0)
        def _():
            for c in chunks:
                scatter(q, i, c, True).start()

        @pl.when(t == n - 1)
        def _():
            for c in chunks:
                scatter(q, n - 1 - i, c, False).start()

    def forward(i):
        s = order[i]
        if i:
            keep_h(i - 1).wait()
        r.acc[...] = jnp.zeros_like(r.acc)

        def one_tile(j, carry):
            if i == 0:
                for copy in load_weights(j):
                    copy.wait()
            if 2 <= i < n - 1:
                pl.when(is_mid & (j == tiles // 2))(functools.partial(arrive, gather, i + 1))
            cols = pl.ds(pl.multiple_of(j * tile, tile), tile)
            rows_in = r.n_buf[s]
            gate = mm(rows_in, r.wg[:, cols])
            up = mm(rows_in, r.wu[:, cols])
            sig = jax.nn.sigmoid(gate)
            silu = gate * sig
            h = (silu * up).astype(BF)
            r.h_st[:, cols] = h
            r.gu[0, s, :, cols] = (up * (sig * (1.0 + gate * (1.0 - sig)))).astype(BF)
            r.gu[1, s, :, cols] = silu.astype(BF)
            for k in range(0, width, 512):
                piece = slice(k, k + 512)
                r.acc[:, piece] += mm(h, r.wd[cols, piece])
            return carry

        lax.fori_loop(0, tiles, one_tile, 0)
        keep_h(i).start()
        r.part[0, s] = r.acc[...].astype(BF)
        if 0 < i < n - 1:
            end_sends(0, i, range(parts))

    def backward(i, chunks):
        s = order[i]
        r.acc[...] = jnp.zeros_like(r.acc)
        load_cot(i).wait()

        def one_tile(j, carry):
            cols = pl.ds(pl.multiple_of(j * tile, tile), tile)
            act_grad = mm_bt(r.c_buf[i % 2], r.wd[cols, :])
            gg = (act_grad * r.gu[0, s, :, cols].astype(F32)).astype(BF)
            ug = (act_grad * r.gu[1, s, :, cols].astype(F32)).astype(BF)
            r.gu[0, s, :, cols] = gg
            r.gu[1, s, :, cols] = ug
            for k in range(0, width, 512):
                piece = slice(k, k + 512)
                r.acc[:, piece] += mm_bt(gg, r.wg[piece, cols]) + mm_bt(ug, r.wu[piece, cols])
            return carry

        lax.fori_loop(0, tiles, one_tile, 0)
        r.part[1, s] = r.acc[...].astype(BF)
        if i:
            end_sends(1, i, chunks)

    from_left = t * 2 < n - 1

    def pass_on(q, index, near):
        for c in range(parts):
            piece = pl.ds(c * part_rows, part_rows)
            for to_right in (True, False):
                s = index if to_right else n - 1 - index
                has_source = t > 0 if to_right else t < n - 1
                now = from_left == (to_right == near)

                @pl.when(has_source & now & (s > t if to_right else s < t))
                def _():
                    scatter(q, s, c, to_right).wait_recv()
                    total = r.part[q, s, piece].astype(F32) + r.land[q, s, piece].astype(F32)
                    r.part[q, s, piece] = total.astype(BF)
                    scatter(q, s, c, to_right).start()

    everything = range(parts)
    forward(0)
    load_cot(1).start()
    backward(0, everything)
    arrive(gather, 1)
    pl.when(is_mid)(functools.partial(arrive, gather, 2))
    pl.when(is_mid)(lambda: load_cot(2).start())
    forward(1)
    backward(1, everything)
    pl.when(is_end)(functools.partial(arrive, gather, 2))
    forward(2)
    @pl.when(is_mid)
    def _():
        gather_cot(t - 1, True).start()
        gather_cot(t + 1, False).start()

    pl.when(is_mid)(functools.partial(backward, 2, everything))
    pl.when(is_end)(functools.partial(arrive, gather, 3))
    forward(3)

    @pl.when(is_end)
    def _():
        arrive(gather_cot, 2)
        load_cot(2).start()
        backward(2, everything)

    arrive(gather_cot, 3)
    load_cot(3).start()
    backward(3, (0, 1))
    keep_h(3).wait()

    first, second = pl.ds(0, tokens), pl.ds(tokens, tokens)
    reload = []
    for k, (src, dst, base) in enumerate(((r.h_out, r.wg, 0), (r.cot, r.wu, tokens))):
        for s in range(n):
            place = dst.at[pl.ds(base + s * rows, rows)]
            reload.append(pltpu.make_async_copy(src.at[s], place, r.re_sem.at[k, s]))
    for copy in reload:
        copy.start()
    pl.semaphore_signal(r.ready, inc=1, device_id={"dp": d ^ 1}, device_id_type=pl.DeviceIdType.MESH)
    pl.semaphore_wait(r.ready, 1)

    def block(w, j):
        if w == 2:
            return r.wg.at[pl.ds(tokens + j * chunk, chunk)]
        return r.wd.at[pl.ds((w * 4 + j) * chunk, chunk)]

    def lhs(w, j, who):
        cols = pl.ds(pl.multiple_of((2 * j + who) * chunk, chunk), chunk)
        if w == 0:
            return r.wu[second, cols]
        return r.n_buf[:, :, cols].reshape(tokens, chunk)

    def rhs(w, part):
        if w == 0:
            return r.wg[first, part]
        return r.gu[w - 1, :, :, part].reshape(tokens, part.stop - part.start)

    def stage_one(w, j):
        return copy_to(r.c_buf.at[lax.rem(j, 2)], block(w, j), r.one_send.at[w, j], r.one_recv.at[w, j], dp=d ^ 1)

    def stage_two(w, k):
        j = (2 * y + 1 - x, 2 * (1 - y) + 1 - x, 2 * (1 - y) + x, 2 * (1 - y) + 1 - x)[k]
        cols = pl.ds((k // 2) * halves, halves)
        return copy_to(
            block(w, j).at[:, cols], r.two.at[w, k], r.two_send.at[w, k], r.two_recv.at[w, k], dp=d ^ (2, 2, 4, 4)[k]
        )

    def keep_late(i):
        k = i if i < 4 else 2 * (i - 4)
        j = (2 * y + 1 - x, 2 * (1 - y) + 1 - x, 2 * (1 - y) + x, 2 * (1 - y) + 1 - x)[k]
        cols = pl.ds((k // 2) * halves, halves)
        return pltpu.make_async_copy(block(2 if i < 4 else 1, j).at[:, cols], r.late.at[i], r.late_sem.at[i])

    def leave(w, k):
        if w == 0 or (w == 1 and k % 2):
            return stage_two(w, k)
        return keep_late(k if w == 2 else 4 + k // 2)

    def keep_total(w, k):
        j = (2 * y + x, 2 * (1 - y) + x, 2 * y + x, 2 * y + 1 - x)[k]
        cols = pl.ds((k // 2) * halves, halves)
        return pltpu.make_async_copy(block(w, j).at[:, cols], r.tot.at[w, k], r.tot_sem.at[w, k])

    for w in range(3):
        if w == 0:
            for copy in reload:
                copy.wait()

        def give(j, carry):
            @pl.when(j >= 2)
            def _():
                stage_one(w, j - 2).wait_send()

            grads = lhs(w, j, 1 - core)
            for k in range(0, units, 512):
                part = slice(k, k + 512)
                r.c_buf[lax.rem(j, 2), :, part] = mm_at(grads, rhs(w, part)).astype(BF)
            stage_one(w, j).start()
            return carry

        def keep(j, carry):
            stage_one(w, j).wait_recv()
            grads = lhs(w, j, core)
            for k in range(0, units, 512):
                part = slice(k, k + 512)
                piece = block(w, j).at[:, part]
                piece[...] = (piece[...].astype(F32) + mm_at(grads, rhs(w, part))).astype(BF)
            return carry

        lax.fori_loop(0, 4, give, 0)
        if w == 0:
            end_sends(1, 3, (2,))
        lax.fori_loop(0, 4, keep, 0)
        if w == 0:
            end_sends(1, 3, (3,))
        for j in (2, 3):
            stage_one(w, j).wait_send()
        for k in range(4):
            leave(w, k).start()
            keep_total(w, k).start()
        if w == 0:
            pass_on(0, 2, True)
        if w == 1:
            end_sends(0, n - 1, everything)
    def total_of(q):
        r.acc[...] += r.part[q, t].astype(F32)
        for to_right in (True, False):
            has_source = (t > 0 if to_right else t < n - 1) if q else is_mid

            @pl.when(has_source)
            def _():
                for s in range(n):

                    @pl.when(s == t)
                    def _():
                        for c in range(parts):
                            scatter(q, s, c, to_right).wait_recv()

                slot = t if to_right else n
                r.acc[...] += r.land[q, slot].astype(F32)

    add_middle = pltpu.make_async_copy(r.middle_h, r.acc, r.out_sem.at[0])
    add_middle.start()
    add_middle.wait()
    total_of(0)
    keep_base = pltpu.make_async_copy(r.acc, r.base, r.out_sem.at[0])
    keep_base.start()
    pass_on(1, 2, True)
    pass_on(1, 3, True)
    pass_on(1, 3, False)
    keep_base.wait()

    for to_right in (True, False):
        s = n - 1 if to_right else 0

        @pl.when(is_mid & (from_left == to_right))
        def _():
            for c in range(parts):
                scatter(0, s, c, to_right).wait_recv()
            r.part[0, s] = (r.part[0, s].astype(F32) + r.land[0, s].astype(F32)).astype(BF)

    keep_far = [pltpu.make_async_copy(r.part.at[0, s], r.far.at[i], r.far_sem.at[i]) for i, s in ((0, 0), (1, n - 1))]
    for copy in keep_far:
        copy.start()

    r.acc[...] = jnp.zeros_like(r.acc)
    total_of(1)
    keep_fi = pltpu.make_async_copy(r.acc, r.fi_out, r.out_sem.at[1])
    keep_fi.start()
    keep_fi.wait()
    for copy in keep_far:
        copy.wait()
    for w in range(3):
        for k in range(4):
            keep_total(w, k).wait()
            leave(w, k).wait()
    for s in range(n):
        for to_right in (True, False):
            goes_on = t < n - 1 if to_right else t > 0

            @pl.when(goes_on & (s <= t if to_right else s >= t))
            def _():
                gather(s, to_right).wait_send()

            @pl.when(goes_on & (s < t if to_right else s > t))
            def _():
                gather_cot(s, to_right).wait_send()

            @pl.when(goes_on & (s > t if to_right else s < t))
            def _():
                for c in range(parts):
                    scatter(1, s, c, to_right).wait_send()
                    if 0 < s < n - 1:
                        scatter(0, s, c, to_right).wait_send()
                    else:
                        pl.when(is_end)(lambda: scatter(0, s, c, to_right).wait_send())


def middle_call(n, own_rows, cot_part, w_gate, w_up, w_down, middle):
    rows, width = own_rows.shape
    units = w_gate.shape[1]
    parts = rows // 64
    shape = jax.ShapeDtypeStruct
    wide = shape((n, rows, width), BF)
    piece = (4, width // 8, units // 2)
    any_spec = pl.BlockSpec(memory_space=pl.ANY)
    dma = pltpu.SemaphoreType.DMA
    return pl.pallas_call(
        functools.partial(middle_kernel, n),
        out_shape=[wide, shape((n, rows, units), BF), shape((3, *piece), BF), shape((2, *piece), BF)]
        + [shape((6, *piece[1:]), BF), shape((rows, width), F32), shape((rows, width), F32)]
        + [shape((2, rows, width), BF)],
        in_specs=[any_spec] * 6,
        out_specs=[any_spec] * 8,
        input_output_aliases={1: 0},
        scratch_shapes=[
            pltpu.VMEM((width, units), BF),
            pltpu.VMEM((width, units), BF),
            pltpu.VMEM((units, width), BF),
            pltpu.VMEM((n, rows, width), BF),
            pltpu.VMEM((2, n, rows, units), BF),
            pltpu.VMEM((rows, units), BF),
            pltpu.VMEM((2, rows, width), BF),
            pltpu.VMEM((2, n, rows, width), BF),
            pltpu.VMEM((2, n + 1, rows, width), BF),
            pltpu.VMEM((rows, width), F32),
            dma((3, units // 512)),
            dma((1,)),
            dma((2,)),
            dma((1,)),
            dma((2, n)),
            dma((3, 4)),
            dma((2,)),
            pltpu.SemaphoreType.REGULAR,
            dma((2, n)),
            dma((n,)),
            dma((2, n)),
            dma((n,)),
            dma((2, 2, n - 1, parts)),
            dma((2, 2, n - 1, parts)),
            dma((3, 4)),
            dma((3, 4)),
            dma((3, 4)),
            dma((3, 4)),
            dma((6,)),
            dma((2,)),
        ],
        compiler_params=pltpu.CompilerParams(
            vmem_limit_bytes=64 * 1024 * 1024 - 65536, collective_id=1, has_side_effects=True
        ),
        cost_estimate=pl.CostEstimate(
            flops=18 * n * rows * width * units, bytes_accessed=6 * width * units, transcendentals=0
        ),
        name="middle",
    )(own_rows, cot_part, w_gate, w_up, w_down, middle)


def full_call(kernel, out_shapes, args, scratch=(), flops=0, name=None):
    spec = pl.BlockSpec(memory_space=pltpu.VMEM)
    return pl.pallas_call(
        kernel,
        out_shape=out_shapes,
        in_specs=[spec] * len(args),
        out_specs=[spec] * len(out_shapes),
        scratch_shapes=list(scratch),
        compiler_params=pltpu.CompilerParams(vmem_limit_bytes=VMEM_LIMIT),
        cost_estimate=pl.CostEstimate(flops=flops, bytes_accessed=flops // 400, transcendentals=0),
        name=name,
    )(*args)


def normalize(rows_wide, gain_wide):
    inverse = lax.rsqrt(jnp.mean(rows_wide * rows_wide, axis=-1, keepdims=True) + NORM_EPS)
    scaled_rows = rows_wide * inverse
    return scaled_rows, inverse, (scaled_rows * gain_wide).astype(BF)


def norm_back(normed_grad, scaled_rows, inverse, gain_wide):
    weighted = normed_grad * gain_wide
    return inverse * (weighted - scaled_rows * jnp.mean(weighted * scaled_rows, axis=-1, keepdims=True))


def pairs(n, bit):
    return [(i, i ^ bit) for i in range(n)]


def pick(array, index, axis):
    return lax.dynamic_index_in_dim(array, index, axis, keepdims=False)


def dp_scatter(give, keep, n_dp):
    me = lax.axis_index("dp")
    total = keep + lax.ppermute(give, "dp", pairs(n_dp, 1))
    if n_dp != 8:
        bit = 2
        while total.shape[0] > 1:
            parts = total.reshape(-1, 2, *total.shape[1:])
            mine = (me // bit) % 2
            total = pick(parts, mine, 1) + lax.ppermute(pick(parts, 1 - mine, 1), "dp", pairs(n_dp, bit))
            bit *= 2
        return total[0].astype(F32)
    x, y = (me // 2) % 2, me // 4
    cols = total.shape[-1] // 2
    parts = total.reshape(2, 2, *total.shape[1:])
    a, b = parts[..., :cols], parts[..., cols:]
    got_a = lax.ppermute(pick(a, 1 - x, 1), "dp", pairs(n_dp, 2))
    got_b = lax.ppermute(pick(b, 1 - y, 0), "dp", pairs(n_dp, 4))
    a = pick(a, x, 1) + got_a
    b = pick(b, y, 0) + got_b
    got_a = lax.ppermute(pick(a, 1 - y, 0), "dp", pairs(n_dp, 4))
    got_b = lax.ppermute(pick(b, 1 - x, 0), "dp", pairs(n_dp, 2))
    a = pick(a, y, 0).astype(F32) + got_a.astype(F32)
    b = pick(b, x, 0).astype(F32) + got_b.astype(F32)
    return jnp.concatenate([a, b], axis=-1)


def core_split(rows, n_dp):
    tokens, width = rows.shape
    core = lax.axis_index("dp") % 2
    parts = rows.reshape(tokens, n_dp // 2, 2, width // n_dp)
    return [pick(parts, c, 2).reshape(tokens, width // 2) for c in (1 - core, core)]


def grad_scatter(split_rows, cols, n_dp):
    give, keep = [
        mm_at(part, cols).astype(BF).reshape(n_dp // 2, 2 * part.shape[1] // n_dp, cols.shape[1])
        for part in split_rows
    ]
    return dp_scatter(give, keep, n_dp)


def after(value, *others):
    return lax.optimization_barrier((value, *others))[0]


def shards(n_dp, n_t, hidden_in, gain_attn, w_query, w_key, w_value, w_out, gain_ffn, w_gate, w_up, w_down, segments, parents, cotangent):
    tokens = segments.shape[0]
    own, width = hidden_in.shape
    q_cols, kv_cols, units = w_query.shape[1], w_key.shape[1], w_gate.shape[1]
    heads = q_cols // HD
    me_t = lax.axis_index("tensor")
    me_dp = lax.axis_index("dp")
    gain_attn_wide = gain_attn.astype(F32)
    gain_ffn_wide = gain_ffn.astype(F32)

    def ring(value, shift):
        return lax.ppermute(value, "tensor", [(i, (i + shift) % n_t) for i in range(n_t)])

    ancestry, depth = tree_tables(segments, parents)
    bias = jnp.where(jnp.repeat(ancestry, BLK, axis=1) > 0.5, 0.0, NEG)
    bias = jnp.concatenate([bias, jnp.broadcast_to(depth[:, None] * BLK, (depth.shape[0], HD))], axis=1)
    gains = jnp.stack([gain_attn_wide, gain_ffn_wide])
    fused = n_dp == 8 and n_t == 4 and units == width and q_cols == 2 * own and tokens * 2 == width
    x_all, cot_all, w_out_all, queries, keys, values, mixed, lse, mixed_own, middle, normed_ffn, cosine, sine = attn_call(
        n_dp, n_t, fused, hidden_in, cotangent, gains, w_query, w_key, w_value, w_out, bias
    )
    x_all = x_all.reshape(tokens, width)
    w_out_all = w_out_all.reshape(n_t * q_cols, width)
    rows_wide = hidden_in.astype(F32)
    if fused:
        unused_cot, unused_h, totals, twos, late, ffn_in_grad, base, far = middle_call(
            n_t, normed_ffn, cot_all, w_gate, w_up, w_down, middle
        )
        arrays = dict(
            fi=ffn_in_grad,
            mid=middle,
            cot=cotangent,
            hid=hidden_in,
            q=queries,
            k=keys,
            v=values,
            m=mixed,
            lse=lse,
            cos=cosine,
            sin=sine,
            mixed=mixed_own,
            wq=w_query,
            wk=w_key,
            wv=w_value,
        )
        input_grad, project_wgrad, out_grad, gain_grads, threes, late_twos, far_sum = back_call(
            n_t,
            arrays,
            gains,
            bias,
            x_all.reshape(n_t, own, width),
            w_out_all.reshape(n_t, q_cols, width),
            totals,
            twos,
            late,
            far,
        )
        w_gate_grad, w_up_grad, w_down_grad, w_query_grad, w_key_grad, w_value_grad, w_out_grad, input_grad, output = (
            finish_call(totals, twos, late_twos, threes, project_wgrad, out_grad, input_grad, base, far_sum)
        )
        gain_attn_grad, gain_ffn_grad = gain_grads[0], gain_grads[1]
    else:
        w_project = jnp.concatenate([w_query, w_key, w_value], axis=1)
        h_all, gg_all, ug_all, n_all, fb_part, ffn_in_grad = ffn_call(n_t, normed_ffn, cot_all, w_gate, w_up, w_down)
        fb_sum = lax.psum_scatter(fb_part.reshape(tokens, width), "tensor", scatter_dimension=0, tiled=True)
        output = (middle + fb_sum.astype(F32)).astype(BF)
        h_all, gg_all, ug_all = [a.reshape(tokens, units) for a in (h_all, gg_all, ug_all)]
        cot_split = core_split(cot_all.reshape(tokens, width), n_dp)
        normed_split = core_split(n_all.reshape(tokens, width), n_dp)
        w_down_grad = grad_scatter(cot_split, h_all, n_dp).T
        w_gate_grad = grad_scatter(normed_split, gg_all, n_dp)
        w_up_grad = grad_scatter(normed_split, ug_all, n_dp)

        scaled_attn, inverse_attn, _ = normalize(rows_wide, gain_attn_wide)
        scaled_ffn, inverse_ffn, _ = normalize(middle, gain_ffn_wide)
        middle_grad = cotangent.astype(F32) + norm_back(ffn_in_grad, scaled_ffn, inverse_ffn, gain_ffn_wide)
        branch_grad = middle_grad.astype(BF)
        mixed_grads = mm_bt(branch_grad, w_out_all).astype(BF).reshape(own, n_t, q_cols)
        mixed_grads = [pick(mixed_grads, (me_t + n_t - d) % n_t, 1) for d in range(n_t)]
        mixed_grads = [mixed_grads[0]] + [ring(mixed_grads[d], n_t - d) for d in range(1, n_t)]
        mixed_grad = jnp.roll(jnp.concatenate(mixed_grads, axis=0), me_t * own, axis=0)

        (project_grad,) = full_call(
            attn_bwd_kernel,
            [jax.ShapeDtypeStruct((tokens, q_cols + 2 * kv_cols), BF)],
            (queries, keys, values, mixed, lse, mixed_grad, cosine, sine, bias),
            scratch=[pltpu.VMEM((tokens, kv_cols), F32)] * 2,
            flops=10 * heads * tokens * tokens * HD,
            name="attn_bwd",
        )
        dq, dk, dv = (
            project_grad[:, :q_cols],
            project_grad[:, q_cols : q_cols + kv_cols],
            project_grad[:, q_cols + kv_cols :],
        )
        attn_in_part = mm_bt(project_grad, w_project).astype(BF)
        attn_in_grad = lax.psum_scatter(attn_in_part, "tensor", scatter_dimension=0, tiled=True).astype(F32)

        mixed_wide = jnp.moveaxis(mixed_own, 0, 1).reshape(own, n_t * q_cols)
        out_grad = grad_scatter(core_split(branch_grad, n_dp), mixed_wide, n_dp)
        out_parts = out_grad.reshape(-1, n_t, q_cols)
        w_out_grad = pick(out_parts, me_t, 1)
        for d in range(1, n_t):
            piece = pick(out_parts, (me_t + d) % n_t, 1).astype(BF)
            w_out_grad = w_out_grad + ring(piece, d).astype(F32)
        w_out_grad = w_out_grad.T

        project_wgrad = grad_scatter(core_split(x_all, n_dp), project_grad, n_dp)
        w_query_grad = project_wgrad[:, :q_cols]
        w_key_grad = project_wgrad[:, q_cols : q_cols + kv_cols]
        w_value_grad = project_wgrad[:, q_cols + kv_cols :]

        input_grad = (middle_grad + norm_back(attn_in_grad, scaled_attn, inverse_attn, gain_attn_wide)).astype(BF)

        def own_rows(array):
            return lax.dynamic_slice_in_dim(array, me_dp * (width // n_dp), width // n_dp, 0).astype(F32)

        gain_sums = jnp.stack(
            [
                jnp.sum(own_rows(w_project) * project_wgrad, axis=1),
                jnp.sum(own_rows(w_gate) * w_gate_grad, axis=1) + jnp.sum(own_rows(w_up) * w_up_grad, axis=1),
            ]
        )
        bit = 1
        while bit < n_t:
            gain_sums = gain_sums + lax.ppermute(gain_sums, "tensor", pairs(n_t, bit))
            bit *= 2
        gain_attn_grad = gain_sums[0] / own_rows(gain_attn)
        gain_ffn_grad = gain_sums[1] / own_rows(gain_ffn)

    return (
        output,
        input_grad,
        gain_attn_grad,
        w_query_grad,
        w_key_grad,
        w_value_grad,
        w_out_grad,
        gain_ffn_grad,
        w_gate_grad,
        w_up_grad,
        w_down_grad,
    )


def solution(mesh):
    return jax.shard_map(
        functools.partial(shards, mesh.shape["dp"], mesh.shape["tensor"]),
        mesh=mesh,
        in_specs=(
            P(("dp", "tensor"), None),
            P(),
            P(None, "tensor"),
            P(None, "tensor"),
            P(None, "tensor"),
            P("tensor", None),
            P(),
            P(None, "tensor"),
            P(None, "tensor"),
            P("tensor", None),
            P("dp"),
            P("dp"),
            P(("dp", "tensor"), None),
        ),
        out_specs=(
            P(("dp", "tensor"), None),
            P(("dp", "tensor"), None),
            P("dp"),
            P("dp", "tensor"),
            P("dp", "tensor"),
            P("dp", "tensor"),
            P("tensor", "dp"),
            P("dp"),
            P("dp", "tensor"),
            P("dp", "tensor"),
            P("tensor", "dp"),
        ),
        check_vma=False,
    )
```
